512 devices in a mesh: rows: 64 (over y, z), cent: 8 (over x, core).
Axes of the slice: x: 4, y: 4, z: 16, core: 2. Of those that a mesh axis runs over, the one named last changes fastest.
Arguments:
- embeddings: bfloat16 [24576, 1024], P('rows'), may hold values from -288 to 288
- centroids: bfloat16 [16384, 1024], P('cent'), may hold values from -12 to 12
- codebook: bfloat16 [8, 4096, 128], P('cent', 'rows'), may hold values from -6 to 6
Outputs:
- residual: bfloat16 [1024, 24576], P('cent', 'rows')
- new_codebook: float32 [8, 4096, 128], P('cent', 'rows')
- pq_error: float32 [8, 24576], P('cent', 'rows')
The draws below stay inside these ranges and needn't reach their ends.
All inputs are finite; a program needn't handle non-finite values.
Results may differ from the reference program's by a relative error of at most 0.04.
Values may be sent and summed in bfloat16 or wider, within the bound.
No kernel may reach another device: no remote copies, remote signals or barrier semaphores. Data moves between devices by JAX's collectives and lax.ppermute only.
A program may use at most 64 MiB of HBM per device.

```python
import functools
import math
import jax
import jax.numpy as jnp
from jax import lax

NC = 16384
M = 8
DS = 128
K = 4096
D = 1024
ROWS = 24576


def draw_embeddings(key, part):
    key = jax.random.fold_in(key, 7)
    noise_key = jax.random.fold_in(key, 0)
    values = jnp.clip(jax.random.normal(noise_key, (ROWS, D), jnp.float32), -6.0, 6.0)
    return values.astype(jnp.bfloat16)


def levels(rng, shape, shards, smallest, largest):
    def one(position, blocks):
        steps = jax.random.uniform(jax.random.fold_in(jax.random.fold_in(rng, 6), position), (blocks,), jnp.float32, smallest / len(shards), largest / len(shards))
        return jnp.repeat(jnp.exp(steps), shape[position] // blocks).reshape((-1,) + (1,) * (len(shape) - position - 1))

    gain = one(*shards[0])
    for cut in shards[1:]:
        gain = gain * one(*cut)
    return gain


def gaussian(own_key, shape, width, most, pieces=(), kind=jnp.bfloat16):
    gain = levels(own_key, shape, pieces, -0.22, 0.18) if pieces else 1.0
    values = jax.random.normal(own_key, shape, jnp.float32) * width * gain
    return jnp.minimum(jnp.maximum(values, -most), most).astype(kind)


def setup_inputs(seed: int = 0) -> dict:
    seeds = jax.random.split(jax.random.key(seed), 4)
    return {
        "embeddings": draw_embeddings(jax.random.fold_in(seeds[3], 71), 0),
        "centroids": gaussian(seeds[1], (NC, D), 2.0, 12.0, ((0, 8),)),
        "codebook": gaussian(seeds[2], (M, K, DS), 1.0, 6.0, ((0, 8), (1, 64))),
    }


smoothing = 1.0

def coarse_block(block, centroids, half_norm, scale):
    products = jnp.dot(block, centroids.T, preferred_element_type=jnp.float32)
    logits = (products - half_norm[None, :]) * scale
    row_max = lax.optimization_barrier(jnp.max(logits, axis=1, keepdims=True))
    shifted = jnp.exp(logits - row_max)
    row_total = lax.optimization_barrier(jnp.sum(shifted, axis=1, keepdims=True))
    pulled = jnp.dot(shifted.astype(jnp.bfloat16), centroids, preferred_element_type=jnp.float32)
    return (block.astype(jnp.float32) - pulled / row_total).astype(jnp.bfloat16)

def subspace_update(pair, scale):
    book, column_block = pair
    book_wide = book.astype(jnp.float32)
    scores = jnp.dot(book, column_block, preferred_element_type=jnp.float32)
    book_half = 0.5 * lax.optimization_barrier(jnp.sum(book_wide * book_wide, axis=1))
    logits = (scores - book_half[:, None]) * scale
    pq_peak = lax.optimization_barrier(jnp.max(logits, axis=0, keepdims=True))
    raised = jnp.exp(logits - pq_peak)
    pq_probs = raised / lax.optimization_barrier(jnp.sum(raised, axis=0, keepdims=True))
    pq_weights = pq_probs.astype(jnp.bfloat16)
    rebuilt = jnp.dot(book.T, pq_weights, preferred_element_type=jnp.float32)
    error = lax.optimization_barrier(jnp.mean(jnp.square(column_block.astype(jnp.float32) - rebuilt), axis=0))
    word_sums = jnp.dot(pq_weights, column_block.T, preferred_element_type=jnp.float32)
    counts = lax.optimization_barrier(jnp.sum(pq_probs, axis=1))
    updated = (word_sums + smoothing * book_wide) / (counts[:, None] + smoothing)
    return (updated, error)

def reference(embeddings, centroids, codebook):
    cent_wide = centroids.astype(jnp.float32)
    half_norm = 0.5 * lax.optimization_barrier(jnp.sum(cent_wide * cent_wide, axis=1))
    block_rows = math.gcd(ROWS, 512)
    grouped = embeddings.reshape(ROWS // block_rows, block_rows, D)
    coarse_fn = functools.partial(coarse_block, centroids=centroids, half_norm=half_norm, scale=2.0 / math.sqrt(D))
    residual_rows = lax.map(coarse_fn, grouped).reshape(ROWS, D)
    residual = residual_rows.T
    column_groups = residual.reshape(M, DS, ROWS)
    update_fn = functools.partial(subspace_update, scale=2.0 / math.sqrt(DS))
    new_codebook, pq_error = lax.map(update_fn, (codebook, column_groups))
    return (residual, new_codebook, pq_error)
```

```python
import math

import jax
import jax.numpy as jnp
from jax import lax
from jax.sharding import Mesh, PartitionSpec as P

smoothing = 1.0
CENT = ("x", "c")


def split(value):
    terms = []
    for _ in range(3):
        term = lax.reduce_precision(value, 8, 7)
        terms.append(term.astype(jnp.bfloat16))
        value = value - term
    return jnp.stack(terms)


def join(terms):
    wide = terms.astype(jnp.float32)
    return (wide[..., 2, :] + wide[..., 1, :]) + wide[..., 0, :]


def exchange(parts, axis):
    return lax.all_to_all(parts, axis, 0, 0, tiled=True)


def local(embeddings, centroids, codebook):
    rows_here, model_width = embeddings.shape
    cent_count = lax.axis_size(CENT)
    slice_width = model_width // cent_count
    _, book_rows, sub_width = codebook.shape
    y_count, z_count = lax.axis_size("y"), lax.axis_size("z")
    words = book_rows * y_count * z_count

    own = codebook.reshape(book_rows, sub_width)
    book = exchange(jnp.broadcast_to(own, (z_count, book_rows, sub_width)), "z")
    book = lax.all_gather(book.reshape(words // y_count, sub_width), "y", axis=0, tiled=True)

    products = lax.dot_general(
        embeddings, centroids, (((1,), (1,)), ((), ())), preferred_element_type=jnp.float32
    )
    cent_wide = centroids.astype(jnp.float32)
    half_norm = 0.5 * jnp.sum(cent_wide * cent_wide, axis=1)
    logits = (products - half_norm[None, :]) * (2.0 / math.sqrt(model_width))
    slab_max = jnp.max(logits, axis=1)
    shifted = jnp.exp(logits - slab_max[:, None])
    slab_total = jnp.sum(shifted, axis=1)
    pulled = lax.dot_general(
        centroids, shifted.astype(jnp.bfloat16), (((0,), (1,)), ((), ())), preferred_element_type=jnp.float32
    )
    pulled = (pulled / slab_total[None, :]).astype(jnp.bfloat16)

    stats = jnp.concatenate([split(slab_max), split(slab_total)])
    stats = jnp.pad(stats, ((0, 10), (0, 0)))
    parts = jnp.concatenate(
        [
            pulled.reshape(cent_count, slice_width, rows_here),
            jnp.broadcast_to(stats, (cent_count,) + stats.shape),
        ],
        axis=1,
    )
    parts = exchange(parts, CENT)
    slab_maxes = join(parts[:, slice_width : slice_width + 3])
    slab_totals = join(parts[:, slice_width + 3 : slice_width + 6])
    row_max = jnp.max(slab_maxes, axis=0)
    shares = jnp.exp(slab_maxes - row_max) * slab_totals
    shares = shares / jnp.sum(shares, axis=0)
    mean = jnp.sum(parts[:, :slice_width].astype(jnp.float32) * shares[:, None, :], axis=0)
    own_cols = lax.dynamic_slice_in_dim(
        embeddings, lax.axis_index(CENT) * slice_width, slice_width, 1
    )
    residual = (own_cols.T.astype(jnp.float32) - mean).astype(jnp.bfloat16)

    scores = jnp.dot(book, residual, preferred_element_type=jnp.float32)
    book_wide = book.astype(jnp.float32)
    book_half = 0.5 * jnp.sum(book_wide * book_wide, axis=1)
    pq_logits = (scores - book_half[:, None]) * (2.0 / math.sqrt(sub_width))
    pq_peak = jnp.max(pq_logits, axis=0, keepdims=True)
    raised = jnp.exp(pq_logits - pq_peak)
    pq_probs = raised / jnp.sum(raised, axis=0, keepdims=True)
    pq_weights = pq_probs.astype(jnp.bfloat16)
    rebuilt = lax.dot_general(
        book, pq_weights, (((0,), (0,)), ((), ())), preferred_element_type=jnp.float32
    )
    pq_error = jnp.mean(jnp.square(residual.astype(jnp.float32) - rebuilt), axis=0)
    word_sums = lax.dot_general(
        pq_weights, residual, (((1,), (1,)), ((), ())), preferred_element_type=jnp.float32
    )
    counts = jnp.sum(pq_probs, axis=1)

    counts = jnp.swapaxes(split(counts).reshape(3, y_count, words // y_count), 0, 1)
    counts = jnp.pad(counts.reshape(y_count, -1, sub_width), ((0, 0), (0, 8), (0, 0)))
    sums = jnp.concatenate(
        [word_sums.astype(jnp.bfloat16).reshape(y_count, words // y_count, sub_width), counts], axis=1
    )
    sums = exchange(sums, "y")
    quarter = words // y_count
    counts = join(sums[:, quarter : quarter + 3 * quarter // sub_width].reshape(y_count, 3, quarter))
    counts = jnp.sum(counts, axis=0)
    sums = jnp.sum(sums[:, :quarter].astype(jnp.float32), axis=0)
    counts = jnp.swapaxes(split(counts).reshape(3, z_count, book_rows), 0, 1)
    counts = jnp.pad(counts.reshape(z_count, 1, 3 * book_rows), ((0, 0), (0, 0), (0, 4 * sub_width - 3 * book_rows)))
    sums = jnp.concatenate(
        [
            sums.astype(jnp.bfloat16).reshape(z_count, book_rows, sub_width),
            counts.reshape(z_count, 4, sub_width),
            jnp.zeros((z_count, 12, sub_width), jnp.bfloat16),
        ],
        axis=1,
    )
    sums = exchange(sums, "z")
    counts = sums[:, book_rows : book_rows + 4].reshape(z_count, -1)[:, : 3 * book_rows]
    counts = jnp.sum(join(counts.reshape(z_count, 3, book_rows)), axis=0)
    sums = jnp.sum(sums[:, :book_rows].astype(jnp.float32), axis=0)
    new_codebook = (sums + smoothing * own.astype(jnp.float32)) / (counts[:, None] + smoothing)
    return (residual, new_codebook[None], pq_error[None])


def solution(mesh):
    sizes = (4, 16, 4, 2)
    wide = Mesh(mesh.devices.reshape(sizes), ("y", "z", "x", "c"))
    rows = ("y", "z")
    placed = (P(rows, None), P(CENT, None), P(CENT, rows, None))
    return jax.shard_map(
        local,
        mesh=wide,
        in_specs=placed,
        out_specs=(P(CENT, rows), P(CENT, rows, None), P(CENT, rows)),
        check_vma=False,
    )
```

```python
import functools
import math

import jax
import jax.numpy as jnp
from jax import lax
from jax.experimental import pallas as pl
from jax.experimental.pallas import tpu as pltpu
from jax.sharding import Mesh, PartitionSpec as P

smoothing = 1.0
CENT = ("x", "c")


def split(value):
    terms = []
    for _ in range(3):
        term = lax.reduce_precision(value, 8, 7)
        terms.append(term.astype(jnp.bfloat16))
        value = value - term
    return jnp.stack(terms)


def join(terms):
    wide = terms.astype(jnp.float32)
    return (wide[..., 2, :] + wide[..., 1, :]) + wide[..., 0, :]


PACKED = 16


def packed(largest, total):
    return jnp.pad(jnp.concatenate([split(largest), split(total)]), ((0, PACKED - 6), (0, 0)))


def unpacked(terms):
    return join(terms[:3]), join(terms[3:6])


def exchange(parts, axis):
    return lax.all_to_all(parts, axis, 0, 0, tiled=True)


def wide_row(columns):
    return jnp.transpose(jnp.broadcast_to(columns, (columns.shape[0], 128)))[:1]


def coarse_kernel(core_ref, e_ref, c_ref, sent_ref, stats_ref, weights_ref, inverse_ref, logits_ref):
    rows, width = e_ref.shape
    chunks, _, chunk = logits_ref.shape
    used = sent_ref.shape[0] - PACKED
    scale = 2.0 / math.sqrt(width)

    def score(j, peak):
        block = c_ref[pl.ds(pl.multiple_of(j * chunk, chunk), chunk), :]
        wide = block.astype(jnp.float32)
        half_norm = wide_row(0.5 * jnp.sum(wide * wide, axis=1, keepdims=True))
        products = lax.dot_general(
            e_ref[...], block, (((1,), (1,)), ((), ())), preferred_element_type=jnp.float32
        )
        logits = (products - half_norm) * scale
        logits_ref[j] = logits
        for part in range(chunk // 128):
            peak = jnp.maximum(peak, logits[:, part * 128 : part * 128 + 128])
        return peak

    peak = lax.fori_loop(0, chunks, score, jnp.full((rows, 128), -jnp.inf, jnp.float32), unroll=2)
    peak = jnp.max(peak, axis=1, keepdims=True)

    def raise_(j, total):
        shifted = jnp.exp(logits_ref[j] - peak)
        weights_ref[:, pl.ds(pl.multiple_of(j * chunk, chunk), chunk)] = shifted.astype(jnp.bfloat16)
        for part in range(chunk // 128):
            total = total + shifted[:, part * 128 : part * 128 + 128]
        return total

    total = lax.fori_loop(0, chunks, raise_, jnp.zeros((rows, 128), jnp.float32), unroll=2)
    total = jnp.sum(total, axis=1, keepdims=True)
    inverse_ref[...] = jnp.broadcast_to(1.0 / total, inverse_ref.shape)
    pull(1 - core_ref[0], weights_ref, inverse_ref, c_ref, sent_ref)
    stats = [wide_row(peak), wide_row(total)]
    stats_ref[...] = jnp.concatenate(stats + [jnp.zeros((6, rows), jnp.float32)], axis=0)
    terms = []
    for value in stats:
        for _ in range(3):
            term = value.astype(jnp.bfloat16).astype(jnp.float32)
            terms.append(term)
            value = value - term
    terms.append(jnp.zeros((PACKED - len(terms), rows), jnp.float32))
    sent_ref[used:, :] = jnp.concatenate(terms, axis=0).astype(jnp.bfloat16)


def pull(core, weights_ref, inverse_ref, c_ref, out_ref):
    sub = inverse_ref.shape[1]
    for pair in range(2):
        columns = [pl.ds(pl.multiple_of(((2 * pair + k) * 2 + core) * sub, sub), sub) for k in range(2)]
        block = jnp.concatenate([c_ref[:, column] for column in columns], axis=1)
        pulled = jnp.dot(weights_ref[...], block, preferred_element_type=jnp.float32)
        for k in range(2):
            part = pulled[:, k * sub : k * sub + sub] * inverse_ref[...]
            row = (2 * pair + k) * sub
            out_ref[row : row + sub, :] = jnp.transpose(part).astype(out_ref.dtype)


def kept_kernel(core_ref, weights_ref, inverse_ref, c_ref, kept_ref):
    pull(core_ref[0], weights_ref, inverse_ref, c_ref, kept_ref)


def coarse(embeddings, centroids, core):
    rows, width = embeddings.shape
    count = centroids.shape[0]
    half, sub, chunk = width // 2, 128, 256
    vmem, smem = pl.BlockSpec(memory_space=pltpu.VMEM), pl.BlockSpec(memory_space=pltpu.SMEM)
    params = pltpu.CompilerParams(vmem_limit_bytes=32 * 2**20)
    core = core.astype(jnp.int32).reshape(1)
    sent, stats, weights, inverse = pl.pallas_call(
        coarse_kernel,
        out_shape=(
            jax.ShapeDtypeStruct((half + PACKED, rows), jnp.bfloat16),
            jax.ShapeDtypeStruct((8, rows), jnp.float32),
            jax.ShapeDtypeStruct((rows, count), jnp.bfloat16),
            jax.ShapeDtypeStruct((rows, sub), jnp.float32),
        ),
        in_specs=[smem, vmem, vmem],
        out_specs=(vmem,) * 4,
        scratch_shapes=[pltpu.VMEM((count // chunk, rows, chunk), jnp.float32)],
        compiler_params=params,
        cost_estimate=pl.CostEstimate(flops=1, bytes_accessed=1, transcendentals=0),
    )(core, embeddings, centroids)
    kept = pl.pallas_call(
        kept_kernel,
        out_shape=jax.ShapeDtypeStruct((half, rows), jnp.float32),
        in_specs=[smem, vmem, vmem, vmem],
        out_specs=vmem,
        compiler_params=params,
        cost_estimate=pl.CostEstimate(flops=1, bytes_accessed=1, transcendentals=0),
    )(core, weights, inverse, centroids)
    return kept.reshape(-1, sub, rows), sent, stats[0], stats[1]


def local(embeddings, centroids, codebook):
    rows_here, model_width = embeddings.shape
    cent_count = lax.axis_size(CENT)
    slice_width = model_width // cent_count
    _, book_rows, sub_width = codebook.shape
    y_count, z_count = lax.axis_size("y"), lax.axis_size("z")
    words = book_rows * y_count * z_count

    own = codebook.reshape(book_rows, sub_width)
    book = exchange(jnp.broadcast_to(own, (z_count, book_rows, sub_width)), "z")
    book = book.reshape(words // y_count, sub_width)
    core, column = lax.axis_index("c"), lax.axis_index("x")
    kept, sent, slab_max, slab_total = coarse(embeddings, centroids, core)

    got = lax.ppermute(sent, "c", [(0, 1), (1, 0)])
    book, got, kept = lax.optimization_barrier((book, got, kept))
    other_max, other_total = unpacked(got[-PACKED:])
    chip_max = jnp.maximum(slab_max, other_max)
    own_share = jnp.exp(slab_max - chip_max) * slab_total
    other_share = jnp.exp(other_max - chip_max) * other_total
    chip_total = own_share + other_share
    chip_mean = kept * (own_share / chip_total) + got[:-PACKED].astype(jnp.float32).reshape(kept.shape) * (
        other_share / chip_total
    )
    chip_stats = packed(chip_max, chip_total)
    book = exchange(jnp.broadcast_to(book, (y_count,) + book.shape), "y").reshape(words, sub_width)
    count = lax.axis_size("x")
    means = [lax.dynamic_index_in_dim(chip_mean, column, 0, keepdims=False)]
    maxes, totals = [chip_max], [chip_total]
    for step in range(1, count):
        target = lax.rem(column + step, count)
        block = lax.dynamic_index_in_dim(chip_mean, target, 0, keepdims=False).astype(jnp.bfloat16)
        block = jnp.concatenate([block, chip_stats], axis=0)
        got = lax.ppermute(block, "x", [(i, (i + step) % count) for i in range(count)])
        slab_max, slab_total = unpacked(got[-PACKED:])
        means.append(got[:-PACKED].astype(jnp.float32))
        maxes.append(slab_max)
        totals.append(slab_total)
    book, means, maxes, totals = lax.optimization_barrier((book, means, maxes, totals))
    row_max = functools.reduce(jnp.maximum, maxes)
    shares = [jnp.exp(largest - row_max) * total for largest, total in zip(maxes, totals)]
    row_total = sum(shares)
    mean = sum(part * (share / row_total) for part, share in zip(means, shares))
    own_cols = lax.dynamic_slice_in_dim(
        embeddings, lax.axis_index(CENT) * slice_width, slice_width, 1
    )
    residual = (own_cols.T.astype(jnp.float32) - mean).astype(jnp.bfloat16)

    scores = jnp.dot(book, residual, preferred_element_type=jnp.float32)
    book_wide = book.astype(jnp.float32)
    book_half = 0.5 * jnp.sum(book_wide * book_wide, axis=1)
    pq_logits = (scores - book_half[:, None]) * (2.0 / math.sqrt(sub_width))
    pq_peak = jnp.max(pq_logits, axis=0, keepdims=True)
    raised = jnp.exp(pq_logits - pq_peak)
    pq_probs = raised / jnp.sum(raised, axis=0, keepdims=True)
    pq_weights = pq_probs.astype(jnp.bfloat16)
    rebuilt = lax.dot_general(
        book, pq_weights, (((0,), (0,)), ((), ())), preferred_element_type=jnp.float32
    )
    pq_error = jnp.mean(jnp.square(residual.astype(jnp.float32) - rebuilt), axis=0)
    word_sums = lax.dot_general(
        pq_weights, residual, (((1,), (1,)), ((), ())), preferred_element_type=jnp.float32
    )
    counts = jnp.sum(pq_probs, axis=1)

    counts = jnp.swapaxes(split(counts).reshape(3, y_count, words // y_count), 0, 1)
    counts = jnp.pad(counts.reshape(y_count, -1, sub_width), ((0, 0), (0, 8), (0, 0)))
    sums = jnp.concatenate(
        [word_sums.astype(jnp.bfloat16).reshape(y_count, words // y_count, sub_width), counts], axis=1
    )
    sums = exchange(sums, "y")
    quarter = words // y_count
    counts = join(sums[:, quarter : quarter + 3 * quarter // sub_width].reshape(y_count, 3, quarter))
    counts = jnp.sum(counts, axis=0)
    sums = jnp.sum(sums[:, :quarter].astype(jnp.float32), axis=0)
    counts = jnp.swapaxes(split(counts).reshape(3, z_count, book_rows), 0, 1)
    counts = jnp.pad(counts.reshape(z_count, 1, 3 * book_rows), ((0, 0), (0, 0), (0, 4 * sub_width - 3 * book_rows)))
    sums = jnp.concatenate(
        [
            sums.astype(jnp.bfloat16).reshape(z_count, book_rows, sub_width),
            counts.reshape(z_count, 4, sub_width),
            jnp.zeros((z_count, 12, sub_width), jnp.bfloat16),
        ],
        axis=1,
    )
    sums = exchange(sums, "z")
    counts = sums[:, book_rows : book_rows + 4].reshape(z_count, -1)[:, : 3 * book_rows]
    counts = jnp.sum(join(counts.reshape(z_count, 3, book_rows)), axis=0)
    sums = jnp.sum(sums[:, :book_rows].astype(jnp.float32), axis=0)
    new_codebook = (sums + smoothing * own.astype(jnp.float32)) / (counts[:, None] + smoothing)
    return (residual, new_codebook[None], pq_error[None])


def solution(mesh):
    sizes = (4, 16, 4, 2)
    wide = Mesh(mesh.devices.reshape(sizes), ("y", "z", "x", "c"))
    rows = ("y", "z")
    placed = (P(rows, None), P(CENT, None), P(CENT, rows, None))
    return jax.shard_map(
        local,
        mesh=wide,
        in_specs=placed,
        out_specs=(P(CENT, rows), P(CENT, rows, None), P(CENT, rows)),
        check_vma=False,
    )
```

```python
import functools
import math

import jax
import jax.numpy as jnp
from jax import lax
from jax.experimental import pallas as pl
from jax.experimental.pallas import tpu as pltpu
from jax.sharding import Mesh, PartitionSpec as P

smoothing = 1.0
CENT = ("x", "c")


PACKED = 16


def exchange(parts, axis):
    return lax.all_to_all(parts, axis, 0, 0, tiled=True)


def wide_row(columns):
    return jnp.transpose(jnp.broadcast_to(columns, (columns.shape[0], 128)))[:1]


def coarse_kernel(place_ref, e_ref, c_ref, sent_ref, stats_ref, weights_ref, inverse_ref, logits_ref):
    rows, width = e_ref.shape
    chunks, _, chunk = logits_ref.shape
    used = sent_ref.shape[0] - PACKED
    scale = 2.0 / math.sqrt(width)

    def score(j, peak):
        block = c_ref[pl.ds(pl.multiple_of(j * chunk, chunk), chunk), :]
        wide = block.astype(jnp.float32)
        half_norm = wide_row(0.5 * jnp.sum(wide * wide, axis=1, keepdims=True))
        products = lax.dot_general(
            e_ref[...], block, (((1,), (1,)), ((), ())), preferred_element_type=jnp.float32
        )
        logits = (products - half_norm) * scale
        logits_ref[j] = logits
        for part in range(chunk // 128):
            peak = jnp.maximum(peak, logits[:, part * 128 : part * 128 + 128])
        return peak

    peak = lax.fori_loop(0, chunks, score, jnp.full((rows, 128), -jnp.inf, jnp.float32), unroll=2)
    peak = jnp.max(peak, axis=1, keepdims=True)

    def raise_(j, total):
        shifted = jnp.exp(logits_ref[j] - peak)
        weights_ref[:, pl.ds(pl.multiple_of(j * chunk, chunk), chunk)] = shifted.astype(jnp.bfloat16)
        for part in range(chunk // 128):
            total = total + shifted[:, part * 128 : part * 128 + 128]
        return total

    total = lax.fori_loop(0, chunks, raise_, jnp.zeros((rows, 128), jnp.float32), unroll=2)
    total = jnp.sum(total, axis=1, keepdims=True)
    inverse_ref[...] = jnp.broadcast_to(1.0 / total, inverse_ref.shape)
    pull(1 - place_ref[0], weights_ref, inverse_ref, c_ref, sent_ref)
    largest, total = wide_row(peak), wide_row(total)
    stats_ref[...] = jnp.concatenate([largest, total, jnp.zeros((6, rows), jnp.float32)], axis=0)
    sent_ref[used:, :] = packed(largest, total)


def pull(core, weights_ref, inverse_ref, c_ref, out_ref):
    sub = inverse_ref.shape[1]
    for pair in range(2):
        columns = [pl.ds(pl.multiple_of(((2 * pair + k) * 2 + core) * sub, sub), sub) for k in range(2)]
        block = jnp.concatenate([c_ref[:, column] for column in columns], axis=1)
        pulled = jnp.dot(weights_ref[...], block, preferred_element_type=jnp.float32)
        for k in range(2):
            part = pulled[:, k * sub : k * sub + sub] * inverse_ref[...]
            row = (2 * pair + k) * sub
            out_ref[row : row + sub, :] = jnp.transpose(part).astype(out_ref.dtype)


def kept_kernel(place_ref, weights_ref, inverse_ref, c_ref, e_ref, kept_ref, base_ref):
    pull(place_ref[0], weights_ref, inverse_ref, c_ref, kept_ref)
    sub = base_ref.shape[0]
    own = pl.multiple_of((2 * place_ref[1] + place_ref[0]) * sub, sub)
    base_ref[...] = jnp.transpose(e_ref[:, pl.ds(own, sub)].astype(jnp.float32))


def weigh(maxes, totals):
    largest = functools.reduce(jnp.maximum, maxes)
    shares = [jnp.exp(own - largest) * total for own, total in zip(maxes, totals)]
    whole = functools.reduce(jnp.add, shares)
    return [share / whole for share in shares], largest, whole


def terms_of(value, count=3):
    terms = []
    for _ in range(count):
        term = value.astype(jnp.bfloat16).astype(jnp.float32)
        terms.append(term)
        value = value - term
    return terms


def packed(largest, total):
    terms = terms_of(largest) + terms_of(total)
    terms.append(jnp.zeros((PACKED - len(terms), largest.shape[1]), jnp.float32))
    return jnp.concatenate(terms, axis=0).astype(jnp.bfloat16)


def unpacked(rows):
    wide = rows.astype(jnp.float32)
    return (wide[2:3] + wide[1:2]) + wide[0:1], (wide[5:6] + wide[4:5]) + wide[3:4]


def chip_kernel(place_ref, kept_ref, got_ref, stats_ref, mean_ref, chip_ref, *block_refs):
    sub, rows = mean_ref.shape
    count = len(block_refs) + 1
    used = count * sub
    other_max, other_total = unpacked(got_ref[used:, :])
    (own, other), largest, total = weigh(
        [stats_ref[0:1], other_max], [stats_ref[1:2], other_total]
    )
    chip_ref[...] = jnp.concatenate([largest, total, jnp.zeros((6, rows), jnp.float32)], axis=0)
    stats = packed(largest, total)
    for step in range(count):
        at = pl.ds(pl.multiple_of(lax.rem(place_ref[1] + step, count) * sub, sub), sub)
        mean = kept_ref[at, :] * own + got_ref[at, :].astype(jnp.float32) * other
        if step == 0:
            mean_ref[...] = mean
        else:
            block_refs[step - 1][:sub, :] = mean.astype(jnp.bfloat16)
            block_refs[step - 1][sub:, :] = stats


def quantize_kernel(mean_ref, chip_ref, *refs):
    *got_refs, base_ref, book_ref, residual_ref, sums_ref, raised_ref, inverse_ref, gaps_ref = refs
    sub, rows = mean_ref.shape
    parts, held, _ = sums_ref.shape
    words = book_ref.shape[0]
    quarter = words // parts
    scale = 2.0 / math.sqrt(sub)
    stats = [(chip_ref[0:1], chip_ref[1:2])] + [unpacked(got[sub:, :]) for got in got_refs]
    shares, _, _ = weigh(*zip(*stats))
    mean = mean_ref[...] * shares[0]
    for got, share in zip(got_refs, shares[1:]):
        mean = mean + got[:sub, :].astype(jnp.float32) * share
    residual = (base_ref[...] - mean).astype(jnp.bfloat16)
    residual_ref[...] = residual

    chunk = 512

    def score(j, peak):
        at = pl.ds(pl.multiple_of(j * chunk, chunk), chunk)
        block = book_ref[at, :]
        wide = block.astype(jnp.float32)
        half = 0.5 * jnp.sum(wide * wide, axis=1, keepdims=True)
        gap = jnp.dot(block, residual, preferred_element_type=jnp.float32) - half
        gaps_ref[at, :] = gap
        return jnp.maximum(peak, jnp.max(gap.reshape(chunk // 8, 8, rows), axis=0))

    peak = lax.fori_loop(0, words // chunk, score, jnp.full((8, rows), -jnp.inf, jnp.float32), unroll=2)
    peak = jnp.max(peak, axis=0, keepdims=True)

    def raise_(j, total):
        at = pl.ds(pl.multiple_of(j * chunk, chunk), chunk)
        raised = jnp.exp((gaps_ref[at, :] - peak) * scale)
        raised_ref[at, :] = raised.astype(jnp.bfloat16)
        return total + jnp.sum(raised.reshape(chunk // 8, 8, rows), axis=0)

    total = lax.fori_loop(0, words // chunk, raise_, jnp.zeros((8, rows), jnp.float32), unroll=2)
    inverse = 1.0 / jnp.sum(total, axis=0, keepdims=True)
    inverse_ref[...] = jnp.broadcast_to(inverse, inverse_ref.shape)

    scaled = residual.astype(jnp.float32) * inverse
    high, low = (jnp.broadcast_to(term, (sub // 2, rows)) for term in terms_of(inverse, 2))
    sides = jnp.transpose(jnp.concatenate([scaled, high, low], axis=0)).astype(jnp.bfloat16)
    row = lax.broadcasted_iota(jnp.int32, (128, 128), 0)
    diagonal = row == lax.broadcasted_iota(jnp.int32, (128, 128), 1)

    def add(j, _):
        at = pl.ds(pl.multiple_of(j * quarter, quarter), quarter)
        sums = jnp.dot(raised_ref[at, :], sides, preferred_element_type=jnp.float32)
        sums_ref[j, :quarter, :] = sums[:, :sub].astype(jnp.bfloat16)
        counts = sums[:, sub:]
        counts = counts + pltpu.roll(counts, sub // 2, 1)
        counts = jnp.concatenate(
            [
                jnp.sum(jnp.where(diagonal, counts[k * 128 : k * 128 + 128], 0.0), axis=0, keepdims=True)
                for k in range(quarter // 128)
            ],
            axis=0,
        )
        sums_ref[j, quarter:, :] = jnp.concatenate(terms_of(counts, 2), axis=0).astype(jnp.bfloat16)
        return 0

    lax.fori_loop(0, parts, add, 0)


def middle_kernel(sums_ref, out_ref):
    parts, held, sub = sums_ref.shape
    targets, rows, _ = out_ref.shape
    words = rows - 8
    quarter = targets * words
    counts = jnp.zeros((quarter // 128, 128), jnp.float32)
    for part in range(parts):
        pair = sums_ref[part, quarter:, :].astype(jnp.float32)
        counts = counts + (pair[: quarter // 128] + pair[quarter // 128 :])
    high, low = terms_of(counts, 2)
    left = lax.broadcasted_iota(jnp.int32, high.shape, 1) < 64
    even = jnp.where(left, high, pltpu.roll(low, 64, 1))
    odd = jnp.where(left, pltpu.roll(high, 64, 1), low)
    for target in range(targets):
        at = slice(target * words, target * words + words)
        total = sums_ref[0, at, :].astype(jnp.float32)
        for part in range(1, parts):
            total = total + sums_ref[part, at, :].astype(jnp.float32)
        row = (even if target % 2 == 0 else odd)[target // 2 : target // 2 + 1]
        row = jnp.concatenate([row, jnp.zeros((7, sub), jnp.float32)], axis=0)
        out_ref[target] = jnp.concatenate([total, row], axis=0).astype(jnp.bfloat16)


def last_kernel(sums_ref, own_ref, out_ref):
    parts = sums_ref.shape[0]
    words, sub = own_ref.shape
    total = sums_ref[0].astype(jnp.float32)
    for part in range(1, parts):
        total = total + sums_ref[part].astype(jnp.float32)
    pair = total[words : words + 1]
    counts = jnp.broadcast_to(pair + pltpu.roll(pair, 64, 1), (words, sub))
    diagonal = lax.broadcasted_iota(jnp.int32, (words, sub), 0) == lax.broadcasted_iota(jnp.int32, (words, sub), 1)
    counts = jnp.sum(jnp.where(diagonal, counts, 0.0), axis=1, keepdims=True)
    own = own_ref[...].astype(jnp.float32)
    out_ref[...] = (total[:words] + smoothing * own) / (counts + smoothing)


VMEM = pl.BlockSpec(memory_space=pltpu.VMEM)
SMEM = pl.BlockSpec(memory_space=pltpu.SMEM)


def call(kernel, out_shape, ins, *args, scratch=(), flops=1):
    return pl.pallas_call(
        kernel,
        out_shape=out_shape,
        in_specs=ins,
        out_specs=jax.tree.map(lambda _: VMEM, out_shape),
        scratch_shapes=scratch,
        compiler_params=pltpu.CompilerParams(vmem_limit_bytes=40 * 2**20),
        cost_estimate=pl.CostEstimate(flops=flops, bytes_accessed=1, transcendentals=0),
    )(*args)


def array(shape, dtype=jnp.float32):
    return jax.ShapeDtypeStruct(shape, dtype)


def coarse(embeddings, centroids, place):
    rows, width = embeddings.shape
    count = centroids.shape[0]
    half, sub, chunk = width // 2, 128, 256
    sent, stats, weights, inverse = call(
        coarse_kernel,
        (
            array((half + PACKED, rows), jnp.bfloat16),
            array((8, rows)),
            array((rows, count), jnp.bfloat16),
            array((rows, sub)),
        ),
        [SMEM, VMEM, VMEM],
        place,
        embeddings,
        centroids,
        scratch=[pltpu.VMEM((count // chunk, rows, chunk), jnp.float32)],
    )
    kept, base = call(
        kept_kernel,
        (array((half, rows)), array((sub, rows))),
        [SMEM] + [VMEM] * 4,
        place,
        weights,
        inverse,
        centroids,
        embeddings,
    )
    return kept, sent, stats, base


def chip(place, kept, got, stats):
    sub, rows, count = 128, stats.shape[1], 4
    blocks = [array((sub + PACKED, rows), jnp.bfloat16)] * (count - 1)
    return call(
        chip_kernel,
        [array((sub, rows)), array((8, rows))] + blocks,
        [SMEM] + [VMEM] * 3,
        place,
        kept,
        got,
        stats,
    )


def quantize(mean, stats, gots, base, book, parts):
    (sub, rows), words = mean.shape, book.shape[0]
    quarter = words // parts
    return call(
        quantize_kernel,
        (
            array((sub, rows), jnp.bfloat16),
            array((parts, quarter + quarter // 64, sub), jnp.bfloat16),
            array((words, rows), jnp.bfloat16),
            array((8, rows)),
        ),
        [VMEM] * (len(gots) + 4),
        mean,
        stats,
        *gots,
        base,
        book,
        scratch=[pltpu.VMEM((words, rows), jnp.float32)],
    )


def local(embeddings, centroids, codebook):
    _, book_rows, sub_width = codebook.shape
    y_count, z_count, x_count = lax.axis_size("y"), lax.axis_size("z"), lax.axis_size("x")
    words = book_rows * y_count * z_count
    place = jnp.stack([lax.axis_index("c"), lax.axis_index("x")]).astype(jnp.int32)

    own = codebook.reshape(book_rows, sub_width)
    book = exchange(jnp.broadcast_to(own, (z_count, book_rows, sub_width)), "z")
    book = book.reshape(words // y_count, sub_width)

    kept, sent, stats, base = coarse(embeddings, centroids, place)
    got = lax.ppermute(sent, "c", [(0, 1), (1, 0)])
    book, got, kept = lax.optimization_barrier((book, got, kept))
    mean, stats, *blocks = chip(place, kept, got, stats)
    gots = [
        lax.ppermute(block, "x", [(i, (i + step) % x_count) for i in range(x_count)])
        for step, block in enumerate(blocks, 1)
    ]
    book = exchange(jnp.broadcast_to(book, (y_count,) + book.shape), "y").reshape(words, sub_width)
    residual, sums, raised, inverse = quantize(mean, stats, gots, base, book, y_count)

    sums = exchange(sums, "y")
    rebuilt = lax.dot_general(
        book, raised, (((0,), (0,)), ((), ())), preferred_element_type=jnp.float32
    ) * inverse[:1]
    pq_error = jnp.mean(jnp.square(residual.astype(jnp.float32) - rebuilt), axis=0)
    sums, pq_error = lax.optimization_barrier((sums, pq_error))
    sums = call(
        middle_kernel, array((z_count, book_rows + 8, sub_width), jnp.bfloat16), [VMEM], sums
    )
    sums = exchange(sums, "z")
    new_codebook = call(last_kernel, array((book_rows, sub_width)), [VMEM] * 2, sums, own)
    return (residual, new_codebook[None], pq_error[None])


def solution(mesh):
    sizes = (4, 16, 4, 2)
    wide = Mesh(mesh.devices.reshape(sizes), ("y", "z", "x", "c"))
    rows = ("y", "z")
    placed = (P(rows, None), P(CENT, None), P(CENT, rows, None))
    return jax.shard_map(
        local,
        mesh=wide,
        in_specs=placed,
        out_specs=(P(CENT, rows), P(CENT, rows, None), P(CENT, rows)),
        check_vma=False,
    )
```

```python
import functools
import math

import jax
import jax.numpy as jnp
from jax import lax
from jax.experimental import pallas as pl
from jax.experimental.pallas import tpu as pltpu
from jax.sharding import Mesh, PartitionSpec as P

smoothing = 1.0
CENT = ("x", "c")


PACKED = 16


def exchange(parts, axis):
    return lax.all_to_all(parts, axis, 0, 0, tiled=True)


def wide_row(columns):
    return jnp.transpose(jnp.broadcast_to(columns, (columns.shape[0], 128)))[:1]


def coarse_kernel(place_ref, e_ref, c_ref, sent_ref, stats_ref, weights_ref, inverse_ref, logits_ref):
    rows, width = e_ref.shape
    chunks, _, chunk = logits_ref.shape
    used = sent_ref.shape[0] - PACKED
    scale = 2.0 / math.sqrt(width)

    def score(j, peak):
        block = c_ref[pl.ds(pl.multiple_of(j * chunk, chunk), chunk), :]
        wide = block.astype(jnp.float32)
        half_norm = wide_row(0.5 * jnp.sum(wide * wide, axis=1, keepdims=True))
        products = lax.dot_general(
            e_ref[...], block, (((1,), (1,)), ((), ())), preferred_element_type=jnp.float32
        )
        logits = (products - half_norm) * scale
        logits_ref[j] = logits
        for part in range(chunk // 128):
            peak = jnp.maximum(peak, logits[:, part * 128 : part * 128 + 128])
        return peak

    peak = lax.fori_loop(0, chunks, score, jnp.full((rows, 128), -jnp.inf, jnp.float32), unroll=2)
    peak = jnp.max(peak, axis=1, keepdims=True)

    def raise_(j, total):
        shifted = jnp.exp(logits_ref[j] - peak)
        weights_ref[:, pl.ds(pl.multiple_of(j * chunk, chunk), chunk)] = shifted.astype(jnp.bfloat16)
        for part in range(chunk // 128):
            total = total + shifted[:, part * 128 : part * 128 + 128]
        return total

    total = lax.fori_loop(0, chunks, raise_, jnp.zeros((rows, 128), jnp.float32), unroll=2)
    total = jnp.sum(total, axis=1, keepdims=True)
    inverse_ref[...] = jnp.broadcast_to(1.0 / total, inverse_ref.shape)
    pull(1 - place_ref[0], weights_ref, inverse_ref, c_ref, sent_ref)
    largest, total = wide_row(peak), wide_row(total)
    stats_ref[...] = jnp.concatenate([largest, total, jnp.zeros((6, rows), jnp.float32)], axis=0)
    sent_ref[used:, :] = packed(largest, total)


def pull(core, weights_ref, inverse_ref, c_ref, out_ref):
    sub = inverse_ref.shape[1]
    for pair in range(2):
        columns = [pl.ds(pl.multiple_of(((2 * pair + k) * 2 + core) * sub, sub), sub) for k in range(2)]
        block = jnp.concatenate([c_ref[:, column] for column in columns], axis=1)
        pulled = jnp.dot(weights_ref[...], block, preferred_element_type=jnp.float32)
        for k in range(2):
            part = pulled[:, k * sub : k * sub + sub] * inverse_ref[...]
            row = (2 * pair + k) * sub
            out_ref[row : row + sub, :] = jnp.transpose(part).astype(out_ref.dtype)


def kept_kernel(place_ref, weights_ref, inverse_ref, c_ref, e_ref, kept_ref, base_ref):
    pull(place_ref[0], weights_ref, inverse_ref, c_ref, kept_ref)
    sub = base_ref.shape[0]
    own = pl.multiple_of((2 * place_ref[1] + place_ref[0]) * sub, sub)
    base_ref[...] = jnp.transpose(e_ref[:, pl.ds(own, sub)].astype(jnp.float32))


def weigh(maxes, totals):
    largest = functools.reduce(jnp.maximum, maxes)
    shares = [jnp.exp(own - largest) * total for own, total in zip(maxes, totals)]
    whole = functools.reduce(jnp.add, shares)
    return [share / whole for share in shares], largest, whole


def terms_of(value, count=3):
    terms = []
    for _ in range(count):
        term = value.astype(jnp.bfloat16).astype(jnp.float32)
        terms.append(term)
        value = value - term
    return terms


def packed(largest, total):
    terms = terms_of(largest) + terms_of(total)
    terms.append(jnp.zeros((PACKED - len(terms), largest.shape[1]), jnp.float32))
    return jnp.concatenate(terms, axis=0).astype(jnp.bfloat16)


def unpacked(rows):
    wide = rows.astype(jnp.float32)
    return (wide[2:3] + wide[1:2]) + wide[0:1], (wide[5:6] + wide[4:5]) + wide[3:4]


def chip_kernel(place_ref, kept_ref, got_ref, stats_ref, mean_ref, chip_ref, *block_refs):
    sub, rows = mean_ref.shape
    count = len(block_refs) + 1
    used = count * sub
    other_max, other_total = unpacked(got_ref[used:, :])
    (own, other), largest, total = weigh(
        [stats_ref[0:1], other_max], [stats_ref[1:2], other_total]
    )
    chip_ref[...] = jnp.concatenate([largest, total, jnp.zeros((6, rows), jnp.float32)], axis=0)
    stats = packed(largest, total)
    for step in range(count):
        at = pl.ds(pl.multiple_of(lax.rem(place_ref[1] + step, count) * sub, sub), sub)
        mean = kept_ref[at, :] * own + got_ref[at, :].astype(jnp.float32) * other
        if step == 0:
            mean_ref[...] = mean
        else:
            block_refs[step - 1][:sub, :] = mean.astype(jnp.bfloat16)
            block_refs[step - 1][sub:, :] = stats


def quantize_kernel(mean_ref, chip_ref, *refs):
    *got_refs, base_ref, book_ref, residual_ref, sums_ref, raised_hbm, inverse_ref, gaps_ref, raised_ref, sems = refs
    sub, rows = mean_ref.shape
    parts, held, _ = sums_ref.shape
    words = book_ref.shape[0]
    quarter = words // parts
    scale = 2.0 / math.sqrt(sub)
    stats = [(chip_ref[0:1], chip_ref[1:2])] + [unpacked(got[sub:, :]) for got in got_refs]
    shares, _, _ = weigh(*zip(*stats))
    mean = mean_ref[...] * shares[0]
    for got, share in zip(got_refs, shares[1:]):
        mean = mean + got[:sub, :].astype(jnp.float32) * share
    residual = (base_ref[...] - mean).astype(jnp.bfloat16)
    residual_ref[...] = residual

    chunk = 512

    def score(j, peak):
        at = pl.ds(pl.multiple_of(j * chunk, chunk), chunk)
        block = book_ref[at, :]
        wide = block.astype(jnp.float32)
        half = 0.5 * jnp.sum(wide * wide, axis=1, keepdims=True)
        gap = jnp.dot(block, residual, preferred_element_type=jnp.float32) - half
        gaps_ref[at, :] = gap
        return jnp.maximum(peak, jnp.max(gap.reshape(chunk // 8, 8, rows), axis=0))

    peak = lax.fori_loop(0, words // chunk, score, jnp.full((8, rows), -jnp.inf, jnp.float32), unroll=2)
    peak = jnp.max(peak, axis=0, keepdims=True)

    def store(j):
        at = pl.ds(pl.multiple_of(j * chunk, chunk), chunk)
        return pltpu.make_async_copy(raised_ref.at[at, :], raised_hbm.at[at, :], sems.at[j])

    def raise_(j, total):
        at = pl.ds(pl.multiple_of(j * chunk, chunk), chunk)
        raised = jnp.exp((gaps_ref[at, :] - peak) * scale)
        raised_ref[at, :] = raised.astype(jnp.bfloat16)
        store(j).start()
        return total + jnp.sum(raised.reshape(chunk // 8, 8, rows), axis=0)

    total = lax.fori_loop(0, words // chunk, raise_, jnp.zeros((8, rows), jnp.float32), unroll=2)
    inverse = 1.0 / jnp.sum(total, axis=0, keepdims=True)
    inverse_ref[...] = jnp.broadcast_to(inverse, inverse_ref.shape)

    scaled = residual.astype(jnp.float32) * inverse
    high, low = (jnp.broadcast_to(term, (sub // 2, rows)) for term in terms_of(inverse, 2))
    sides = jnp.transpose(jnp.concatenate([scaled, high, low], axis=0)).astype(jnp.bfloat16)
    row = lax.broadcasted_iota(jnp.int32, (128, 128), 0)
    diagonal = row == lax.broadcasted_iota(jnp.int32, (128, 128), 1)

    def add(j, _):
        at = pl.ds(pl.multiple_of(j * quarter, quarter), quarter)
        sums = jnp.dot(raised_ref[at, :], sides, preferred_element_type=jnp.float32)
        sums_ref[j, :quarter, :] = sums[:, :sub].astype(jnp.bfloat16)
        counts = sums[:, sub:]
        counts = counts + pltpu.roll(counts, sub // 2, 1)
        counts = jnp.concatenate(
            [
                jnp.sum(jnp.where(diagonal, counts[k * 128 : k * 128 + 128], 0.0), axis=0, keepdims=True)
                for k in range(quarter // 128)
            ],
            axis=0,
        )
        sums_ref[j, quarter:, :] = jnp.concatenate(terms_of(counts, 2), axis=0).astype(jnp.bfloat16)
        return 0

    lax.fori_loop(0, parts, add, 0)
    for j in range(words // chunk):
        store(j).wait()


def middle_kernel(sums_ref, out_ref):
    parts, held, sub = sums_ref.shape
    targets, rows, _ = out_ref.shape
    words = rows - 8
    quarter = targets * words
    counts = jnp.zeros((quarter // 128, 128), jnp.float32)
    for part in range(parts):
        pair = sums_ref[part, quarter:, :].astype(jnp.float32)
        counts = counts + (pair[: quarter // 128] + pair[quarter // 128 :])
    high, low = terms_of(counts, 2)
    left = lax.broadcasted_iota(jnp.int32, high.shape, 1) < 64
    even = jnp.where(left, high, pltpu.roll(low, 64, 1))
    odd = jnp.where(left, pltpu.roll(high, 64, 1), low)
    for target in range(targets):
        at = slice(target * words, target * words + words)
        total = sums_ref[0, at, :].astype(jnp.float32)
        for part in range(1, parts):
            total = total + sums_ref[part, at, :].astype(jnp.float32)
        row = (even if target % 2 == 0 else odd)[target // 2 : target // 2 + 1]
        row = jnp.concatenate([row, jnp.zeros((7, sub), jnp.float32)], axis=0)
        out_ref[target] = jnp.concatenate([total, row], axis=0).astype(jnp.bfloat16)


def last_kernel(sums_ref, own_ref, out_ref):
    parts = sums_ref.shape[0]
    words, sub = own_ref.shape
    total = sums_ref[0].astype(jnp.float32)
    for part in range(1, parts):
        total = total + sums_ref[part].astype(jnp.float32)
    pair = total[words : words + 1]
    counts = jnp.broadcast_to(pair + pltpu.roll(pair, 64, 1), (words, sub))
    diagonal = lax.broadcasted_iota(jnp.int32, (words, sub), 0) == lax.broadcasted_iota(jnp.int32, (words, sub), 1)
    counts = jnp.sum(jnp.where(diagonal, counts, 0.0), axis=1, keepdims=True)
    own = own_ref[...].astype(jnp.float32)
    out_ref[...] = (total[:words] + smoothing * own) / (counts + smoothing)


VMEM = pl.BlockSpec(memory_space=pltpu.VMEM)
SMEM = pl.BlockSpec(memory_space=pltpu.SMEM)
HBM = pl.BlockSpec(memory_space=pltpu.HBM)


def call(kernel, out_shape, ins, *args, outs=None, scratch=(), mib=8):
    return pl.pallas_call(
        kernel,
        out_shape=out_shape,
        in_specs=ins,
        out_specs=outs or jax.tree.map(lambda _: VMEM, out_shape),
        scratch_shapes=scratch,
        compiler_params=pltpu.CompilerParams(vmem_limit_bytes=mib * 2**20),
        cost_estimate=pl.CostEstimate(flops=1, bytes_accessed=1, transcendentals=0),
    )(*args)


def array(shape, dtype=jnp.float32):
    return jax.ShapeDtypeStruct(shape, dtype)


def coarse(embeddings, centroids, place):
    rows, width = embeddings.shape
    count = centroids.shape[0]
    half, sub, chunk = width // 2, 128, 256
    sent, stats, weights, inverse = call(
        coarse_kernel,
        (
            array((half + PACKED, rows), jnp.bfloat16),
            array((8, rows)),
            array((rows, count), jnp.bfloat16),
            array((rows, sub)),
        ),
        [SMEM, VMEM, VMEM],
        place,
        embeddings,
        centroids,
        scratch=[pltpu.VMEM((count // chunk, rows, chunk), jnp.float32)],
        mib=24,
    )
    kept, base = call(
        kept_kernel,
        (array((half, rows)), array((sub, rows))),
        [SMEM] + [VMEM] * 4,
        place,
        weights,
        inverse,
        centroids,
        embeddings,
        mib=24,
    )
    return kept, sent, stats, base


def chip(place, kept, got, stats):
    sub, rows, count = 128, stats.shape[1], 4
    blocks = [array((sub + PACKED, rows), jnp.bfloat16)] * (count - 1)
    return call(
        chip_kernel,
        [array((sub, rows)), array((8, rows))] + blocks,
        [SMEM] + [VMEM] * 3,
        place,
        kept,
        got,
        stats,
    )


def quantize(mean, stats, gots, base, book, parts):
    (sub, rows), words = mean.shape, book.shape[0]
    quarter = words // parts
    return call(
        quantize_kernel,
        (
            array((sub, rows), jnp.bfloat16),
            array((parts, quarter + quarter // 64, sub), jnp.bfloat16),
            array((words, rows), jnp.bfloat16),
            array((8, rows)),
        ),
        [VMEM] * (len(gots) + 4),
        mean,
        stats,
        *gots,
        base,
        book,
        outs=(VMEM, VMEM, HBM, VMEM),
        scratch=[
            pltpu.VMEM((words, rows), jnp.float32),
            pltpu.VMEM((words, rows), jnp.bfloat16),
            pltpu.SemaphoreType.DMA((words // 512,)),
        ],
        mib=51,
    )


def local(embeddings, centroids, codebook):
    _, book_rows, sub_width = codebook.shape
    y_count, z_count, x_count = lax.axis_size("y"), lax.axis_size("z"), lax.axis_size("x")
    words = book_rows * y_count * z_count
    place = jnp.stack([lax.axis_index("c"), lax.axis_index("x")]).astype(jnp.int32)

    own = codebook.reshape(book_rows, sub_width)
    book = exchange(jnp.broadcast_to(own, (z_count, book_rows, sub_width)), "z")
    book = book.reshape(words // y_count, sub_width)

    kept, sent, stats, base = coarse(embeddings, centroids, place)
    got = lax.ppermute(sent, "c", [(0, 1), (1, 0)])
    book, got, kept = lax.optimization_barrier((book, got, kept))
    mean, stats, *blocks = chip(place, kept, got, stats)
    gots = [
        lax.ppermute(block, "x", [(i, (i + step) % x_count) for i in range(x_count)])
        for step, block in enumerate(blocks, 1)
    ]
    book = exchange(jnp.broadcast_to(book, (y_count,) + book.shape), "y").reshape(words, sub_width)
    residual, sums, raised, inverse = quantize(mean, stats, gots, base, book, y_count)

    sums = exchange(sums, "y")
    rebuilt = lax.dot_general(
        book, raised, (((0,), (0,)), ((), ())), preferred_element_type=jnp.float32
    ) * inverse[:1]
    pq_error = jnp.mean(jnp.square(residual.astype(jnp.float32) - rebuilt), axis=0)
    sums, pq_error = lax.optimization_barrier((sums, pq_error[None]))
    sums = call(
        middle_kernel, array((z_count, book_rows + 8, sub_width), jnp.bfloat16), [VMEM], sums
    )
    sums = exchange(sums, "z")
    new_codebook = call(last_kernel, array((book_rows, sub_width)), [VMEM] * 2, sums, own)
    return (residual, new_codebook[None], pq_error)


def solution(mesh):
    sizes = (4, 16, 4, 2)
    wide = Mesh(mesh.devices.reshape(sizes), ("y", "z", "x", "c"))
    rows = ("y", "z")
    placed = (P(rows, None), P(CENT, None), P(CENT, rows, None))
    return jax.shard_map(
        local,
        mesh=wide,
        in_specs=placed,
        out_specs=(P(CENT, rows), P(CENT, rows, None), P(CENT, rows)),
        check_vma=False,
    )
```

```python
import functools
import math

import jax
import jax.numpy as jnp
from jax import lax
from jax.experimental import pallas as pl
from jax.experimental.pallas import tpu as pltpu
from jax.sharding import Mesh, PartitionSpec as P

smoothing = 1.0
CENT = ("x", "c")


PACKED = 16


def exchange(parts, axis):
    return lax.all_to_all(parts, axis, 0, 0, tiled=True)


def wide_row(columns):
    return jnp.transpose(jnp.broadcast_to(columns, (columns.shape[0], 128)))[:1]


def coarse_kernel(place_ref, e_ref, c_ref, sent_ref, stats_ref, weights_ref, inverse_ref, logits_ref):
    rows, width = e_ref.shape
    chunks, _, chunk = logits_ref.shape
    used = sent_ref.shape[0] - PACKED
    scale = 2.0 / math.sqrt(width)

    def score(j, peak):
        block = c_ref[pl.ds(pl.multiple_of(j * chunk, chunk), chunk), :]
        wide = block.astype(jnp.float32)
        half_norm = wide_row(0.5 * jnp.sum(wide * wide, axis=1, keepdims=True))
        products = lax.dot_general(
            e_ref[...], block, (((1,), (1,)), ((), ())), preferred_element_type=jnp.float32
        )
        logits = (products - half_norm) * scale
        logits_ref[j] = logits
        for part in range(chunk // 128):
            peak = jnp.maximum(peak, logits[:, part * 128 : part * 128 + 128])
        return peak

    peak = lax.fori_loop(0, chunks, score, jnp.full((rows, 128), -jnp.inf, jnp.float32), unroll=2)
    peak = jnp.max(peak, axis=1, keepdims=True)

    def raise_(j, total):
        shifted = jnp.exp(logits_ref[j] - peak)
        weights_ref[:, pl.ds(pl.multiple_of(j * chunk, chunk), chunk)] = shifted.astype(jnp.bfloat16)
        for part in range(chunk // 128):
            total = total + shifted[:, part * 128 : part * 128 + 128]
        return total

    total = lax.fori_loop(0, chunks, raise_, jnp.zeros((rows, 128), jnp.float32), unroll=2)
    total = jnp.sum(total, axis=1, keepdims=True)
    inverse_ref[...] = jnp.broadcast_to(1.0 / total, inverse_ref.shape)
    pull(1 - place_ref[0], weights_ref, inverse_ref, c_ref, sent_ref)
    largest, total = wide_row(peak), wide_row(total)
    stats_ref[...] = jnp.concatenate([largest, total, jnp.zeros((6, rows), jnp.float32)], axis=0)
    sent_ref[used:, :] = packed(largest, total)


def pull(core, weights_ref, inverse_ref, c_ref, out_ref):
    sub = inverse_ref.shape[1]
    for pair in range(2):
        columns = [pl.ds(pl.multiple_of(((2 * pair + k) * 2 + core) * sub, sub), sub) for k in range(2)]
        block = jnp.concatenate([c_ref[:, column] for column in columns], axis=1)
        pulled = jnp.dot(weights_ref[...], block, preferred_element_type=jnp.float32)
        for k in range(2):
            part = pulled[:, k * sub : k * sub + sub] * inverse_ref[...]
            row = (2 * pair + k) * sub
            out_ref[row : row + sub, :] = jnp.transpose(part).astype(out_ref.dtype)


def kept_kernel(place_ref, weights_ref, inverse_ref, c_ref, e_ref, kept_ref, base_ref):
    pull(place_ref[0], weights_ref, inverse_ref, c_ref, kept_ref)
    sub = base_ref.shape[0]
    own = pl.multiple_of((2 * place_ref[1] + place_ref[0]) * sub, sub)
    base_ref[...] = jnp.transpose(e_ref[:, pl.ds(own, sub)].astype(jnp.float32))


def weigh(maxes, totals):
    largest = functools.reduce(jnp.maximum, maxes)
    shares = [jnp.exp(own - largest) * total for own, total in zip(maxes, totals)]
    whole = functools.reduce(jnp.add, shares)
    return [share / whole for share in shares], largest, whole


def terms_of(value, count=3):
    terms = []
    for _ in range(count):
        term = value.astype(jnp.bfloat16).astype(jnp.float32)
        terms.append(term)
        value = value - term
    return terms


def packed(largest, total):
    terms = terms_of(largest) + terms_of(total)
    terms.append(jnp.zeros((PACKED - len(terms), largest.shape[1]), jnp.float32))
    return jnp.concatenate(terms, axis=0).astype(jnp.bfloat16)


def unpacked(rows):
    wide = rows.astype(jnp.float32)
    return (wide[2:3] + wide[1:2]) + wide[0:1], (wide[5:6] + wide[4:5]) + wide[3:4]


def chip_kernel(place_ref, kept_ref, got_ref, stats_ref, mean_ref, chip_ref, *block_refs):
    sub, rows = mean_ref.shape
    count = len(block_refs) + 1
    used = count * sub
    other_max, other_total = unpacked(got_ref[used:, :])
    (own, other), largest, total = weigh(
        [stats_ref[0:1], other_max], [stats_ref[1:2], other_total]
    )
    chip_ref[...] = jnp.concatenate([largest, total, jnp.zeros((6, rows), jnp.float32)], axis=0)
    stats = packed(largest, total)
    for step in range(count):
        at = pl.ds(pl.multiple_of(lax.rem(place_ref[1] + step, count) * sub, sub), sub)
        mean = kept_ref[at, :] * own + got_ref[at, :].astype(jnp.float32) * other
        if step == 0:
            mean_ref[...] = mean
        else:
            block_refs[step - 1][:sub, :] = mean.astype(jnp.bfloat16)
            block_refs[step - 1][sub:, :] = stats


def quantize_kernel(mean_ref, chip_ref, *refs):
    *got_refs, base_ref, book_ref, residual_ref, sums_ref, raised_hbm, inverse_ref, gaps_ref, raised_ref, sems = refs
    sub, rows = mean_ref.shape
    parts, held, _ = sums_ref.shape
    words = book_ref.shape[0]
    quarter = words // parts
    scale = 2.0 / math.sqrt(sub)
    stats = [(chip_ref[0:1], chip_ref[1:2])] + [unpacked(got[sub:, :]) for got in got_refs]
    shares, _, _ = weigh(*zip(*stats))
    mean = mean_ref[...] * shares[0]
    for got, share in zip(got_refs, shares[1:]):
        mean = mean + got[:sub, :].astype(jnp.float32) * share
    residual = (base_ref[...] - mean).astype(jnp.bfloat16)
    residual_ref[...] = residual

    chunk = 512

    def score(j, peak):
        at = pl.ds(pl.multiple_of(j * chunk, chunk), chunk)
        block = book_ref[at, :]
        wide = block.astype(jnp.float32)
        half = 0.5 * jnp.sum(wide * wide, axis=1, keepdims=True)
        gap = jnp.dot(block, residual, preferred_element_type=jnp.float32) - half
        gaps_ref[at, :] = gap
        return jnp.maximum(peak, jnp.max(gap.reshape(chunk // 8, 8, rows), axis=0))

    peak = lax.fori_loop(0, words // chunk, score, jnp.full((8, rows), -jnp.inf, jnp.float32), unroll=2)
    peak = jnp.max(peak, axis=0, keepdims=True)

    def store(j):
        at = pl.ds(pl.multiple_of(j * chunk, chunk), chunk)
        return pltpu.make_async_copy(raised_ref.at[at, :], raised_hbm.at[at, :], sems.at[j])

    def raise_(j, total):
        at = pl.ds(pl.multiple_of(j * chunk, chunk), chunk)
        raised = jnp.exp((gaps_ref[at, :] - peak) * scale)
        raised_ref[at, :] = raised.astype(jnp.bfloat16)
        store(j).start()
        return total + jnp.sum(raised.reshape(chunk // 8, 8, rows), axis=0)

    total = lax.fori_loop(0, words // chunk, raise_, jnp.zeros((8, rows), jnp.float32), unroll=2)
    inverse = 1.0 / jnp.sum(total, axis=0, keepdims=True)
    inverse_ref[...] = jnp.broadcast_to(inverse, inverse_ref.shape)

    scaled = residual.astype(jnp.float32) * inverse
    high, low = (jnp.broadcast_to(term, (sub // 2, rows)) for term in terms_of(inverse, 2))
    sides = jnp.transpose(jnp.concatenate([scaled, high, low], axis=0)).astype(jnp.bfloat16)
    row = lax.broadcasted_iota(jnp.int32, (128, 128), 0)
    diagonal = row == lax.broadcasted_iota(jnp.int32, (128, 128), 1)

    def add(j, _):
        at = pl.ds(pl.multiple_of(j * quarter, quarter), quarter)
        sums = jnp.dot(raised_ref[at, :], sides, preferred_element_type=jnp.float32)
        sums_ref[j, :quarter, :] = sums[:, :sub].astype(jnp.bfloat16)
        counts = sums[:, sub:]
        counts = counts + pltpu.roll(counts, sub // 2, 1)
        counts = jnp.concatenate(
            [
                jnp.sum(jnp.where(diagonal, counts[k * 128 : k * 128 + 128], 0.0), axis=0, keepdims=True)
                for k in range(quarter // 128)
            ],
            axis=0,
        )
        sums_ref[j, quarter:, :] = jnp.concatenate(terms_of(counts, 2), axis=0).astype(jnp.bfloat16)
        return 0

    lax.fori_loop(0, parts, add, 0)
    for j in range(words // chunk):
        store(j).wait()


def middle_kernel(sums_ref, out_ref):
    parts, held, sub = sums_ref.shape
    targets, rows, _ = out_ref.shape
    words = rows - 8
    quarter = targets * words
    counts = jnp.zeros((quarter // 128, 128), jnp.float32)
    for part in range(parts):
        pair = sums_ref[part, quarter:, :].astype(jnp.float32)
        counts = counts + (pair[: quarter // 128] + pair[quarter // 128 :])
    high, low = terms_of(counts, 2)
    left = lax.broadcasted_iota(jnp.int32, high.shape, 1) < 64
    even = jnp.where(left, high, pltpu.roll(low, 64, 1))
    odd = jnp.where(left, pltpu.roll(high, 64, 1), low)
    for target in range(targets):
        at = slice(target * words, target * words + words)
        total = sums_ref[0, at, :].astype(jnp.float32)
        for part in range(1, parts):
            total = total + sums_ref[part, at, :].astype(jnp.float32)
        row = (even if target % 2 == 0 else odd)[target // 2 : target // 2 + 1]
        row = jnp.concatenate([row, jnp.zeros((7, sub), jnp.float32)], axis=0)
        out_ref[target] = jnp.concatenate([total, row], axis=0).astype(jnp.bfloat16)


def last_kernel(sums_ref, own_ref, out_ref):
    parts = sums_ref.shape[0]
    words, sub = own_ref.shape
    total = sums_ref[0].astype(jnp.float32)
    for part in range(1, parts):
        total = total + sums_ref[part].astype(jnp.float32)
    pair = total[words : words + 1]
    counts = jnp.broadcast_to(pair + pltpu.roll(pair, 64, 1), (words, sub))
    diagonal = lax.broadcasted_iota(jnp.int32, (words, sub), 0) == lax.broadcasted_iota(jnp.int32, (words, sub), 1)
    counts = jnp.sum(jnp.where(diagonal, counts, 0.0), axis=1, keepdims=True)
    own = own_ref[...].astype(jnp.float32)
    out_ref[...] = (total[:words] + smoothing * own) / (counts + smoothing)


VMEM = pl.BlockSpec(memory_space=pltpu.VMEM)
SMEM = pl.BlockSpec(memory_space=pltpu.SMEM)
HBM = pl.BlockSpec(memory_space=pltpu.HBM)


def call(kernel, out_shape, ins, *args, outs=None, scratch=(), mib=8):
    return pl.pallas_call(
        kernel,
        out_shape=out_shape,
        in_specs=ins,
        out_specs=outs or jax.tree.map(lambda _: VMEM, out_shape),
        scratch_shapes=scratch,
        compiler_params=pltpu.CompilerParams(vmem_limit_bytes=mib * 2**20),
        cost_estimate=pl.CostEstimate(flops=1, bytes_accessed=1, transcendentals=0),
    )(*args)


def array(shape, dtype=jnp.float32):
    return jax.ShapeDtypeStruct(shape, dtype)


def coarse(embeddings, centroids, place):
    rows, width = embeddings.shape
    count = centroids.shape[0]
    half, sub, chunk = width // 2, 128, 256
    sent, stats, weights, inverse = call(
        coarse_kernel,
        (
            array((half + PACKED, rows), jnp.bfloat16),
            array((8, rows)),
            array((rows, count), jnp.bfloat16),
            array((rows, sub)),
        ),
        [SMEM, VMEM, VMEM],
        place,
        embeddings,
        centroids,
        scratch=[pltpu.VMEM((count // chunk, rows, chunk), jnp.float32)],
        mib=24,
    )
    kept, base = call(
        kept_kernel,
        (array((half, rows)), array((sub, rows))),
        [SMEM] + [VMEM] * 4,
        place,
        weights,
        inverse,
        centroids,
        embeddings,
        mib=24,
    )
    return kept, sent, stats, base


def chip(place, kept, got, stats):
    sub, rows, count = 128, stats.shape[1], 4
    blocks = [array((sub + PACKED, rows), jnp.bfloat16)] * (count - 1)
    return call(
        chip_kernel,
        [array((sub, rows)), array((8, rows))] + blocks,
        [SMEM] + [VMEM] * 3,
        place,
        kept,
        got,
        stats,
    )


def quantize(mean, stats, gots, base, book, parts):
    (sub, rows), words = mean.shape, book.shape[0]
    quarter = words // parts
    return call(
        quantize_kernel,
        (
            array((sub, rows), jnp.bfloat16),
            array((parts, quarter + quarter // 64, sub), jnp.bfloat16),
            array((words, rows), jnp.bfloat16),
            array((8, rows)),
        ),
        [VMEM] * (len(gots) + 4),
        mean,
        stats,
        *gots,
        base,
        book,
        outs=(VMEM, VMEM, HBM, VMEM),
        scratch=[
            pltpu.VMEM((words, rows), jnp.float32),
            pltpu.VMEM((words, rows), jnp.bfloat16),
            pltpu.SemaphoreType.DMA((words // 512,)),
        ],
        mib=51,
    )


def local(embeddings, centroids, codebook):
    _, book_rows, sub_width = codebook.shape
    y_count, z_count, x_count = lax.axis_size("y"), lax.axis_size("z"), lax.axis_size("x")
    words = book_rows * y_count * z_count
    place = jnp.stack([lax.axis_index("c"), lax.axis_index("x")]).astype(jnp.int32)

    own = codebook.reshape(book_rows, sub_width)
    book = exchange(jnp.broadcast_to(own, (z_count, book_rows, sub_width)), "z")
    book = book.reshape(words // y_count, sub_width)

    kept, sent, stats, base = coarse(embeddings, centroids, place)
    got = lax.ppermute(sent, "c", [(0, 1), (1, 0)])
    mean, stats, *blocks = chip(place, kept, got, stats)

    def along(step):
        ring = [(i, (i + step) % x_count) for i in range(x_count)]
        return lax.ppermute(blocks[step - 1], "x", ring)

    gots = {2: along(2)}
    book, gots[2], blocks[0], blocks[2] = lax.optimization_barrier((book, gots[2], blocks[0], blocks[2]))
    gots = [along(1), gots[2], along(3)]
    book = exchange(jnp.broadcast_to(book, (y_count,) + book.shape), "y").reshape(words, sub_width)
    residual, sums, raised, inverse = quantize(mean, stats, gots, base, book, y_count)

    sums = exchange(sums, "y")
    rebuilt = lax.dot_general(
        book, raised, (((0,), (0,)), ((), ())), preferred_element_type=jnp.float32
    ) * inverse[:1]
    pq_error = jnp.mean(jnp.square(residual.astype(jnp.float32) - rebuilt), axis=0)
    sums, pq_error = lax.optimization_barrier((sums, pq_error[None]))
    sums = call(
        middle_kernel, array((z_count, book_rows + 8, sub_width), jnp.bfloat16), [VMEM], sums
    )
    sums = exchange(sums, "z")
    new_codebook = call(last_kernel, array((book_rows, sub_width)), [VMEM] * 2, sums, own)
    return (residual, new_codebook[None], pq_error)


def solution(mesh):
    sizes = (4, 16, 4, 2)
    wide = Mesh(mesh.devices.reshape(sizes), ("y", "z", "x", "c"))
    rows = ("y", "z")
    placed = (P(rows, None), P(CENT, None), P(CENT, rows, None))
    return jax.shard_map(
        local,
        mesh=wide,
        in_specs=placed,
        out_specs=(P(CENT, rows), P(CENT, rows, None), P(CENT, rows)),
        check_vma=False,
    )
```

```python
import functools
import math

import jax
import jax.numpy as jnp
from jax import lax
from jax.experimental import pallas as pl
from jax.experimental.pallas import tpu as pltpu
from jax.sharding import Mesh, PartitionSpec as P

smoothing = 1.0
CENT = ("x", "c")


PACKED = 16


def exchange(parts, axis):
    return lax.all_to_all(parts, axis, 0, 0, tiled=True)


def wide_row(columns):
    return jnp.transpose(jnp.broadcast_to(columns, (columns.shape[0], 128)))[:1]


def coarse_kernel(place_ref, e_ref, c_ref, sent_ref, stats_ref, weights_ref, inverse_ref, logits_ref):
    rows, width = e_ref.shape
    chunks, _, chunk = logits_ref.shape
    used = sent_ref.shape[0] - PACKED
    scale = 2.0 / math.sqrt(width)

    def score(j, peak):
        block = c_ref[pl.ds(pl.multiple_of(j * chunk, chunk), chunk), :]
        wide = block.astype(jnp.float32)
        half_norm = wide_row(0.5 * jnp.sum(wide * wide, axis=1, keepdims=True))
        products = lax.dot_general(
            e_ref[...], block, (((1,), (1,)), ((), ())), preferred_element_type=jnp.float32
        )
        logits = (products - half_norm) * scale
        logits_ref[j] = logits
        for part in range(chunk // 128):
            peak = jnp.maximum(peak, logits[:, part * 128 : part * 128 + 128])
        return peak

    peak = lax.fori_loop(0, chunks, score, jnp.full((rows, 128), -jnp.inf, jnp.float32), unroll=2)
    peak = jnp.max(peak, axis=1, keepdims=True)

    def raise_(j, total):
        shifted = jnp.exp(logits_ref[j] - peak)
        weights_ref[:, pl.ds(pl.multiple_of(j * chunk, chunk), chunk)] = shifted.astype(jnp.bfloat16)
        for part in range(chunk // 128):
            total = total + shifted[:, part * 128 : part * 128 + 128]
        return total

    total = lax.fori_loop(0, chunks, raise_, jnp.zeros((rows, 128), jnp.float32), unroll=2)
    total = jnp.sum(total, axis=1, keepdims=True)
    inverse_ref[...] = jnp.broadcast_to(1.0 / total, inverse_ref.shape)
    pull(1 - place_ref[0], weights_ref, inverse_ref, c_ref, sent_ref)
    largest, total = wide_row(peak), wide_row(total)
    stats_ref[...] = jnp.concatenate([largest, total, jnp.zeros((6, rows), jnp.float32)], axis=0)
    sent_ref[used:, :] = packed(largest, total)


def pull(core, weights_ref, inverse_ref, c_ref, out_ref):
    sub = inverse_ref.shape[1]
    for pair in range(2):
        columns = [pl.ds(pl.multiple_of(((2 * pair + k) * 2 + core) * sub, sub), sub) for k in range(2)]
        block = jnp.concatenate([c_ref[:, column] for column in columns], axis=1)
        pulled = jnp.dot(weights_ref[...], block, preferred_element_type=jnp.float32)
        for k in range(2):
            part = pulled[:, k * sub : k * sub + sub] * inverse_ref[...]
            row = (2 * pair + k) * sub
            out_ref[row : row + sub, :] = jnp.transpose(part).astype(out_ref.dtype)


def kept_kernel(place_ref, weights_ref, inverse_ref, c_ref, e_ref, kept_ref, base_ref):
    pull(place_ref[0], weights_ref, inverse_ref, c_ref, kept_ref)
    sub = base_ref.shape[0]
    own = pl.multiple_of((2 * place_ref[1] + place_ref[0]) * sub, sub)
    base_ref[...] = jnp.transpose(e_ref[:, pl.ds(own, sub)].astype(jnp.float32))


def weigh(maxes, totals):
    largest = functools.reduce(jnp.maximum, maxes)
    shares = [jnp.exp(own - largest) * total for own, total in zip(maxes, totals)]
    whole = functools.reduce(jnp.add, shares)
    return [share / whole for share in shares], largest, whole


def terms_of(value, count=3):
    terms = []
    for _ in range(count):
        term = value.astype(jnp.bfloat16).astype(jnp.float32)
        terms.append(term)
        value = value - term
    return terms


def packed(largest, total):
    terms = terms_of(largest) + terms_of(total)
    terms.append(jnp.zeros((PACKED - len(terms), largest.shape[1]), jnp.float32))
    return jnp.concatenate(terms, axis=0).astype(jnp.bfloat16)


def unpacked(rows):
    wide = rows.astype(jnp.float32)
    return (wide[2:3] + wide[1:2]) + wide[0:1], (wide[5:6] + wide[4:5]) + wide[3:4]


def chip_kernel(place_ref, kept_ref, got_ref, stats_ref, mean_ref, chip_ref, *block_refs):
    sub, rows = mean_ref.shape
    count = len(block_refs) + 1
    used = count * sub
    other_max, other_total = unpacked(got_ref[used:, :])
    (own, other), largest, total = weigh(
        [stats_ref[0:1], other_max], [stats_ref[1:2], other_total]
    )
    chip_ref[...] = jnp.concatenate([largest, total, jnp.zeros((6, rows), jnp.float32)], axis=0)
    stats = packed(largest, total)
    for step in range(count):
        at = pl.ds(pl.multiple_of(lax.rem(place_ref[1] + step, count) * sub, sub), sub)
        mean = kept_ref[at, :] * own + got_ref[at, :].astype(jnp.float32) * other
        if step == 0:
            mean_ref[...] = mean
        else:
            block_refs[step - 1][:sub, :] = mean.astype(jnp.bfloat16)
            block_refs[step - 1][sub:, :] = stats


def residual_kernel(mean_ref, chip_ref, *refs):
    *got_refs, base_ref, residual_ref, copies_ref = refs
    sub = mean_ref.shape[0]
    stats = [(chip_ref[0:1], chip_ref[1:2])] + [unpacked(got[sub:, :]) for got in got_refs]
    shares, _, _ = weigh(*zip(*stats))
    mean = mean_ref[...] * shares[0]
    for got, share in zip(got_refs, shares[1:]):
        mean = mean + got[:sub, :].astype(jnp.float32) * share
    residual = (base_ref[...] - mean).astype(jnp.bfloat16)
    residual_ref[...] = residual
    for copy in range(copies_ref.shape[0]):
        copies_ref[copy] = residual


def score_kernel(book_ref, rows_ref, raised_ref, stats_ref, gaps_ref, half_ref):
    parts, sub, rows = rows_ref.shape
    words = book_ref.shape[0]
    scale = 2.0 / math.sqrt(sub)
    chunk = 256
    spans = [slice(at, at + chunk) for at in range(0, words, chunk)]
    for at in spans:
        wide = book_ref[at, :].astype(jnp.float32)
        half = 0.5 * jnp.sum(wide * wide, axis=1, keepdims=True)
        half_ref[at, :] = jnp.broadcast_to(half, (chunk, 128))
    packs = []
    for part in range(parts):
        peak = jnp.full((8, rows), -jnp.inf, jnp.float32)
        for at in spans:
            gap = jnp.dot(book_ref[at, :], rows_ref[part], preferred_element_type=jnp.float32)
            gap = gap - jnp.concatenate([half_ref[at, :]] * (rows // 128), axis=1)
            gaps_ref[part, at, :] = gap
            peak = jnp.maximum(peak, jnp.max(gap.reshape(chunk // 8, 8, rows), axis=0))
        peak = jnp.max(peak, axis=0, keepdims=True)
        total = jnp.zeros((8, rows), jnp.float32)
        for at in spans:
            raised = jnp.exp((gaps_ref[part, at, :] - peak) * scale)
            raised_ref[at, part * rows : part * rows + rows] = raised.astype(jnp.bfloat16)
            total = total + jnp.sum(raised.reshape(chunk // 8, 8, rows), axis=0)
        packs.append(packed(peak, jnp.sum(total, axis=0, keepdims=True)))
    pack = jnp.concatenate(packs, axis=0)
    for copy in range(stats_ref.shape[0]):
        stats_ref[copy] = pack


def sum_kernel(place_ref, stats_ref, rows_ref, raised_ref, sums_ref, factors_ref, sides_ref):
    parts, sub, rows = rows_ref.shape
    targets, held, _ = sums_ref.shape
    owned = held - 8
    scale = 2.0 / math.sqrt(sub)
    for part in range(parts):
        at = slice(part * PACKED, part * PACKED + PACKED)
        stats = [unpacked(stats_ref[peer, at, :]) for peer in range(parts)]
        peak = functools.reduce(jnp.maximum, [own for own, _ in stats])
        whole = functools.reduce(jnp.add, [jnp.exp((own - peak) * scale) * total for own, total in stats])
        own, _ = unpacked(stats_ref[place_ref[2], at, :])
        factor = jnp.exp((own - peak) * scale) / whole
        factors_ref[:, part * rows : part * rows + rows] = jnp.broadcast_to(factor, (8, rows))
        scaled = rows_ref[part].astype(jnp.float32) * factor
        high, low = (jnp.broadcast_to(term, (sub // 2, rows)) for term in terms_of(factor, 2))
        sides = jnp.transpose(jnp.concatenate([scaled, high, low], axis=0))
        sides_ref[part * rows : part * rows + rows, :] = sides.astype(jnp.bfloat16)
    row = lax.broadcasted_iota(jnp.int32, (128, 128), 0)
    diagonal = row == lax.broadcasted_iota(jnp.int32, (128, 128), 1)
    left = lax.broadcasted_iota(jnp.int32, (1, 128), 1) < 64
    empty = jnp.zeros((7, sub), jnp.float32)
    pair = 2 * owned
    for at in range(0, targets, 4):
        sums = jnp.dot(
            raised_ref[at * owned : (at + 4) * owned, :], sides_ref[...], preferred_element_type=jnp.float32
        )
        for k in range(2):
            both = sums[k * pair : k * pair + pair]
            counts = both[:, sub:]
            counts = counts + pltpu.roll(counts, sub // 2, 1)
            counts = jnp.sum(jnp.where(diagonal, counts, 0.0), axis=0, keepdims=True)
            high, low = terms_of(counts, 2)
            even = jnp.where(left, high, pltpu.roll(low, 64, 1))
            odd = jnp.where(left, pltpu.roll(high, 64, 1), low)
            for n, extra in enumerate((even, odd)):
                block = [both[n * owned : n * owned + owned, :sub], extra, empty]
                sums_ref[at + 2 * k + n] = jnp.concatenate(block, axis=0).astype(jnp.bfloat16)


def share_kernel(place_ref, rebuilt_ref, factors_ref, own_ref, *block_refs):
    sub, rows = own_ref.shape
    count = len(block_refs) + 1
    for step in range(count):
        at = pl.ds(pl.multiple_of(lax.rem(place_ref[2] + step, count) * rows, 128), rows)
        rebuilt = rebuilt_ref[:, at] * factors_ref[0:1, at]
        if step == 0:
            own_ref[...] = rebuilt
        else:
            block_refs[step - 1][...] = rebuilt.astype(jnp.bfloat16)


def last_kernel(sums_ref, own_ref, out_ref):
    parts = sums_ref.shape[0]
    words, sub = own_ref.shape
    total = sums_ref[0].astype(jnp.float32)
    for part in range(1, parts):
        total = total + sums_ref[part].astype(jnp.float32)
    pair = total[words : words + 1]
    counts = jnp.broadcast_to(pair + pltpu.roll(pair, 64, 1), (words, sub))
    diagonal = lax.broadcasted_iota(jnp.int32, (words, sub), 0) == lax.broadcasted_iota(jnp.int32, (words, sub), 1)
    counts = jnp.sum(jnp.where(diagonal, counts, 0.0), axis=1, keepdims=True)
    own = own_ref[...].astype(jnp.float32)
    out_ref[...] = (total[:words] + smoothing * own) / (counts + smoothing)


VMEM = pl.BlockSpec(memory_space=pltpu.VMEM)
SMEM = pl.BlockSpec(memory_space=pltpu.SMEM)


def call(kernel, out_shape, ins, *args, scratch=(), mib=8):
    return pl.pallas_call(
        kernel,
        out_shape=out_shape,
        in_specs=ins,
        out_specs=jax.tree.map(lambda _: VMEM, out_shape),
        scratch_shapes=scratch,
        compiler_params=pltpu.CompilerParams(vmem_limit_bytes=mib * 2**20),
        cost_estimate=pl.CostEstimate(flops=1, bytes_accessed=1, transcendentals=0),
    )(*args)


def array(shape, dtype=jnp.float32):
    return jax.ShapeDtypeStruct(shape, dtype)


def coarse(embeddings, centroids, place):
    rows, width = embeddings.shape
    count = centroids.shape[0]
    half, sub, chunk = width // 2, 128, 256
    sent, stats, weights, inverse = call(
        coarse_kernel,
        (
            array((half + PACKED, rows), jnp.bfloat16),
            array((8, rows)),
            array((rows, count), jnp.bfloat16),
            array((rows, sub)),
        ),
        [SMEM, VMEM, VMEM],
        place,
        embeddings,
        centroids,
        scratch=[pltpu.VMEM((count // chunk, rows, chunk), jnp.float32)],
        mib=24,
    )
    kept, base = call(
        kept_kernel,
        (array((half, rows)), array((sub, rows))),
        [SMEM] + [VMEM] * 4,
        place,
        weights,
        inverse,
        centroids,
        embeddings,
        mib=24,
    )
    return kept, sent, stats, base


def chip(place, kept, got, stats):
    sub, rows, count = 128, stats.shape[1], 4
    blocks = [array((sub + PACKED, rows), jnp.bfloat16)] * (count - 1)
    return call(
        chip_kernel,
        [array((sub, rows)), array((8, rows))] + blocks,
        [SMEM] + [VMEM] * 3,
        place,
        kept,
        got,
        stats,
    )


def local(embeddings, centroids, codebook):
    _, book_rows, sub_width = codebook.shape
    y_count, z_count, x_count = lax.axis_size("y"), lax.axis_size("z"), lax.axis_size("x")
    words = book_rows * z_count
    place = jnp.stack([lax.axis_index(axis) for axis in ("c", "x", "y")]).astype(jnp.int32)

    own = codebook.reshape(book_rows, sub_width)
    book = exchange(jnp.broadcast_to(own, (z_count, book_rows, sub_width)), "z")
    book = book.reshape(words, sub_width)

    def ring(count, step):
        return [(i, (i + step) % count) for i in range(count)]

    kept, sent, stats, base = coarse(embeddings, centroids, place)
    got = lax.ppermute(sent, "c", ring(2, 1))
    mean, stats, *blocks = chip(place, kept, got, stats)
    gots = [lax.ppermute(block, "x", ring(x_count, step)) for step, block in enumerate(blocks, 1)]

    rows = base.shape[1]
    residual, copies = call(
        residual_kernel,
        (array((sub_width, rows), jnp.bfloat16), array((y_count, sub_width, rows), jnp.bfloat16)),
        [VMEM] * (len(gots) + 3),
        mean,
        stats,
        *gots,
        base,
    )
    book, copies = lax.optimization_barrier((book, copies))
    wide = exchange(copies, "y")

    raised, stats = call(
        score_kernel,
        (
            array((words, y_count * rows), jnp.bfloat16),
            array((y_count, y_count * PACKED, rows), jnp.bfloat16),
        ),
        [VMEM] * 2,
        book,
        wide,
        scratch=[pltpu.VMEM((y_count, words, rows), jnp.float32), pltpu.VMEM((words, 128), jnp.float32)],
        mib=24,
    )
    stats = exchange(stats, "y")
    rebuilt = lax.dot_general(book, raised, (((0,), (0,)), ((), ())), preferred_element_type=jnp.float32)
    stats, rebuilt = lax.optimization_barrier((stats, rebuilt))
    sums, factors = call(
        sum_kernel,
        (
            array((z_count, book_rows + 8, sub_width), jnp.bfloat16),
            array((8, y_count * rows)),
        ),
        [SMEM] + [VMEM] * 3,
        place,
        stats,
        wide,
        raised,
        scratch=[pltpu.VMEM((y_count * rows, 2 * sub_width), jnp.bfloat16)],
        mib=16,
    )

    sums = exchange(sums, "z")
    whole, *blocks = call(
        share_kernel,
        [array((sub_width, rows))] + [array((sub_width, rows), jnp.bfloat16)] * (y_count - 1),
        [SMEM] + [VMEM] * 2,
        place,
        rebuilt,
        factors,
    )
    for step, block in enumerate(blocks, 1):
        whole = whole + lax.ppermute(block, "y", ring(y_count, step)).astype(jnp.float32)
    pq_error = jnp.mean(jnp.square(residual.astype(jnp.float32) - whole), axis=0)
    new_codebook = call(last_kernel, array((book_rows, sub_width)), [VMEM] * 2, sums, own)
    return (residual, new_codebook[None], pq_error[None])


def solution(mesh):
    sizes = (4, 16, 4, 2)
    wide = Mesh(mesh.devices.reshape(sizes), ("y", "z", "x", "c"))
    rows = ("y", "z")
    placed = (P(rows, None), P(CENT, None), P(CENT, rows, None))
    return jax.shard_map(
        local,
        mesh=wide,
        in_specs=placed,
        out_specs=(P(CENT, rows), P(CENT, rows, None), P(CENT, rows)),
        check_vma=False,
    )
```

```python
import functools
import math

import jax
import jax.numpy as jnp
from jax import lax
from jax.experimental import pallas as pl
from jax.experimental.pallas import tpu as pltpu
from jax.sharding import Mesh, PartitionSpec as P

smoothing = 1.0
CENT = ("x", "c")


PACKED = 16


def exchange(parts, axis):
    return lax.all_to_all(parts, axis, 0, 0, tiled=True)


def wide_row(columns):
    return jnp.transpose(jnp.broadcast_to(columns, (columns.shape[0], 128)))[:1]


def coarse_kernel(place_ref, e_ref, c_ref, sent_ref, stats_ref, weights_ref, inverse_ref, logits_ref):
    rows, width = e_ref.shape
    chunks, _, chunk = logits_ref.shape
    used = sent_ref.shape[0] - PACKED
    scale = 2.0 / math.sqrt(width)

    def score(j, peak):
        block = c_ref[pl.ds(pl.multiple_of(j * chunk, chunk), chunk), :]
        wide = block.astype(jnp.float32)
        half_norm = wide_row(0.5 * jnp.sum(wide * wide, axis=1, keepdims=True))
        products = lax.dot_general(
            e_ref[...], block, (((1,), (1,)), ((), ())), preferred_element_type=jnp.float32
        )
        logits = (products - half_norm) * scale
        logits_ref[j] = logits
        for part in range(chunk // 128):
            peak = jnp.maximum(peak, logits[:, part * 128 : part * 128 + 128])
        return peak

    peak = lax.fori_loop(0, chunks, score, jnp.full((rows, 128), -jnp.inf, jnp.float32), unroll=2)
    peak = jnp.max(peak, axis=1, keepdims=True)

    def raise_(j, total):
        shifted = jnp.exp(logits_ref[j] - peak)
        weights_ref[:, pl.ds(pl.multiple_of(j * chunk, chunk), chunk)] = shifted.astype(jnp.bfloat16)
        for part in range(chunk // 128):
            total = total + shifted[:, part * 128 : part * 128 + 128]
        return total

    total = lax.fori_loop(0, chunks, raise_, jnp.zeros((rows, 128), jnp.float32), unroll=2)
    total = jnp.sum(total, axis=1, keepdims=True)
    inverse_ref[...] = jnp.broadcast_to(1.0 / total, inverse_ref.shape)
    pull(1 - place_ref[0], weights_ref, inverse_ref, c_ref, sent_ref)
    largest, total = wide_row(peak), wide_row(total)
    stats_ref[...] = jnp.concatenate([largest, total, jnp.zeros((6, rows), jnp.float32)], axis=0)
    sent_ref[used:, :] = packed(largest, total)


def pull(core, weights_ref, inverse_ref, c_ref, out_ref):
    sub = inverse_ref.shape[1]
    for pair in range(2):
        columns = [pl.ds(pl.multiple_of(((2 * pair + k) * 2 + core) * sub, sub), sub) for k in range(2)]
        block = jnp.concatenate([c_ref[:, column] for column in columns], axis=1)
        pulled = jnp.dot(weights_ref[...], block, preferred_element_type=jnp.float32)
        for k in range(2):
            part = pulled[:, k * sub : k * sub + sub] * inverse_ref[...]
            row = (2 * pair + k) * sub
            out_ref[row : row + sub, :] = jnp.transpose(part).astype(out_ref.dtype)


def kept_kernel(place_ref, weights_ref, inverse_ref, c_ref, e_ref, kept_ref, base_ref):
    pull(place_ref[0], weights_ref, inverse_ref, c_ref, kept_ref)
    sub = base_ref.shape[0]
    own = pl.multiple_of((2 * place_ref[1] + place_ref[0]) * sub, sub)
    base_ref[...] = jnp.transpose(e_ref[:, pl.ds(own, sub)].astype(jnp.float32))


def weigh(maxes, totals):
    largest = functools.reduce(jnp.maximum, maxes)
    shares = [jnp.exp(own - largest) * total for own, total in zip(maxes, totals)]
    whole = functools.reduce(jnp.add, shares)
    return [share / whole for share in shares], largest, whole


def terms_of(value, count=3):
    terms = []
    for _ in range(count):
        term = value.astype(jnp.bfloat16).astype(jnp.float32)
        terms.append(term)
        value = value - term
    return terms


def packed(largest, total):
    terms = terms_of(largest) + terms_of(total)
    terms.append(jnp.zeros((PACKED - len(terms), largest.shape[1]), jnp.float32))
    return jnp.concatenate(terms, axis=0).astype(jnp.bfloat16)


def unpacked(rows):
    wide = rows.astype(jnp.float32)
    return (wide[2:3] + wide[1:2]) + wide[0:1], (wide[5:6] + wide[4:5]) + wide[3:4]


def chip_kernel(place_ref, kept_ref, got_ref, stats_ref, mean_ref, chip_ref, *block_refs):
    sub, rows = mean_ref.shape
    count = len(block_refs) + 1
    used = count * sub
    other_max, other_total = unpacked(got_ref[used:, :])
    (own, other), largest, total = weigh(
        [stats_ref[0:1], other_max], [stats_ref[1:2], other_total]
    )
    chip_ref[...] = jnp.concatenate([largest, total, jnp.zeros((6, rows), jnp.float32)], axis=0)
    stats = packed(largest, total)
    for step in range(count):
        at = pl.ds(pl.multiple_of(lax.rem(place_ref[1] + step, count) * sub, sub), sub)
        mean = kept_ref[at, :] * own + got_ref[at, :].astype(jnp.float32) * other
        if step == 0:
            mean_ref[...] = mean
        else:
            block_refs[step - 1][:sub, :] = mean.astype(jnp.bfloat16)
            block_refs[step - 1][sub:, :] = stats


def residual_kernel(mean_ref, chip_ref, *refs):
    *got_refs, base_ref, residual_ref, copies_ref = refs
    sub = mean_ref.shape[0]
    stats = [(chip_ref[0:1], chip_ref[1:2])] + [unpacked(got[sub:, :]) for got in got_refs]
    shares, _, _ = weigh(*zip(*stats))
    mean = mean_ref[...] * shares[0]
    for got, share in zip(got_refs, shares[1:]):
        mean = mean + got[:sub, :].astype(jnp.float32) * share
    residual = (base_ref[...] - mean).astype(jnp.bfloat16)
    residual_ref[...] = residual
    for copy in range(copies_ref.shape[0]):
        copies_ref[copy] = residual


def half_kernel(book_ref, half_ref):
    wide = book_ref[...].astype(jnp.float32)
    half_ref[...] = jnp.broadcast_to(0.5 * jnp.sum(wide * wide, axis=1, keepdims=True), half_ref.shape)


def score_kernel(book_ref, half_ref, rows_ref, raised_hbm, stats_ref, own_ref, gaps_ref, raised_ref, sems):
    parts, sub, rows = rows_ref.shape
    words = book_ref.shape[0]
    scale = 2.0 / math.sqrt(sub)
    chunk = 256
    spans = [slice(at, at + chunk) for at in range(0, words, chunk)]
    packs = []
    stores = []
    for part in range(parts):
        peak = jnp.full((8, rows), -jnp.inf, jnp.float32)
        for at in spans:
            gap = jnp.dot(book_ref[at, :], rows_ref[part], preferred_element_type=jnp.float32)
            gap = gap - jnp.concatenate([half_ref[at, :]] * (rows // 128), axis=1)
            gaps_ref[part, at, :] = gap
            peak = jnp.maximum(peak, jnp.max(gap.reshape(chunk // 8, 8, rows), axis=0))
        peak = jnp.max(peak, axis=0, keepdims=True)
        total = jnp.zeros((8, rows), jnp.float32)
        for at in spans:
            raised = jnp.exp((gaps_ref[part, at, :] - peak) * scale)
            raised_ref[part, at, :] = raised.astype(jnp.bfloat16)
            total = total + jnp.sum(raised.reshape(chunk // 8, 8, rows), axis=0)
        stores.append(pltpu.make_async_copy(raised_ref.at[part], raised_hbm.at[part], sems.at[part]))
        stores[-1].start()
        total = jnp.sum(total, axis=0, keepdims=True)
        packs.append(packed(peak, total))
        own = jnp.concatenate([peak, 1.0 / total, jnp.zeros((6, rows), jnp.float32)], axis=0)
        own_ref[:, part * rows : part * rows + rows] = own
    pack = jnp.concatenate(packs, axis=0)
    for copy in range(stats_ref.shape[0]):
        stats_ref[copy] = pack
    for store in stores:
        store.wait()


def sum_kernel(stats_ref, own_ref, rows_ref, raised_ref, sums_ref, sides_ref):
    parts, sub, rows = rows_ref.shape
    targets, held, _ = sums_ref.shape
    owned = held - 8
    scale = 2.0 / math.sqrt(sub)
    for part in range(parts):
        at = slice(part * PACKED, part * PACKED + PACKED)
        stats = [unpacked(stats_ref[peer, at, :]) for peer in range(parts)]
        peak = functools.reduce(jnp.maximum, [own for own, _ in stats])
        whole = functools.reduce(jnp.add, [jnp.exp((own - peak) * scale) * total for own, total in stats])
        own = own_ref[0:1, part * rows : part * rows + rows]
        factor = jnp.exp((own - peak) * scale) / whole
        scaled = rows_ref[part].astype(jnp.float32) * factor
        high, low = (jnp.broadcast_to(term, (sub // 2, rows)) for term in terms_of(factor, 2))
        sides = jnp.transpose(jnp.concatenate([scaled, high, low], axis=0))
        sides_ref[part * rows : part * rows + rows, :] = sides.astype(jnp.bfloat16)
    row = lax.broadcasted_iota(jnp.int32, (128, 128), 0)
    diagonal = row == lax.broadcasted_iota(jnp.int32, (128, 128), 1)
    left = lax.broadcasted_iota(jnp.int32, (1, 128), 1) < 64
    empty = jnp.zeros((7, sub), jnp.float32)
    pair = 2 * owned
    for at in range(0, targets, 4):
        raised = [raised_ref[part, at * owned : (at + 4) * owned, :] for part in range(parts)]
        sums = jnp.dot(
            jnp.concatenate(raised, axis=1), sides_ref[...], preferred_element_type=jnp.float32
        )
        for k in range(2):
            both = sums[k * pair : k * pair + pair]
            counts = both[:, sub:]
            counts = counts + pltpu.roll(counts, sub // 2, 1)
            counts = jnp.sum(jnp.where(diagonal, counts, 0.0), axis=0, keepdims=True)
            high, low = terms_of(counts, 2)
            even = jnp.where(left, high, pltpu.roll(low, 64, 1))
            odd = jnp.where(left, pltpu.roll(high, 64, 1), low)
            for n, extra in enumerate((even, odd)):
                block = [both[n * owned : n * owned + owned, :sub], extra, empty]
                sums_ref[at + 2 * k + n] = jnp.concatenate(block, axis=0).astype(jnp.bfloat16)


def share_kernel(place_ref, rebuilt_ref, stats_ref, own_ref, *block_refs):
    sub, rows = own_ref.shape
    count = len(block_refs) + 1
    for step in range(count):
        part = lax.rem(place_ref[2] + step, count)
        at = pl.ds(pl.multiple_of(part * rows, 128), rows)
        rebuilt = rebuilt_ref[part] * stats_ref[1:2, at]
        if step == 0:
            own_ref[...] = rebuilt
        else:
            block_refs[step - 1][...] = rebuilt.astype(jnp.bfloat16)


def error_kernel(place_ref, stats_ref, residual_ref, own_ref, *refs):
    *got_refs, error_ref = refs
    sub, rows = own_ref.shape
    count = len(got_refs) + 1
    scale = 2.0 / math.sqrt(sub)
    at = pl.ds(pl.multiple_of(place_ref[2] * PACKED, PACKED), PACKED)
    stats = [unpacked(stats_ref[lax.rem(place_ref[2] + count - step, count), at, :]) for step in range(count)]
    shares, _, _ = weigh([peak * scale for peak, _ in stats], [total for _, total in stats])
    rebuilt = own_ref[...] * shares[0]
    for got, share in zip(got_refs, shares[1:]):
        rebuilt = rebuilt + got[...].astype(jnp.float32) * share
    gap = residual_ref[...].astype(jnp.float32) - rebuilt
    error_ref[...] = jnp.sum(gap * gap, axis=0, keepdims=True) * (1.0 / sub)


def last_kernel(sums_ref, own_ref, out_ref):
    parts = sums_ref.shape[0]
    words, sub = own_ref.shape
    total = sums_ref[0].astype(jnp.float32)
    for part in range(1, parts):
        total = total + sums_ref[part].astype(jnp.float32)
    pair = total[words : words + 1]
    counts = jnp.broadcast_to(pair + pltpu.roll(pair, 64, 1), (words, sub))
    diagonal = lax.broadcasted_iota(jnp.int32, (words, sub), 0) == lax.broadcasted_iota(jnp.int32, (words, sub), 1)
    counts = jnp.sum(jnp.where(diagonal, counts, 0.0), axis=1, keepdims=True)
    own = own_ref[...].astype(jnp.float32)
    out_ref[...] = (total[:words] + smoothing * own) / (counts + smoothing)


VMEM = pl.BlockSpec(memory_space=pltpu.VMEM)
SMEM = pl.BlockSpec(memory_space=pltpu.SMEM)
HBM = pl.BlockSpec(memory_space=pltpu.HBM)


def call(kernel, out_shape, ins, *args, outs=None, scratch=(), mib=8):
    return pl.pallas_call(
        kernel,
        out_shape=out_shape,
        in_specs=ins,
        out_specs=outs or jax.tree.map(lambda _: VMEM, out_shape),
        scratch_shapes=scratch,
        compiler_params=pltpu.CompilerParams(vmem_limit_bytes=mib * 2**20),
        cost_estimate=pl.CostEstimate(flops=1, bytes_accessed=1, transcendentals=0),
    )(*args)


def array(shape, dtype=jnp.float32):
    return jax.ShapeDtypeStruct(shape, dtype)


def coarse(embeddings, centroids, place):
    rows, width = embeddings.shape
    count = centroids.shape[0]
    half, sub, chunk = width // 2, 128, 256
    sent, stats, weights, inverse = call(
        coarse_kernel,
        (
            array((half + PACKED, rows), jnp.bfloat16),
            array((8, rows)),
            array((rows, count), jnp.bfloat16),
            array((rows, sub)),
        ),
        [SMEM, VMEM, VMEM],
        place,
        embeddings,
        centroids,
        scratch=[pltpu.VMEM((count // chunk, rows, chunk), jnp.float32)],
        mib=24,
    )
    kept, base = call(
        kept_kernel,
        (array((half, rows)), array((sub, rows))),
        [SMEM] + [VMEM] * 4,
        place,
        weights,
        inverse,
        centroids,
        embeddings,
        mib=24,
    )
    return kept, sent, stats, base


def chip(place, kept, got, stats):
    sub, rows, count = 128, stats.shape[1], 4
    blocks = [array((sub + PACKED, rows), jnp.bfloat16)] * (count - 1)
    return call(
        chip_kernel,
        [array((sub, rows)), array((8, rows))] + blocks,
        [SMEM] + [VMEM] * 3,
        place,
        kept,
        got,
        stats,
    )


def local(embeddings, centroids, codebook):
    _, book_rows, sub_width = codebook.shape
    y_count, z_count, x_count = lax.axis_size("y"), lax.axis_size("z"), lax.axis_size("x")
    words = book_rows * z_count
    place = jnp.stack([lax.axis_index(axis) for axis in ("c", "x", "y")]).astype(jnp.int32)

    own = codebook.reshape(book_rows, sub_width)
    book = exchange(jnp.broadcast_to(own, (z_count, book_rows, sub_width)), "z")
    book = book.reshape(words, sub_width)

    def ring(count, step):
        return [(i, (i + step) % count) for i in range(count)]

    kept, sent, stats, base = coarse(embeddings, centroids, place)
    got = lax.ppermute(sent, "c", ring(2, 1))
    mean, stats, *blocks = chip(place, kept, got, stats)
    gots = [lax.ppermute(block, "x", ring(x_count, step)) for step, block in enumerate(blocks, 1)]

    rows = base.shape[1]
    residual, copies = call(
        residual_kernel,
        (array((sub_width, rows), jnp.bfloat16), array((y_count, sub_width, rows), jnp.bfloat16)),
        [VMEM] * (len(gots) + 3),
        mean,
        stats,
        *gots,
        base,
    )
    book, copies = lax.optimization_barrier((book, copies))
    wide = exchange(copies, "y")
    half = call(half_kernel, array((words, 128)), [VMEM], book)
    wide, half = lax.optimization_barrier((wide, half))

    raised, stats, own_stats = call(
        score_kernel,
        (
            array((y_count, words, rows), jnp.bfloat16),
            array((y_count, y_count * PACKED, rows), jnp.bfloat16),
            array((8, y_count * rows)),
        ),
        [VMEM] * 3,
        book,
        half,
        wide,
        outs=(HBM, VMEM, VMEM),
        scratch=[
            pltpu.VMEM((y_count, words, rows), jnp.float32),
            pltpu.VMEM((y_count, words, rows), jnp.bfloat16),
            pltpu.SemaphoreType.DMA((y_count,)),
        ],
        mib=51,
    )
    stats = exchange(stats, "y")
    rebuilt = jnp.einsum("kd,pkr->pdr", book, raised, preferred_element_type=jnp.float32)
    whole, *blocks = call(
        share_kernel,
        [array((sub_width, rows))] + [array((sub_width, rows), jnp.bfloat16)] * (y_count - 1),
        [SMEM] + [VMEM] * 2,
        place,
        rebuilt,
        own_stats,
    )
    stats, whole, *blocks = lax.optimization_barrier((stats, whole, *blocks))
    sums = call(
        sum_kernel,
        array((z_count, book_rows + 8, sub_width), jnp.bfloat16),
        [VMEM] * 4,
        stats,
        own_stats,
        wide,
        raised,
        scratch=[pltpu.VMEM((y_count * rows, 2 * sub_width), jnp.bfloat16)],
        mib=16,
    )

    sums = exchange(sums, "z")
    gots = [lax.ppermute(block, "y", ring(y_count, step)) for step, block in enumerate(blocks, 1)]
    pq_error = call(
        error_kernel, array((1, rows)), [SMEM] + [VMEM] * 6, place, stats, residual, whole, *gots
    )
    new_codebook = call(last_kernel, array((book_rows, sub_width)), [VMEM] * 2, sums, own)
    return (residual, new_codebook[None], pq_error)


def solution(mesh):
    sizes = (4, 16, 4, 2)
    wide = Mesh(mesh.devices.reshape(sizes), ("y", "z", "x", "c"))
    rows = ("y", "z")
    placed = (P(rows, None), P(CENT, None), P(CENT, rows, None))
    return jax.shard_map(
        local,
        mesh=wide,
        in_specs=placed,
        out_specs=(P(CENT, rows), P(CENT, rows, None), P(CENT, rows)),
        check_vma=False,
    )
```

```python
import functools
import math

import jax
import jax.numpy as jnp
from jax import lax
from jax.experimental import pallas as pl
from jax.experimental.pallas import tpu as pltpu
from jax.sharding import Mesh, PartitionSpec as P

smoothing = 1.0
CENT = ("x", "c")


PACKED = 16


def exchange(parts, axis):
    return lax.all_to_all(parts, axis, 0, 0, tiled=True)


def wide_row(columns):
    return jnp.transpose(jnp.broadcast_to(columns, (columns.shape[0], 128)))[:1]


def coarse_kernel(place_ref, e_ref, c_ref, sent_ref, stats_ref, weights_ref, inverse_ref, logits_ref):
    rows, width = e_ref.shape
    chunks, _, chunk = logits_ref.shape
    used = sent_ref.shape[0] - PACKED
    scale = 2.0 / math.sqrt(width)

    def score(j, peak):
        block = c_ref[pl.ds(pl.multiple_of(j * chunk, chunk), chunk), :]
        wide = block.astype(jnp.float32)
        half_norm = wide_row(0.5 * jnp.sum(wide * wide, axis=1, keepdims=True))
        products = lax.dot_general(
            e_ref[...], block, (((1,), (1,)), ((), ())), preferred_element_type=jnp.float32
        )
        logits = (products - half_norm) * scale
        logits_ref[j] = logits
        for part in range(chunk // 128):
            peak = jnp.maximum(peak, logits[:, part * 128 : part * 128 + 128])
        return peak

    peak = lax.fori_loop(0, chunks, score, jnp.full((rows, 128), -jnp.inf, jnp.float32), unroll=2)
    peak = jnp.max(peak, axis=1, keepdims=True)

    def raise_(j, total):
        shifted = jnp.exp(logits_ref[j] - peak)
        weights_ref[:, pl.ds(pl.multiple_of(j * chunk, chunk), chunk)] = shifted.astype(jnp.bfloat16)
        for part in range(chunk // 128):
            total = total + shifted[:, part * 128 : part * 128 + 128]
        return total

    total = lax.fori_loop(0, chunks, raise_, jnp.zeros((rows, 128), jnp.float32), unroll=2)
    total = jnp.sum(total, axis=1, keepdims=True)
    inverse_ref[...] = jnp.broadcast_to(1.0 / total, inverse_ref.shape)
    pull(1 - place_ref[0], weights_ref, inverse_ref, c_ref, sent_ref)
    largest, total = wide_row(peak), wide_row(total)
    stats_ref[...] = jnp.concatenate([largest, total, jnp.zeros((6, rows), jnp.float32)], axis=0)
    sent_ref[used:, :] = packed(largest, total)


def pull(core, weights_ref, inverse_ref, c_ref, out_ref):
    sub = inverse_ref.shape[1]
    for pair in range(2):
        columns = [pl.ds(pl.multiple_of(((2 * pair + k) * 2 + core) * sub, sub), sub) for k in range(2)]
        block = jnp.concatenate([c_ref[:, column] for column in columns], axis=1)
        pulled = jnp.dot(weights_ref[...], block, preferred_element_type=jnp.float32)
        for k in range(2):
            part = pulled[:, k * sub : k * sub + sub] * inverse_ref[...]
            row = (2 * pair + k) * sub
            out_ref[row : row + sub, :] = jnp.transpose(part).astype(out_ref.dtype)


def kept_kernel(place_ref, weights_ref, inverse_ref, c_ref, e_ref, kept_ref, base_ref):
    pull(place_ref[0], weights_ref, inverse_ref, c_ref, kept_ref)
    sub = base_ref.shape[0]
    own = pl.multiple_of((2 * place_ref[1] + place_ref[0]) * sub, sub)
    base_ref[...] = jnp.transpose(e_ref[:, pl.ds(own, sub)].astype(jnp.float32))


def weigh(maxes, totals):
    largest = functools.reduce(jnp.maximum, maxes)
    shares = [jnp.exp(own - largest) * total for own, total in zip(maxes, totals)]
    whole = functools.reduce(jnp.add, shares)
    return [share / whole for share in shares], largest, whole


def terms_of(value, count=3):
    terms = []
    for _ in range(count):
        term = value.astype(jnp.bfloat16).astype(jnp.float32)
        terms.append(term)
        value = value - term
    return terms


def packed(largest, total):
    terms = terms_of(largest) + terms_of(total)
    terms.append(jnp.zeros((PACKED - len(terms), largest.shape[1]), jnp.float32))
    return jnp.concatenate(terms, axis=0).astype(jnp.bfloat16)


def unpacked(rows):
    wide = rows.astype(jnp.float32)
    return (wide[2:3] + wide[1:2]) + wide[0:1], (wide[5:6] + wide[4:5]) + wide[3:4]


def chip_kernel(place_ref, kept_ref, got_ref, stats_ref, mean_ref, chip_ref, *block_refs):
    sub, rows = mean_ref.shape
    count = len(block_refs) + 1
    used = count * sub
    other_max, other_total = unpacked(got_ref[used:, :])
    (own, other), largest, total = weigh(
        [stats_ref[0:1], other_max], [stats_ref[1:2], other_total]
    )
    chip_ref[...] = jnp.concatenate([largest, total, jnp.zeros((6, rows), jnp.float32)], axis=0)
    stats = packed(largest, total)
    for step in range(count):
        at = pl.ds(pl.multiple_of(lax.rem(place_ref[1] + step, count) * sub, sub), sub)
        mean = kept_ref[at, :] * own + got_ref[at, :].astype(jnp.float32) * other
        if step == 0:
            mean_ref[...] = mean
        else:
            block_refs[step - 1][:sub, :] = mean.astype(jnp.bfloat16)
            block_refs[step - 1][sub:, :] = stats


def quantize_kernel(mean_ref, chip_ref, *refs):
    *got_refs, base_ref, book_ref, residual_ref, sums_ref, raised_hbm, inverse_ref, gaps_ref, raised_ref, sems = refs
    sub, rows = mean_ref.shape
    parts, held, _ = sums_ref.shape
    words = book_ref.shape[0]
    quarter = words // parts
    scale = 2.0 / math.sqrt(sub)
    stats = [(chip_ref[0:1], chip_ref[1:2])] + [unpacked(got[sub:, :]) for got in got_refs]
    shares, _, _ = weigh(*zip(*stats))
    mean = mean_ref[...] * shares[0]
    for got, share in zip(got_refs, shares[1:]):
        mean = mean + got[:sub, :].astype(jnp.float32) * share
    residual = (base_ref[...] - mean).astype(jnp.bfloat16)
    residual_ref[...] = residual

    spans = [slice(at, at + 256) for at in range(0, words, 256)]
    peak = jnp.full((8, rows), -jnp.inf, jnp.float32)
    for at in spans:
        block = book_ref[at, :]
        wide = block.astype(jnp.float32)
        half = 0.5 * jnp.sum(wide * wide, axis=1, keepdims=True)
        gap = jnp.dot(block, residual, preferred_element_type=jnp.float32) - half
        gaps_ref[at, :] = gap
        peak = jnp.maximum(peak, jnp.max(gap.reshape(32, 8, rows), axis=0))
    peak = jnp.max(peak, axis=0, keepdims=True)
    total = jnp.zeros((8, rows), jnp.float32)
    stores = []
    for j, at in enumerate(spans):
        raised = jnp.exp((gaps_ref[at, :] - peak) * scale)
        raised_ref[at, :] = raised.astype(jnp.bfloat16)
        total = total + jnp.sum(raised.reshape(32, 8, rows), axis=0)
        if j % 4 == 3:
            at = slice((j - 3) * 256, (j + 1) * 256)
            stores.append(pltpu.make_async_copy(raised_ref.at[at, :], raised_hbm.at[at, :], sems.at[j // 4]))
            stores[-1].start()
    inverse = 1.0 / jnp.sum(total, axis=0, keepdims=True)
    inverse_ref[...] = jnp.broadcast_to(inverse, inverse_ref.shape)

    scaled = residual.astype(jnp.float32) * inverse
    high, low = (jnp.broadcast_to(term, (sub // 2, rows)) for term in terms_of(inverse, 2))
    sides = jnp.transpose(jnp.concatenate([scaled, high, low], axis=0)).astype(jnp.bfloat16)
    row = lax.broadcasted_iota(jnp.int32, (128, 128), 0)
    diagonal = row == lax.broadcasted_iota(jnp.int32, (128, 128), 1)
    for part in range(parts):
        lines = []
        for at in range(0, quarter, 256):
            span = slice(part * quarter + at, part * quarter + at + 256)
            sums = jnp.dot(raised_ref[span, :], sides, preferred_element_type=jnp.float32)
            sums_ref[part, at : at + 256, :] = sums[:, :sub].astype(jnp.bfloat16)
            counts = sums[:, sub:]
            counts = counts + pltpu.roll(counts, sub // 2, 1)
            for k in range(2):
                tile = counts[k * 128 : k * 128 + 128]
                lines.append(jnp.sum(jnp.where(diagonal, tile, 0.0), axis=0, keepdims=True))
        counts = jnp.concatenate(lines, axis=0)
        sums_ref[part, quarter:, :] = jnp.concatenate(terms_of(counts, 2), axis=0).astype(jnp.bfloat16)
    for store in stores:
        store.wait()


def middle_kernel(sums_ref, out_ref):
    parts, held, sub = sums_ref.shape
    targets, rows, _ = out_ref.shape
    words = rows - 8
    quarter = targets * words
    counts = jnp.zeros((quarter // 128, 128), jnp.float32)
    for part in range(parts):
        pair = sums_ref[part, quarter:, :].astype(jnp.float32)
        counts = counts + (pair[: quarter // 128] + pair[quarter // 128 :])
    high, low = terms_of(counts, 2)
    left = lax.broadcasted_iota(jnp.int32, high.shape, 1) < 64
    even = jnp.where(left, high, pltpu.roll(low, 64, 1))
    odd = jnp.where(left, pltpu.roll(high, 64, 1), low)
    for target in range(targets):
        at = slice(target * words, target * words + words)
        total = sums_ref[0, at, :].astype(jnp.float32)
        for part in range(1, parts):
            total = total + sums_ref[part, at, :].astype(jnp.float32)
        row = (even if target % 2 == 0 else odd)[target // 2 : target // 2 + 1]
        row = jnp.concatenate([row, jnp.zeros((7, sub), jnp.float32)], axis=0)
        out_ref[target] = jnp.concatenate([total, row], axis=0).astype(jnp.bfloat16)


def last_kernel(sums_ref, own_ref, out_ref):
    parts = sums_ref.shape[0]
    words, sub = own_ref.shape
    total = sums_ref[0].astype(jnp.float32)
    for part in range(1, parts):
        total = total + sums_ref[part].astype(jnp.float32)
    pair = total[words : words + 1]
    counts = jnp.broadcast_to(pair + pltpu.roll(pair, 64, 1), (words, sub))
    diagonal = lax.broadcasted_iota(jnp.int32, (words, sub), 0) == lax.broadcasted_iota(jnp.int32, (words, sub), 1)
    counts = jnp.sum(jnp.where(diagonal, counts, 0.0), axis=1, keepdims=True)
    own = own_ref[...].astype(jnp.float32)
    out_ref[...] = (total[:words] + smoothing * own) / (counts + smoothing)


VMEM = pl.BlockSpec(memory_space=pltpu.VMEM)
SMEM = pl.BlockSpec(memory_space=pltpu.SMEM)
HBM = pl.BlockSpec(memory_space=pltpu.HBM)


def call(kernel, out_shape, ins, *args, outs=None, scratch=(), mib=8):
    return pl.pallas_call(
        kernel,
        out_shape=out_shape,
        in_specs=ins,
        out_specs=outs or jax.tree.map(lambda _: VMEM, out_shape),
        scratch_shapes=scratch,
        compiler_params=pltpu.CompilerParams(vmem_limit_bytes=mib * 2**20),
        cost_estimate=pl.CostEstimate(flops=1, bytes_accessed=1, transcendentals=0),
    )(*args)


def array(shape, dtype=jnp.float32):
    return jax.ShapeDtypeStruct(shape, dtype)


def coarse(embeddings, centroids, place):
    rows, width = embeddings.shape
    count = centroids.shape[0]
    half, sub, chunk = width // 2, 128, 256
    sent, stats, weights, inverse = call(
        coarse_kernel,
        (
            array((half + PACKED, rows), jnp.bfloat16),
            array((8, rows)),
            array((rows, count), jnp.bfloat16),
            array((rows, sub)),
        ),
        [SMEM, VMEM, VMEM],
        place,
        embeddings,
        centroids,
        scratch=[pltpu.VMEM((count // chunk, rows, chunk), jnp.float32)],
        mib=24,
    )
    kept, base = call(
        kept_kernel,
        (array((half, rows)), array((sub, rows))),
        [SMEM] + [VMEM] * 4,
        place,
        weights,
        inverse,
        centroids,
        embeddings,
        mib=24,
    )
    return kept, sent, stats, base


def chip(place, kept, got, stats):
    sub, rows, count = 128, stats.shape[1], 4
    blocks = [array((sub + PACKED, rows), jnp.bfloat16)] * (count - 1)
    return call(
        chip_kernel,
        [array((sub, rows)), array((8, rows))] + blocks,
        [SMEM] + [VMEM] * 3,
        place,
        kept,
        got,
        stats,
    )


def quantize(mean, stats, gots, base, book, parts):
    (sub, rows), words = mean.shape, book.shape[0]
    quarter = words // parts
    return call(
        quantize_kernel,
        (
            array((sub, rows), jnp.bfloat16),
            array((parts, quarter + quarter // 64, sub), jnp.bfloat16),
            array((words, rows), jnp.bfloat16),
            array((8, rows)),
        ),
        [VMEM] * (len(gots) + 4),
        mean,
        stats,
        *gots,
        base,
        book,
        outs=(VMEM, VMEM, HBM, VMEM),
        scratch=[
            pltpu.VMEM((words, rows), jnp.float32),
            pltpu.VMEM((words, rows), jnp.bfloat16),
            pltpu.SemaphoreType.DMA((parts,)),
        ],
        mib=51,
    )


def local(embeddings, centroids, codebook):
    _, book_rows, sub_width = codebook.shape
    y_count, z_count, x_count = lax.axis_size("y"), lax.axis_size("z"), lax.axis_size("x")
    words = book_rows * y_count * z_count
    place = jnp.stack([lax.axis_index("c"), lax.axis_index("x")]).astype(jnp.int32)

    own = codebook.reshape(book_rows, sub_width)
    book = exchange(jnp.broadcast_to(own, (z_count, book_rows, sub_width)), "z")
    book = book.reshape(words // y_count, sub_width)

    kept, sent, stats, base = coarse(embeddings, centroids, place)
    got = lax.ppermute(sent, "c", [(0, 1), (1, 0)])
    mean, stats, *blocks = chip(place, kept, got, stats)
    book, *blocks = lax.optimization_barrier((book, *blocks))
    gots = [
        lax.ppermute(block, "x", [(i, (i + step) % x_count) for i in range(x_count)])
        for step, block in enumerate(blocks, 1)
    ]
    book = exchange(jnp.broadcast_to(book, (y_count,) + book.shape), "y").reshape(words, sub_width)
    residual, sums, raised, inverse = quantize(mean, stats, gots, base, book, y_count)

    sums = exchange(sums, "y")
    rebuilt = lax.dot_general(
        book, raised, (((0,), (0,)), ((), ())), preferred_element_type=jnp.float32
    ) * inverse[:1]
    pq_error = jnp.mean(jnp.square(residual.astype(jnp.float32) - rebuilt), axis=0)
    sums, pq_error = lax.optimization_barrier((sums, pq_error[None]))
    sums = call(
        middle_kernel, array((z_count, book_rows + 8, sub_width), jnp.bfloat16), [VMEM], sums
    )
    sums = exchange(sums, "z")
    new_codebook = call(last_kernel, array((book_rows, sub_width)), [VMEM] * 2, sums, own)
    return (residual, new_codebook[None], pq_error)


def solution(mesh):
    sizes = (4, 16, 4, 2)
    wide = Mesh(mesh.devices.reshape(sizes), ("y", "z", "x", "c"))
    rows = ("y", "z")
    placed = (P(rows, None), P(CENT, None), P(CENT, rows, None))
    return jax.shard_map(
        local,
        mesh=wide,
        in_specs=placed,
        out_specs=(P(CENT, rows), P(CENT, rows, None), P(CENT, rows)),
        check_vma=False,
    )
```

```python
import functools
import math

import jax
import jax.numpy as jnp
from jax import lax
from jax.experimental import pallas as pl
from jax.experimental.pallas import tpu as pltpu
from jax.sharding import Mesh, PartitionSpec as P

smoothing = 1.0
CENT = ("x", "c")


PACKED = 16


def exchange(parts, axis):
    return lax.all_to_all(parts, axis, 0, 0, tiled=True)


def wide_row(columns):
    return jnp.transpose(jnp.broadcast_to(columns, (columns.shape[0], 128)))[:1]


def coarse_kernel(
    place_ref, e_hbm, c_hbm, sent_ref, stats_ref, weights_ref, inverse_ref, e_ref, c_ref, logits_ref, e_sem, c_sems
):
    rows, width = e_ref.shape
    chunks, _, chunk = logits_ref.shape
    used = sent_ref.shape[0] - PACKED
    scale = 2.0 / math.sqrt(width)
    spans = [slice(j * chunk, j * chunk + chunk) for j in range(chunks)]
    whole = pltpu.make_async_copy(e_hbm, e_ref, e_sem)
    whole.start()
    copies = [
        pltpu.make_async_copy(c_hbm.at[at, :], c_ref.at[at, :], c_sems.at[j]) for j, at in enumerate(spans)
    ]
    for copy in copies:
        copy.start()
    whole.wait()
    peak = jnp.full((rows, 128), -jnp.inf, jnp.float32)
    for j, at in enumerate(spans):
        copies[j].wait()
        block = c_ref[at, :]
        wide = block.astype(jnp.float32)
        half_norm = wide_row(0.5 * jnp.sum(wide * wide, axis=1, keepdims=True))
        products = lax.dot_general(
            e_ref[...], block, (((1,), (1,)), ((), ())), preferred_element_type=jnp.float32
        )
        logits = (products - half_norm) * scale
        logits_ref[j] = logits
        for part in range(chunk // 128):
            peak = jnp.maximum(peak, logits[:, part * 128 : part * 128 + 128])
    peak = jnp.max(peak, axis=1, keepdims=True)
    total = jnp.zeros((rows, 128), jnp.float32)
    for j, at in enumerate(spans):
        shifted = jnp.exp(logits_ref[j] - peak)
        weights_ref[:, at] = shifted.astype(jnp.bfloat16)
        for part in range(chunk // 128):
            total = total + shifted[:, part * 128 : part * 128 + 128]
    total = jnp.sum(total, axis=1, keepdims=True)
    inverse_ref[...] = jnp.broadcast_to(1.0 / total, inverse_ref.shape)
    sub = inverse_ref.shape[1]
    blocks = [c_ref.at[:, owned(place_ref, 1 - place_ref[0], k, sub)] for k in range(4)]
    pull(blocks, weights_ref, inverse_ref, sent_ref)
    largest, total = wide_row(peak), wide_row(total)
    stats_ref[...] = jnp.concatenate([largest, total, jnp.zeros((6, rows), jnp.float32)], axis=0)
    sent_ref[used:, :] = packed(largest, total)


def owned(place_ref, core, column, sub):
    return pl.ds(pl.multiple_of((2 * column + core) * sub, sub), sub)


def pull(blocks, weights_ref, inverse_ref, out_ref):
    sub = inverse_ref.shape[1]
    for pair in range(0, len(blocks), 2):
        block = jnp.concatenate([blocks[pair][...], blocks[pair + 1][...]], axis=1)
        pulled = jnp.dot(weights_ref[...], block, preferred_element_type=jnp.float32)
        for k in range(2):
            part = pulled[:, k * sub : k * sub + sub] * inverse_ref[...]
            row = (pair + k) * sub
            out_ref[row : row + sub, :] = jnp.transpose(part).astype(out_ref.dtype)


def kept_kernel(place_ref, weights_ref, inverse_ref, c_hbm, e_hbm, kept_ref, base_ref, c_ref, e_ref, sems, e_sem):
    sub = base_ref.shape[0]
    core = place_ref[0]
    copies = [
        pltpu.make_async_copy(c_hbm.at[:, owned(place_ref, core, k, sub)], c_ref.at[k], sems.at[k]) for k in range(4)
    ]
    copies.append(pltpu.make_async_copy(e_hbm.at[:, owned(place_ref, core, place_ref[1], sub)], e_ref, e_sem))
    for copy in copies:
        copy.start()
    for copy in copies:
        copy.wait()
    pull([c_ref.at[k] for k in range(4)], weights_ref, inverse_ref, kept_ref)
    base_ref[...] = jnp.transpose(e_ref[...].astype(jnp.float32))


def weigh(maxes, totals):
    largest = functools.reduce(jnp.maximum, maxes)
    shares = [jnp.exp(own - largest) * total for own, total in zip(maxes, totals)]
    whole = functools.reduce(jnp.add, shares)
    return [share / whole for share in shares], largest, whole


def terms_of(value, count=3):
    terms = []
    for _ in range(count):
        term = value.astype(jnp.bfloat16).astype(jnp.float32)
        terms.append(term)
        value = value - term
    return terms


def packed(largest, total):
    terms = terms_of(largest) + terms_of(total)
    terms.append(jnp.zeros((PACKED - len(terms), largest.shape[1]), jnp.float32))
    return jnp.concatenate(terms, axis=0).astype(jnp.bfloat16)


def unpacked(rows):
    wide = rows.astype(jnp.float32)
    return (wide[2:3] + wide[1:2]) + wide[0:1], (wide[5:6] + wide[4:5]) + wide[3:4]


def chip_kernel(place_ref, kept_ref, got_ref, stats_ref, mean_ref, chip_ref, *block_refs):
    sub, rows = mean_ref.shape
    count = len(block_refs) + 1
    used = count * sub
    other_max, other_total = unpacked(got_ref[used:, :])
    (own, other), largest, total = weigh(
        [stats_ref[0:1], other_max], [stats_ref[1:2], other_total]
    )
    chip_ref[...] = jnp.concatenate([largest, total, jnp.zeros((6, rows), jnp.float32)], axis=0)
    stats = packed(largest, total)
    for step in range(count):
        at = pl.ds(pl.multiple_of(lax.rem(place_ref[1] + step, count) * sub, sub), sub)
        mean = kept_ref[at, :] * own + got_ref[at, :].astype(jnp.float32) * other
        if step == 0:
            mean_ref[...] = mean
        else:
            block_refs[step - 1][:sub, :] = mean.astype(jnp.bfloat16)
            block_refs[step - 1][sub:, :] = stats


def quantize_kernel(mean_ref, chip_ref, *refs):
    *got_refs, base_ref, book_ref, residual_ref, sums_ref, raised_hbm, inverse_ref, gaps_ref, raised_ref, sems = refs
    sub, rows = mean_ref.shape
    parts, held, _ = sums_ref.shape
    words = book_ref.shape[0]
    quarter = words // parts
    scale = 2.0 / math.sqrt(sub)
    stats = [(chip_ref[0:1], chip_ref[1:2])] + [unpacked(got[sub:, :]) for got in got_refs]
    shares, _, _ = weigh(*zip(*stats))
    mean = mean_ref[...] * shares[0]
    for got, share in zip(got_refs, shares[1:]):
        mean = mean + got[:sub, :].astype(jnp.float32) * share
    residual = (base_ref[...] - mean).astype(jnp.bfloat16)
    residual_ref[...] = residual

    spans = [slice(at, at + 256) for at in range(0, words, 256)]
    peak = jnp.full((8, rows), -jnp.inf, jnp.float32)
    for at in spans:
        block = book_ref[at, :]
        wide = block.astype(jnp.float32)
        half = 0.5 * jnp.sum(wide * wide, axis=1, keepdims=True)
        gap = jnp.dot(block, residual, preferred_element_type=jnp.float32) - half
        gaps_ref[at, :] = gap
        peak = jnp.maximum(peak, jnp.max(gap.reshape(32, 8, rows), axis=0))
    peak = jnp.max(peak, axis=0, keepdims=True)
    total = jnp.zeros((8, rows), jnp.float32)
    stores = []
    for j, at in enumerate(spans):
        raised = jnp.exp((gaps_ref[at, :] - peak) * scale)
        raised_ref[at, :] = raised.astype(jnp.bfloat16)
        total = total + jnp.sum(raised.reshape(32, 8, rows), axis=0)
        if j % 4 == 3:
            at = slice((j - 3) * 256, (j + 1) * 256)
            stores.append(pltpu.make_async_copy(raised_ref.at[at, :], raised_hbm.at[at, :], sems.at[j // 4]))
            stores[-1].start()
    inverse = 1.0 / jnp.sum(total, axis=0, keepdims=True)
    inverse_ref[...] = jnp.broadcast_to(inverse, inverse_ref.shape)

    scaled = residual.astype(jnp.float32) * inverse
    high, low = (jnp.broadcast_to(term, (sub // 2, rows)) for term in terms_of(inverse, 2))
    sides = jnp.transpose(jnp.concatenate([scaled, high, low], axis=0)).astype(jnp.bfloat16)
    row = lax.broadcasted_iota(jnp.int32, (128, 128), 0)
    diagonal = row == lax.broadcasted_iota(jnp.int32, (128, 128), 1)
    for part in range(parts):
        lines = []
        for at in range(0, quarter, 256):
            span = slice(part * quarter + at, part * quarter + at + 256)
            sums = jnp.dot(raised_ref[span, :], sides, preferred_element_type=jnp.float32)
            sums_ref[part, at : at + 256, :] = sums[:, :sub].astype(jnp.bfloat16)
            counts = sums[:, sub:]
            counts = counts + pltpu.roll(counts, sub // 2, 1)
            for k in range(2):
                tile = counts[k * 128 : k * 128 + 128]
                lines.append(jnp.sum(jnp.where(diagonal, tile, 0.0), axis=0, keepdims=True))
        counts = jnp.concatenate(lines, axis=0)
        sums_ref[part, quarter:, :] = jnp.concatenate(terms_of(counts, 2), axis=0).astype(jnp.bfloat16)
    for store in stores:
        store.wait()


def middle_kernel(sums_ref, out_ref):
    parts, held, sub = sums_ref.shape
    targets, rows, _ = out_ref.shape
    words = rows - 8
    quarter = targets * words
    counts = jnp.zeros((quarter // 128, 128), jnp.float32)
    for part in range(parts):
        pair = sums_ref[part, quarter:, :].astype(jnp.float32)
        counts = counts + (pair[: quarter // 128] + pair[quarter // 128 :])
    high, low = terms_of(counts, 2)
    left = lax.broadcasted_iota(jnp.int32, high.shape, 1) < 64
    even = jnp.where(left, high, pltpu.roll(low, 64, 1))
    odd = jnp.where(left, pltpu.roll(high, 64, 1), low)
    for target in range(targets):
        at = slice(target * words, target * words + words)
        total = sums_ref[0, at, :].astype(jnp.float32)
        for part in range(1, parts):
            total = total + sums_ref[part, at, :].astype(jnp.float32)
        row = (even if target % 2 == 0 else odd)[target // 2 : target // 2 + 1]
        row = jnp.concatenate([row, jnp.zeros((7, sub), jnp.float32)], axis=0)
        out_ref[target] = jnp.concatenate([total, row], axis=0).astype(jnp.bfloat16)


def last_kernel(sums_ref, own_ref, out_ref):
    parts = sums_ref.shape[0]
    words, sub = own_ref.shape
    total = sums_ref[0].astype(jnp.float32)
    for part in range(1, parts):
        total = total + sums_ref[part].astype(jnp.float32)
    pair = total[words : words + 1]
    counts = jnp.broadcast_to(pair + pltpu.roll(pair, 64, 1), (words, sub))
    diagonal = lax.broadcasted_iota(jnp.int32, (words, sub), 0) == lax.broadcasted_iota(jnp.int32, (words, sub), 1)
    counts = jnp.sum(jnp.where(diagonal, counts, 0.0), axis=1, keepdims=True)
    own = own_ref[...].astype(jnp.float32)
    out_ref[...] = (total[:words] + smoothing * own) / (counts + smoothing)


VMEM = pl.BlockSpec(memory_space=pltpu.VMEM)
SMEM = pl.BlockSpec(memory_space=pltpu.SMEM)
HBM = pl.BlockSpec(memory_space=pltpu.HBM)


def call(kernel, out_shape, ins, *args, outs=None, scratch=(), mib=8):
    return pl.pallas_call(
        kernel,
        out_shape=out_shape,
        in_specs=ins,
        out_specs=outs or jax.tree.map(lambda _: VMEM, out_shape),
        scratch_shapes=scratch,
        compiler_params=pltpu.CompilerParams(vmem_limit_bytes=mib * 2**20),
        cost_estimate=pl.CostEstimate(flops=1, bytes_accessed=1, transcendentals=0),
    )(*args)


def array(shape, dtype=jnp.float32):
    return jax.ShapeDtypeStruct(shape, dtype)


def coarse(embeddings, centroids, place):
    rows, width = embeddings.shape
    count = centroids.shape[0]
    half, sub, chunk = width // 2, 128, 256
    chunks = count // chunk
    sent, stats, weights, inverse = call(
        coarse_kernel,
        (
            array((half + PACKED, rows), jnp.bfloat16),
            array((8, rows)),
            array((rows, count), jnp.bfloat16),
            array((rows, sub)),
        ),
        [SMEM, HBM, HBM],
        place,
        embeddings,
        centroids,
        scratch=[
            pltpu.VMEM((rows, width), jnp.bfloat16),
            pltpu.VMEM((count, width), jnp.bfloat16),
            pltpu.VMEM((chunks, rows, chunk), jnp.float32),
            pltpu.SemaphoreType.DMA,
            pltpu.SemaphoreType.DMA((chunks,)),
        ],
        mib=56,
    )
    kept, base = call(
        kept_kernel,
        (array((half, rows)), array((sub, rows))),
        [SMEM, VMEM, VMEM, HBM, HBM],
        place,
        weights,
        inverse,
        centroids,
        embeddings,
        scratch=[
            pltpu.VMEM((4, count, sub), jnp.bfloat16),
            pltpu.VMEM((rows, sub), jnp.bfloat16),
            pltpu.SemaphoreType.DMA((4,)),
            pltpu.SemaphoreType.DMA,
        ],
        mib=56,
    )
    return kept, sent, stats, base


def chip(place, kept, got, stats):
    sub, rows, count = 128, stats.shape[1], 4
    blocks = [array((sub + PACKED, rows), jnp.bfloat16)] * (count - 1)
    return call(
        chip_kernel,
        [array((sub, rows)), array((8, rows))] + blocks,
        [SMEM] + [VMEM] * 3,
        place,
        kept,
        got,
        stats,
    )


def quantize(mean, stats, gots, base, book, parts):
    (sub, rows), words = mean.shape, book.shape[0]
    quarter = words // parts
    return call(
        quantize_kernel,
        (
            array((sub, rows), jnp.bfloat16),
            array((parts, quarter + quarter // 64, sub), jnp.bfloat16),
            array((words, rows), jnp.bfloat16),
            array((8, rows)),
        ),
        [VMEM] * (len(gots) + 4),
        mean,
        stats,
        *gots,
        base,
        book,
        outs=(VMEM, VMEM, HBM, VMEM),
        scratch=[
            pltpu.VMEM((words, rows), jnp.float32),
            pltpu.VMEM((words, rows), jnp.bfloat16),
            pltpu.SemaphoreType.DMA((parts,)),
        ],
        mib=51,
    )


def local(embeddings, centroids, codebook):
    _, book_rows, sub_width = codebook.shape
    y_count, z_count, x_count = lax.axis_size("y"), lax.axis_size("z"), lax.axis_size("x")
    words = book_rows * y_count * z_count
    place = jnp.stack([lax.axis_index("c"), lax.axis_index("x")]).astype(jnp.int32)

    own = codebook.reshape(book_rows, sub_width)
    book = exchange(jnp.broadcast_to(own, (z_count, book_rows, sub_width)), "z")
    book = book.reshape(words // y_count, sub_width)

    kept, sent, stats, base = coarse(embeddings, centroids, place)
    got = lax.ppermute(sent, "c", [(0, 1), (1, 0)])
    mean, stats, *blocks = chip(place, kept, got, stats)
    book, *blocks = lax.optimization_barrier((book, *blocks))
    gots = [
        lax.ppermute(block, "x", [(i, (i + step) % x_count) for i in range(x_count)])
        for step, block in enumerate(blocks, 1)
    ]
    book = exchange(jnp.broadcast_to(book, (y_count,) + book.shape), "y").reshape(words, sub_width)
    residual, sums, raised, inverse = quantize(mean, stats, gots, base, book, y_count)

    sums = exchange(sums, "y")
    rebuilt = lax.dot_general(
        book, raised, (((0,), (0,)), ((), ())), preferred_element_type=jnp.float32
    ) * inverse[:1]
    pq_error = jnp.mean(jnp.square(residual.astype(jnp.float32) - rebuilt), axis=0)
    sums, pq_error = lax.optimization_barrier((sums, pq_error[None]))
    sums = call(
        middle_kernel, array((z_count, book_rows + 8, sub_width), jnp.bfloat16), [VMEM], sums
    )
    sums = exchange(sums, "z")
    new_codebook = call(last_kernel, array((book_rows, sub_width)), [VMEM] * 2, sums, own)
    return (residual, new_codebook[None], pq_error)


def solution(mesh):
    sizes = (4, 16, 4, 2)
    wide = Mesh(mesh.devices.reshape(sizes), ("y", "z", "x", "c"))
    rows = ("y", "z")
    placed = (P(rows, None), P(CENT, None), P(CENT, rows, None))
    return jax.shard_map(
        local,
        mesh=wide,
        in_specs=placed,
        out_specs=(P(CENT, rows), P(CENT, rows, None), P(CENT, rows)),
        check_vma=False,
    )
```

```python
import functools
import math

import jax
import jax.numpy as jnp
from jax import lax
from jax.experimental import pallas as pl
from jax.experimental.pallas import tpu as pltpu
from jax.sharding import Mesh, PartitionSpec as P

smoothing = 1.0
CENT = ("x", "c")


PACKED = 16
BOOK_FIRST = 10
SUMS_FIRST = 2


def exchange(parts, axis, first=0):
    count = lax.axis_size(axis)
    order = [[(first + i) % count for i in range(count)]]
    return lax.all_to_all(parts, axis, 0, 0, axis_index_groups=order, tiled=True)


def wide_row(columns):
    return jnp.transpose(jnp.broadcast_to(columns, (columns.shape[0], 128)))[:1]


def coarse_kernel(place_ref, e_ref, c_ref, sent_ref, stats_ref, weights_ref, inverse_ref, logits_ref):
    rows, width = e_ref.shape
    chunks, _, chunk = logits_ref.shape
    used = sent_ref.shape[0] - PACKED
    scale = 2.0 / math.sqrt(width)

    def score(j, peak):
        block = c_ref[pl.ds(pl.multiple_of(j * chunk, chunk), chunk), :]
        wide = block.astype(jnp.float32)
        half_norm = wide_row(0.5 * jnp.sum(wide * wide, axis=1, keepdims=True))
        products = lax.dot_general(
            e_ref[...], block, (((1,), (1,)), ((), ())), preferred_element_type=jnp.float32
        )
        logits = (products - half_norm) * scale
        logits_ref[j] = logits
        for part in range(chunk // 128):
            peak = jnp.maximum(peak, logits[:, part * 128 : part * 128 + 128])
        return peak

    peak = lax.fori_loop(0, chunks, score, jnp.full((rows, 128), -jnp.inf, jnp.float32), unroll=2)
    peak = jnp.max(peak, axis=1, keepdims=True)

    def raise_(j, total):
        shifted = jnp.exp(logits_ref[j] - peak)
        weights_ref[:, pl.ds(pl.multiple_of(j * chunk, chunk), chunk)] = shifted.astype(jnp.bfloat16)
        for part in range(chunk // 128):
            total = total + shifted[:, part * 128 : part * 128 + 128]
        return total

    total = lax.fori_loop(0, chunks, raise_, jnp.zeros((rows, 128), jnp.float32), unroll=2)
    total = jnp.sum(total, axis=1, keepdims=True)
    inverse_ref[...] = jnp.broadcast_to(1.0 / total, inverse_ref.shape)
    pull(1 - place_ref[0], weights_ref, inverse_ref, c_ref, sent_ref)
    largest, total = wide_row(peak), wide_row(total)
    stats_ref[...] = jnp.concatenate([largest, total, jnp.zeros((6, rows), jnp.float32)], axis=0)
    sent_ref[used:, :] = packed(largest, total)


def pull(core, weights_ref, inverse_ref, c_ref, out_ref):
    sub = inverse_ref.shape[1]
    for pair in range(2):
        columns = [pl.ds(pl.multiple_of(((2 * pair + k) * 2 + core) * sub, sub), sub) for k in range(2)]
        block = jnp.concatenate([c_ref[:, column] for column in columns], axis=1)
        pulled = jnp.dot(weights_ref[...], block, preferred_element_type=jnp.float32)
        for k in range(2):
            part = pulled[:, k * sub : k * sub + sub] * inverse_ref[...]
            row = (2 * pair + k) * sub
            out_ref[row : row + sub, :] = jnp.transpose(part).astype(out_ref.dtype)


def kept_kernel(place_ref, weights_ref, inverse_ref, c_ref, e_ref, kept_ref, base_ref):
    pull(place_ref[0], weights_ref, inverse_ref, c_ref, kept_ref)
    sub = base_ref.shape[0]
    own = pl.multiple_of((2 * place_ref[1] + place_ref[0]) * sub, sub)
    base_ref[...] = jnp.transpose(e_ref[:, pl.ds(own, sub)].astype(jnp.float32))


def weigh(maxes, totals):
    largest = functools.reduce(jnp.maximum, maxes)
    shares = [jnp.exp(own - largest) * total for own, total in zip(maxes, totals)]
    whole = functools.reduce(jnp.add, shares)
    return [share / whole for share in shares], largest, whole


def terms_of(value, count=3):
    terms = []
    for _ in range(count):
        term = value.astype(jnp.bfloat16).astype(jnp.float32)
        terms.append(term)
        value = value - term
    return terms


def packed(largest, total):
    terms = terms_of(largest) + terms_of(total)
    terms.append(jnp.zeros((PACKED - len(terms), largest.shape[1]), jnp.float32))
    return jnp.concatenate(terms, axis=0).astype(jnp.bfloat16)


def unpacked(rows):
    wide = rows.astype(jnp.float32)
    return (wide[2:3] + wide[1:2]) + wide[0:1], (wide[5:6] + wide[4:5]) + wide[3:4]


def chip_kernel(place_ref, kept_ref, got_ref, stats_ref, mean_ref, chip_ref, *block_refs):
    sub, rows = mean_ref.shape
    count = len(block_refs) + 1
    used = count * sub
    other_max, other_total = unpacked(got_ref[used:, :])
    (own, other), largest, total = weigh(
        [stats_ref[0:1], other_max], [stats_ref[1:2], other_total]
    )
    chip_ref[...] = jnp.concatenate([largest, total, jnp.zeros((6, rows), jnp.float32)], axis=0)
    stats = packed(largest, total)
    for step in range(count):
        at = pl.ds(pl.multiple_of(lax.rem(place_ref[1] + step, count) * sub, sub), sub)
        mean = kept_ref[at, :] * own + got_ref[at, :].astype(jnp.float32) * other
        if step == 0:
            mean_ref[...] = mean
        else:
            block_refs[step - 1][:sub, :] = mean.astype(jnp.bfloat16)
            block_refs[step - 1][sub:, :] = stats


def quantize_kernel(mean_ref, chip_ref, *refs):
    *got_refs, base_ref, book_ref, residual_ref, sums_ref, raised_hbm, inverse_ref, gaps_ref, raised_ref, sems = refs
    sub, rows = mean_ref.shape
    parts, held, _ = sums_ref.shape
    words = book_ref.shape[0]
    quarter = words // parts
    scale = 2.0 / math.sqrt(sub)
    stats = [(chip_ref[0:1], chip_ref[1:2])] + [unpacked(got[sub:, :]) for got in got_refs]
    shares, _, _ = weigh(*zip(*stats))
    mean = mean_ref[...] * shares[0]
    for got, share in zip(got_refs, shares[1:]):
        mean = mean + got[:sub, :].astype(jnp.float32) * share
    residual = (base_ref[...] - mean).astype(jnp.bfloat16)
    residual_ref[...] = residual

    spans = [slice(at, at + 256) for at in range(0, words, 256)]
    peak = jnp.full((8, rows), -jnp.inf, jnp.float32)
    for at in spans:
        block = book_ref[at, :]
        wide = block.astype(jnp.float32)
        half = 0.5 * jnp.sum(wide * wide, axis=1, keepdims=True)
        gap = jnp.dot(block, residual, preferred_element_type=jnp.float32) - half
        gaps_ref[at, :] = gap
        peak = jnp.maximum(peak, jnp.max(gap.reshape(32, 8, rows), axis=0))
    peak = jnp.max(peak, axis=0, keepdims=True)
    total = jnp.zeros((8, rows), jnp.float32)
    stores = []
    for j, at in enumerate(spans):
        raised = jnp.exp((gaps_ref[at, :] - peak) * scale)
        raised_ref[at, :] = raised.astype(jnp.bfloat16)
        total = total + jnp.sum(raised.reshape(32, 8, rows), axis=0)
        if j % 4 == 3:
            at = slice((j - 3) * 256, (j + 1) * 256)
            stores.append(pltpu.make_async_copy(raised_ref.at[at, :], raised_hbm.at[at, :], sems.at[j // 4]))
            stores[-1].start()
    inverse = 1.0 / jnp.sum(total, axis=0, keepdims=True)
    inverse_ref[...] = jnp.broadcast_to(inverse, inverse_ref.shape)

    scaled = residual.astype(jnp.float32) * inverse
    high, low = (jnp.broadcast_to(term, (sub // 2, rows)) for term in terms_of(inverse, 2))
    sides = jnp.transpose(jnp.concatenate([scaled, high, low], axis=0)).astype(jnp.bfloat16)
    row = lax.broadcasted_iota(jnp.int32, (128, 128), 0)
    diagonal = row == lax.broadcasted_iota(jnp.int32, (128, 128), 1)
    for part in range(parts):
        lines = []
        for at in range(0, quarter, 256):
            span = slice(part * quarter + at, part * quarter + at + 256)
            sums = jnp.dot(raised_ref[span, :], sides, preferred_element_type=jnp.float32)
            sums_ref[part, at : at + 256, :] = sums[:, :sub].astype(jnp.bfloat16)
            counts = sums[:, sub:]
            counts = counts + pltpu.roll(counts, sub // 2, 1)
            for k in range(2):
                tile = counts[k * 128 : k * 128 + 128]
                lines.append(jnp.sum(jnp.where(diagonal, tile, 0.0), axis=0, keepdims=True))
        counts = jnp.concatenate(lines, axis=0)
        sums_ref[part, quarter:, :] = jnp.concatenate(terms_of(counts, 2), axis=0).astype(jnp.bfloat16)
    for store in stores:
        store.wait()


def middle_kernel(sums_ref, out_ref):
    parts, held, sub = sums_ref.shape
    targets, rows, _ = out_ref.shape
    words = rows - 8
    quarter = targets * words
    counts = jnp.zeros((quarter // 128, 128), jnp.float32)
    for part in range(parts):
        pair = sums_ref[part, quarter:, :].astype(jnp.float32)
        counts = counts + (pair[: quarter // 128] + pair[quarter // 128 :])
    high, low = terms_of(counts, 2)
    left = lax.broadcasted_iota(jnp.int32, high.shape, 1) < 64
    even = jnp.where(left, high, pltpu.roll(low, 64, 1))
    odd = jnp.where(left, pltpu.roll(high, 64, 1), low)
    for target in range(targets):
        at = slice(target * words, target * words + words)
        total = sums_ref[0, at, :].astype(jnp.float32)
        for part in range(1, parts):
            total = total + sums_ref[part, at, :].astype(jnp.float32)
        row = (even if target % 2 == 0 else odd)[target // 2 : target // 2 + 1]
        row = jnp.concatenate([row, jnp.zeros((7, sub), jnp.float32)], axis=0)
        place = (target + BOOK_FIRST - SUMS_FIRST) % targets
        out_ref[place] = jnp.concatenate([total, row], axis=0).astype(jnp.bfloat16)


def last_kernel(sums_ref, own_ref, out_ref):
    parts = sums_ref.shape[0]
    words, sub = own_ref.shape
    total = sums_ref[0].astype(jnp.float32)
    for part in range(1, parts):
        total = total + sums_ref[part].astype(jnp.float32)
    pair = total[words : words + 1]
    counts = jnp.broadcast_to(pair + pltpu.roll(pair, 64, 1), (words, sub))
    diagonal = lax.broadcasted_iota(jnp.int32, (words, sub), 0) == lax.broadcasted_iota(jnp.int32, (words, sub), 1)
    counts = jnp.sum(jnp.where(diagonal, counts, 0.0), axis=1, keepdims=True)
    own = own_ref[...].astype(jnp.float32)
    out_ref[...] = (total[:words] + smoothing * own) / (counts + smoothing)


VMEM = pl.BlockSpec(memory_space=pltpu.VMEM)
SMEM = pl.BlockSpec(memory_space=pltpu.SMEM)
HBM = pl.BlockSpec(memory_space=pltpu.HBM)


def call(kernel, out_shape, ins, *args, outs=None, scratch=(), mib=8):
    return pl.pallas_call(
        kernel,
        out_shape=out_shape,
        in_specs=ins,
        out_specs=outs or jax.tree.map(lambda _: VMEM, out_shape),
        scratch_shapes=scratch,
        compiler_params=pltpu.CompilerParams(vmem_limit_bytes=mib * 2**20),
        cost_estimate=pl.CostEstimate(flops=1, bytes_accessed=1, transcendentals=0),
    )(*args)


def array(shape, dtype=jnp.float32):
    return jax.ShapeDtypeStruct(shape, dtype)


def coarse(embeddings, centroids, place):
    rows, width = embeddings.shape
    count = centroids.shape[0]
    half, sub, chunk = width // 2, 128, 256
    sent, stats, weights, inverse = call(
        coarse_kernel,
        (
            array((half + PACKED, rows), jnp.bfloat16),
            array((8, rows)),
            array((rows, count), jnp.bfloat16),
            array((rows, sub)),
        ),
        [SMEM, VMEM, VMEM],
        place,
        embeddings,
        centroids,
        scratch=[pltpu.VMEM((count // chunk, rows, chunk), jnp.float32)],
        mib=24,
    )
    kept, base = call(
        kept_kernel,
        (array((half, rows)), array((sub, rows))),
        [SMEM] + [VMEM] * 4,
        place,
        weights,
        inverse,
        centroids,
        embeddings,
        mib=24,
    )
    return kept, sent, stats, base


def chip(place, kept, got, stats):
    sub, rows, count = 128, stats.shape[1], 4
    blocks = [array((sub + PACKED, rows), jnp.bfloat16)] * (count - 1)
    return call(
        chip_kernel,
        [array((sub, rows)), array((8, rows))] + blocks,
        [SMEM] + [VMEM] * 3,
        place,
        kept,
        got,
        stats,
    )


def quantize(mean, stats, gots, base, book, parts):
    (sub, rows), words = mean.shape, book.shape[0]
    quarter = words // parts
    return call(
        quantize_kernel,
        (
            array((sub, rows), jnp.bfloat16),
            array((parts, quarter + quarter // 64, sub), jnp.bfloat16),
            array((words, rows), jnp.bfloat16),
            array((8, rows)),
        ),
        [VMEM] * (len(gots) + 4),
        mean,
        stats,
        *gots,
        base,
        book,
        outs=(VMEM, VMEM, HBM, VMEM),
        scratch=[
            pltpu.VMEM((words, rows), jnp.float32),
            pltpu.VMEM((words, rows), jnp.bfloat16),
            pltpu.SemaphoreType.DMA((parts,)),
        ],
        mib=51,
    )


def local(embeddings, centroids, codebook):
    _, book_rows, sub_width = codebook.shape
    y_count, z_count, x_count = lax.axis_size("y"), lax.axis_size("z"), lax.axis_size("x")
    words = book_rows * y_count * z_count
    place = jnp.stack([lax.axis_index("c"), lax.axis_index("x")]).astype(jnp.int32)

    own = codebook.reshape(book_rows, sub_width)
    book = exchange(jnp.broadcast_to(own, (z_count, book_rows, sub_width)), "z", BOOK_FIRST)
    book = book.reshape(words // y_count, sub_width)

    kept, sent, stats, base = coarse(embeddings, centroids, place)
    got = lax.ppermute(sent, "c", [(0, 1), (1, 0)])
    mean, stats, *blocks = chip(place, kept, got, stats)
    book, *blocks = lax.optimization_barrier((book, *blocks))
    gots = [
        lax.ppermute(block, "x", [(i, (i + step) % x_count) for i in range(x_count)])
        for step, block in enumerate(blocks, 1)
    ]
    book = exchange(jnp.broadcast_to(book, (y_count,) + book.shape), "y").reshape(words, sub_width)
    residual, sums, raised, inverse = quantize(mean, stats, gots, base, book, y_count)

    sums = exchange(sums, "y")
    rebuilt = lax.dot_general(
        book, raised, (((0,), (0,)), ((), ())), preferred_element_type=jnp.float32
    ) * inverse[:1]
    pq_error = jnp.mean(jnp.square(residual.astype(jnp.float32) - rebuilt), axis=0)
    sums, pq_error = lax.optimization_barrier((sums, pq_error[None]))
    sums = call(
        middle_kernel, array((z_count, book_rows + 8, sub_width), jnp.bfloat16), [VMEM], sums
    )
    sums = exchange(sums, "z", SUMS_FIRST)
    new_codebook = call(last_kernel, array((book_rows, sub_width)), [VMEM] * 2, sums, own)
    return (residual, new_codebook[None], pq_error)


def solution(mesh):
    sizes = (4, 16, 4, 2)
    wide = Mesh(mesh.devices.reshape(sizes), ("y", "z", "x", "c"))
    rows = ("y", "z")
    placed = (P(rows, None), P(CENT, None), P(CENT, rows, None))
    return jax.shard_map(
        local,
        mesh=wide,
        in_specs=placed,
        out_specs=(P(CENT, rows), P(CENT, rows, None), P(CENT, rows)),
        check_vma=False,
    )
```

```python
import functools
import math

import jax
import jax.numpy as jnp
from jax import lax
from jax.experimental import pallas as pl
from jax.experimental.pallas import tpu as pltpu
from jax.sharding import Mesh, PartitionSpec as P

smoothing = 1.0
CENT = ("x", "c")


PACKED = 16
BOOK_FIRST = 10
SUMS_FIRST = 2


def exchange(parts, axis, first=0):
    count = lax.axis_size(axis)
    order = [[(first + i) % count for i in range(count)]]
    return lax.all_to_all(parts, axis, 0, 0, axis_index_groups=order, tiled=True)


def wide_row(columns):
    return jnp.transpose(jnp.broadcast_to(columns, (columns.shape[0], 128)))[:1]


def coarse_kernel(place_ref, e_ref, c_ref, sent_ref, stats_ref, weights_ref, inverse_ref, logits_ref):
    rows, width = e_ref.shape
    chunks, _, chunk = logits_ref.shape
    used = sent_ref.shape[0] - PACKED
    scale = 2.0 / math.sqrt(width)

    def score(j, peak):
        block = c_ref[slice(j * chunk, j * chunk + chunk), :]
        wide = block.astype(jnp.float32)
        half_norm = wide_row(0.5 * jnp.sum(wide * wide, axis=1, keepdims=True))
        products = lax.dot_general(
            e_ref[...], block, (((1,), (1,)), ((), ())), preferred_element_type=jnp.float32
        )
        logits = (products - half_norm) * scale
        logits_ref[j] = logits
        for part in range(chunk // 128):
            peak = jnp.maximum(peak, logits[:, part * 128 : part * 128 + 128])
        return peak

    peak = jnp.full((rows, 128), -jnp.inf, jnp.float32)
    for j in range(chunks):
        peak = score(j, peak)
    peak = jnp.max(peak, axis=1, keepdims=True)

    def raise_(j, total):
        shifted = jnp.exp(logits_ref[j] - peak)
        weights_ref[:, slice(j * chunk, j * chunk + chunk)] = shifted.astype(jnp.bfloat16)
        for part in range(chunk // 128):
            total = total + shifted[:, part * 128 : part * 128 + 128]
        return total

    total = jnp.zeros((rows, 128), jnp.float32)
    for j in range(chunks):
        total = raise_(j, total)
    total = jnp.sum(total, axis=1, keepdims=True)
    inverse_ref[...] = jnp.broadcast_to(1.0 / total, inverse_ref.shape)
    pull(1 - place_ref[0], weights_ref, inverse_ref, c_ref, sent_ref)
    largest, total = wide_row(peak), wide_row(total)
    stats_ref[...] = jnp.concatenate([largest, total, jnp.zeros((6, rows), jnp.float32)], axis=0)
    sent_ref[used:, :] = packed(largest, total)


def pull(core, weights_ref, inverse_ref, c_ref, out_ref):
    sub = inverse_ref.shape[1]
    for pair in range(2):
        columns = [pl.ds(pl.multiple_of(((2 * pair + k) * 2 + core) * sub, sub), sub) for k in range(2)]
        block = jnp.concatenate([c_ref[:, column] for column in columns], axis=1)
        pulled = jnp.dot(weights_ref[...], block, preferred_element_type=jnp.float32)
        for k in range(2):
            part = pulled[:, k * sub : k * sub + sub] * inverse_ref[...]
            row = (2 * pair + k) * sub
            out_ref[row : row + sub, :] = jnp.transpose(part).astype(out_ref.dtype)


def kept_kernel(place_ref, weights_ref, inverse_ref, c_ref, e_ref, kept_ref, base_ref):
    pull(place_ref[0], weights_ref, inverse_ref, c_ref, kept_ref)
    sub = base_ref.shape[0]
    own = pl.multiple_of((2 * place_ref[1] + place_ref[0]) * sub, sub)
    base_ref[...] = jnp.transpose(e_ref[:, pl.ds(own, sub)].astype(jnp.float32))


def weigh(maxes, totals):
    largest = functools.reduce(jnp.maximum, maxes)
    shares = [jnp.exp(own - largest) * total for own, total in zip(maxes, totals)]
    whole = functools.reduce(jnp.add, shares)
    return [share / whole for share in shares], largest, whole


def terms_of(value, count=3):
    terms = []
    for _ in range(count):
        term = value.astype(jnp.bfloat16).astype(jnp.float32)
        terms.append(term)
        value = value - term
    return terms


def packed(largest, total):
    terms = terms_of(largest) + terms_of(total)
    terms.append(jnp.zeros((PACKED - len(terms), largest.shape[1]), jnp.float32))
    return jnp.concatenate(terms, axis=0).astype(jnp.bfloat16)


def unpacked(rows):
    wide = rows.astype(jnp.float32)
    return (wide[2:3] + wide[1:2]) + wide[0:1], (wide[5:6] + wide[4:5]) + wide[3:4]


def chip_kernel(place_ref, kept_ref, got_ref, stats_ref, mean_ref, chip_ref, *block_refs):
    sub, rows = mean_ref.shape
    count = len(block_refs) + 1
    used = count * sub
    other_max, other_total = unpacked(got_ref[used:, :])
    (own, other), largest, total = weigh(
        [stats_ref[0:1], other_max], [stats_ref[1:2], other_total]
    )
    chip_ref[...] = jnp.concatenate([largest, total, jnp.zeros((6, rows), jnp.float32)], axis=0)
    stats = packed(largest, total)
    for step in range(count):
        at = pl.ds(pl.multiple_of(lax.rem(place_ref[1] + step, count) * sub, sub), sub)
        mean = kept_ref[at, :] * own + got_ref[at, :].astype(jnp.float32) * other
        if step == 0:
            mean_ref[...] = mean
        else:
            block_refs[step - 1][:sub, :] = mean.astype(jnp.bfloat16)
            block_refs[step - 1][sub:, :] = stats


def quantize_kernel(mean_ref, chip_ref, *refs):
    *got_refs, base_ref, book_ref, residual_ref, sums_ref, raised_hbm, inverse_ref, gaps_ref, raised_ref, sems = refs
    sub, rows = mean_ref.shape
    parts, held, _ = sums_ref.shape
    words = book_ref.shape[0]
    quarter = words // parts
    scale = 2.0 / math.sqrt(sub)
    stats = [(chip_ref[0:1], chip_ref[1:2])] + [unpacked(got[sub:, :]) for got in got_refs]
    shares, _, _ = weigh(*zip(*stats))
    mean = mean_ref[...] * shares[0]
    for got, share in zip(got_refs, shares[1:]):
        mean = mean + got[:sub, :].astype(jnp.float32) * share
    residual = (base_ref[...] - mean).astype(jnp.bfloat16)
    residual_ref[...] = residual

    spans = [slice(at, at + 256) for at in range(0, words, 256)]
    peak = jnp.full((8, rows), -jnp.inf, jnp.float32)
    for at in spans:
        block = book_ref[at, :]
        wide = block.astype(jnp.float32)
        half = 0.5 * jnp.sum(wide * wide, axis=1, keepdims=True)
        gap = jnp.dot(block, residual, preferred_element_type=jnp.float32) - half
        gaps_ref[at, :] = gap
        peak = jnp.maximum(peak, jnp.max(gap.reshape(32, 8, rows), axis=0))
    peak = jnp.max(peak, axis=0, keepdims=True)
    total = jnp.zeros((8, rows), jnp.float32)
    stores = []
    for j, at in enumerate(spans):
        raised = jnp.exp((gaps_ref[at, :] - peak) * scale)
        raised_ref[at, :] = raised.astype(jnp.bfloat16)
        total = total + jnp.sum(raised.reshape(32, 8, rows), axis=0)
        if j % 4 == 3:
            at = slice((j - 3) * 256, (j + 1) * 256)
            stores.append(pltpu.make_async_copy(raised_ref.at[at, :], raised_hbm.at[at, :], sems.at[j // 4]))
            stores[-1].start()
    inverse = 1.0 / jnp.sum(total, axis=0, keepdims=True)
    inverse_ref[...] = jnp.broadcast_to(inverse, inverse_ref.shape)

    scaled = residual.astype(jnp.float32) * inverse
    high, low = (jnp.broadcast_to(term, (sub // 2, rows)) for term in terms_of(inverse, 2))
    sides = jnp.transpose(jnp.concatenate([scaled, high, low], axis=0)).astype(jnp.bfloat16)
    row = lax.broadcasted_iota(jnp.int32, (128, 128), 0)
    diagonal = row == lax.broadcasted_iota(jnp.int32, (128, 128), 1)
    for part in range(parts):
        lines = []
        for at in range(0, quarter, 256):
            span = slice(part * quarter + at, part * quarter + at + 256)
            sums = jnp.dot(raised_ref[span, :], sides, preferred_element_type=jnp.float32)
            sums_ref[part, at : at + 256, :] = sums[:, :sub].astype(jnp.bfloat16)
            counts = sums[:, sub:]
            counts = counts + pltpu.roll(counts, sub // 2, 1)
            for k in range(2):
                tile = counts[k * 128 : k * 128 + 128]
                lines.append(jnp.sum(jnp.where(diagonal, tile, 0.0), axis=0, keepdims=True))
        counts = jnp.concatenate(lines, axis=0)
        sums_ref[part, quarter:, :] = jnp.concatenate(terms_of(counts, 2), axis=0).astype(jnp.bfloat16)
    for store in stores:
        store.wait()


def middle_kernel(sums_ref, out_ref):
    parts, held, sub = sums_ref.shape
    targets, rows, _ = out_ref.shape
    words = rows - 8
    quarter = targets * words
    counts = jnp.zeros((quarter // 128, 128), jnp.float32)
    for part in range(parts):
        pair = sums_ref[part, quarter:, :].astype(jnp.float32)
        counts = counts + (pair[: quarter // 128] + pair[quarter // 128 :])
    high, low = terms_of(counts, 2)
    left = lax.broadcasted_iota(jnp.int32, high.shape, 1) < 64
    even = jnp.where(left, high, pltpu.roll(low, 64, 1))
    odd = jnp.where(left, pltpu.roll(high, 64, 1), low)
    for target in range(targets):
        at = slice(target * words, target * words + words)
        total = sums_ref[0, at, :].astype(jnp.float32)
        for part in range(1, parts):
            total = total + sums_ref[part, at, :].astype(jnp.float32)
        row = (even if target % 2 == 0 else odd)[target // 2 : target // 2 + 1]
        row = jnp.concatenate([row, jnp.zeros((7, sub), jnp.float32)], axis=0)
        place = (target + BOOK_FIRST - SUMS_FIRST) % targets
        out_ref[place] = jnp.concatenate([total, row], axis=0).astype(jnp.bfloat16)


def last_kernel(sums_ref, own_ref, out_ref):
    parts = sums_ref.shape[0]
    words, sub = own_ref.shape
    total = sums_ref[0].astype(jnp.float32)
    for part in range(1, parts):
        total = total + sums_ref[part].astype(jnp.float32)
    pair = total[words : words + 1]
    counts = jnp.broadcast_to(pair + pltpu.roll(pair, 64, 1), (words, sub))
    diagonal = lax.broadcasted_iota(jnp.int32, (words, sub), 0) == lax.broadcasted_iota(jnp.int32, (words, sub), 1)
    counts = jnp.sum(jnp.where(diagonal, counts, 0.0), axis=1, keepdims=True)
    own = own_ref[...].astype(jnp.float32)
    out_ref[...] = (total[:words] + smoothing * own) / (counts + smoothing)


VMEM = pl.BlockSpec(memory_space=pltpu.VMEM)
SMEM = pl.BlockSpec(memory_space=pltpu.SMEM)
HBM = pl.BlockSpec(memory_space=pltpu.HBM)


def call(kernel, out_shape, ins, *args, outs=None, scratch=(), mib=8):
    return pl.pallas_call(
        kernel,
        out_shape=out_shape,
        in_specs=ins,
        out_specs=outs or jax.tree.map(lambda _: VMEM, out_shape),
        scratch_shapes=scratch,
        compiler_params=pltpu.CompilerParams(vmem_limit_bytes=mib * 2**20),
        cost_estimate=pl.CostEstimate(flops=1, bytes_accessed=1, transcendentals=0),
    )(*args)


def array(shape, dtype=jnp.float32):
    return jax.ShapeDtypeStruct(shape, dtype)


def coarse(embeddings, centroids, place):
    rows, width = embeddings.shape
    count = centroids.shape[0]
    half, sub, chunk = width // 2, 128, 256
    sent, stats, weights, inverse = call(
        coarse_kernel,
        (
            array((half + PACKED, rows), jnp.bfloat16),
            array((8, rows)),
            array((rows, count), jnp.bfloat16),
            array((rows, sub)),
        ),
        [SMEM, VMEM, VMEM],
        place,
        embeddings,
        centroids,
        scratch=[pltpu.VMEM((count // chunk, rows, chunk), jnp.float32)],
        mib=24,
    )
    kept, base = call(
        kept_kernel,
        (array((half, rows)), array((sub, rows))),
        [SMEM] + [VMEM] * 4,
        place,
        weights,
        inverse,
        centroids,
        embeddings,
        mib=24,
    )
    return kept, sent, stats, base


def chip(place, kept, got, stats):
    sub, rows, count = 128, stats.shape[1], 4
    blocks = [array((sub + PACKED, rows), jnp.bfloat16)] * (count - 1)
    return call(
        chip_kernel,
        [array((sub, rows)), array((8, rows))] + blocks,
        [SMEM] + [VMEM] * 3,
        place,
        kept,
        got,
        stats,
    )


def quantize(mean, stats, gots, base, book, parts):
    (sub, rows), words = mean.shape, book.shape[0]
    quarter = words // parts
    return call(
        quantize_kernel,
        (
            array((sub, rows), jnp.bfloat16),
            array((parts, quarter + quarter // 64, sub), jnp.bfloat16),
            array((words, rows), jnp.bfloat16),
            array((8, rows)),
        ),
        [VMEM] * (len(gots) + 4),
        mean,
        stats,
        *gots,
        base,
        book,
        outs=(VMEM, VMEM, HBM, VMEM),
        scratch=[
            pltpu.VMEM((words, rows), jnp.float32),
            pltpu.VMEM((words, rows), jnp.bfloat16),
            pltpu.SemaphoreType.DMA((parts,)),
        ],
        mib=51,
    )


def local(embeddings, centroids, codebook):
    _, book_rows, sub_width = codebook.shape
    y_count, z_count, x_count = lax.axis_size("y"), lax.axis_size("z"), lax.axis_size("x")
    words = book_rows * y_count * z_count
    place = jnp.stack([lax.axis_index("c"), lax.axis_index("x")]).astype(jnp.int32)

    own = codebook.reshape(book_rows, sub_width)
    book = exchange(jnp.broadcast_to(own, (z_count, book_rows, sub_width)), "z", BOOK_FIRST)
    book = book.reshape(words // y_count, sub_width)

    kept, sent, stats, base = coarse(embeddings, centroids, place)
    got = lax.ppermute(sent, "c", [(0, 1), (1, 0)])
    mean, stats, *blocks = chip(place, kept, got, stats)
    book, *blocks = lax.optimization_barrier((book, *blocks))
    gots = {}
    for step in (2, 1, 3):
        ring = [(i, (i + step) % x_count) for i in range(x_count)]
        gots[step] = lax.ppermute(blocks[step - 1], "x", ring)
    gots = [gots[step] for step in (1, 2, 3)]
    book = exchange(jnp.broadcast_to(book, (y_count,) + book.shape), "y").reshape(words, sub_width)
    residual, sums, raised, inverse = quantize(mean, stats, gots, base, book, y_count)

    sums = exchange(sums, "y")
    rebuilt = lax.dot_general(
        book, raised, (((0,), (0,)), ((), ())), preferred_element_type=jnp.float32
    ) * inverse[:1]
    pq_error = jnp.mean(jnp.square(residual.astype(jnp.float32) - rebuilt), axis=0)
    sums, pq_error = lax.optimization_barrier((sums, pq_error[None]))
    sums = call(
        middle_kernel, array((z_count, book_rows + 8, sub_width), jnp.bfloat16), [VMEM], sums
    )
    sums = exchange(sums, "z", SUMS_FIRST)
    new_codebook = call(last_kernel, array((book_rows, sub_width)), [VMEM] * 2, sums, own)
    return (residual, new_codebook[None], pq_error)


def solution(mesh):
    sizes = (4, 16, 4, 2)
    wide = Mesh(mesh.devices.reshape(sizes), ("y", "z", "x", "c"))
    rows = ("y", "z")
    placed = (P(rows, None), P(CENT, None), P(CENT, rows, None))
    return jax.shard_map(
        local,
        mesh=wide,
        in_specs=placed,
        out_specs=(P(CENT, rows), P(CENT, rows, None), P(CENT, rows)),
        check_vma=False,
    )
```

```python
import functools
import math

import jax
import jax.numpy as jnp
from jax import lax
from jax.experimental import pallas as pl
from jax.experimental.pallas import tpu as pltpu
from jax.sharding import Mesh, PartitionSpec as P

smoothing = 1.0
CENT = ("x", "c")


PACKED = 16
BOOK_FIRST = 10
SUMS_FIRST = 8


def exchange(parts, axis, first=0):
    count = lax.axis_size(axis)
    order = [[(first + i) % count for i in range(count)]]
    return lax.all_to_all(parts, axis, 0, 0, axis_index_groups=order, tiled=True)


def wide_row(columns):
    return jnp.transpose(jnp.broadcast_to(columns, (columns.shape[0], 128)))[:1]


def coarse_kernel(place_ref, e_ref, c_ref, sent_ref, stats_ref, weights_ref, inverse_ref, logits_ref):
    rows, width = e_ref.shape
    chunks, _, chunk = logits_ref.shape
    used = sent_ref.shape[0] - PACKED
    scale = 2.0 / math.sqrt(width)

    def score(j, peak):
        block = c_ref[slice(j * chunk, j * chunk + chunk), :]
        wide = block.astype(jnp.float32)
        half_norm = wide_row(0.5 * jnp.sum(wide * wide, axis=1, keepdims=True))
        products = lax.dot_general(
            e_ref[...], block, (((1,), (1,)), ((), ())), preferred_element_type=jnp.float32
        )
        logits = (products - half_norm) * scale
        logits_ref[j] = logits
        for part in range(chunk // 128):
            peak = jnp.maximum(peak, logits[:, part * 128 : part * 128 + 128])
        return peak

    peak = jnp.full((rows, 128), -jnp.inf, jnp.float32)
    for j in range(chunks):
        peak = score(j, peak)
    peak = jnp.max(peak, axis=1, keepdims=True)

    def raise_(j, total):
        shifted = jnp.exp(logits_ref[j] - peak)
        weights_ref[:, slice(j * chunk, j * chunk + chunk)] = shifted.astype(jnp.bfloat16)
        for part in range(chunk // 128):
            total = total + shifted[:, part * 128 : part * 128 + 128]
        return total

    total = jnp.zeros((rows, 128), jnp.float32)
    for j in range(chunks):
        total = raise_(j, total)
    total = jnp.sum(total, axis=1, keepdims=True)
    inverse_ref[...] = jnp.broadcast_to(1.0 / total, inverse_ref.shape)
    pull(1 - place_ref[0], weights_ref, inverse_ref, c_ref, sent_ref)
    largest, total = wide_row(peak), wide_row(total)
    stats_ref[...] = jnp.concatenate([largest, total, jnp.zeros((6, rows), jnp.float32)], axis=0)
    sent_ref[used:, :] = packed(largest, total)


def pull(core, weights_ref, inverse_ref, c_ref, out_ref):
    sub = inverse_ref.shape[1]
    for pair in range(2):
        columns = [pl.ds(pl.multiple_of(((2 * pair + k) * 2 + core) * sub, sub), sub) for k in range(2)]
        block = jnp.concatenate([c_ref[:, column] for column in columns], axis=1)
        pulled = jnp.dot(weights_ref[...], block, preferred_element_type=jnp.float32)
        for k in range(2):
            part = pulled[:, k * sub : k * sub + sub] * inverse_ref[...]
            row = (2 * pair + k) * sub
            out_ref[row : row + sub, :] = jnp.transpose(part).astype(out_ref.dtype)


def kept_kernel(place_ref, weights_ref, inverse_ref, c_ref, e_ref, kept_ref, base_ref):
    pull(place_ref[0], weights_ref, inverse_ref, c_ref, kept_ref)
    sub = base_ref.shape[0]
    own = pl.multiple_of((2 * place_ref[1] + place_ref[0]) * sub, sub)
    base_ref[...] = jnp.transpose(e_ref[:, pl.ds(own, sub)].astype(jnp.float32))


def weigh(maxes, totals):
    largest = functools.reduce(jnp.maximum, maxes)
    shares = [jnp.exp(own - largest) * total for own, total in zip(maxes, totals)]
    whole = functools.reduce(jnp.add, shares)
    return [share / whole for share in shares], largest, whole


def terms_of(value, count=3):
    terms = []
    for _ in range(count):
        term = value.astype(jnp.bfloat16).astype(jnp.float32)
        terms.append(term)
        value = value - term
    return terms


def packed(largest, total):
    terms = terms_of(largest) + terms_of(total)
    terms.append(jnp.zeros((PACKED - len(terms), largest.shape[1]), jnp.float32))
    return jnp.concatenate(terms, axis=0).astype(jnp.bfloat16)


def unpacked(rows):
    wide = rows.astype(jnp.float32)
    return (wide[2:3] + wide[1:2]) + wide[0:1], (wide[5:6] + wide[4:5]) + wide[3:4]


def chip_kernel(place_ref, kept_ref, got_ref, stats_ref, mean_ref, chip_ref, *block_refs):
    sub, rows = mean_ref.shape
    count = len(block_refs) + 1
    used = count * sub
    other_max, other_total = unpacked(got_ref[used:, :])
    (own, other), largest, total = weigh(
        [stats_ref[0:1], other_max], [stats_ref[1:2], other_total]
    )
    chip_ref[...] = jnp.concatenate([largest, total, jnp.zeros((6, rows), jnp.float32)], axis=0)
    stats = packed(largest, total)
    for step in range(count):
        at = pl.ds(pl.multiple_of(lax.rem(place_ref[1] + step, count) * sub, sub), sub)
        mean = kept_ref[at, :] * own + got_ref[at, :].astype(jnp.float32) * other
        if step == 0:
            mean_ref[...] = mean
        else:
            block_refs[step - 1][:sub, :] = mean.astype(jnp.bfloat16)
            block_refs[step - 1][sub:, :] = stats


def quantize_kernel(mean_ref, chip_ref, *refs):
    *got_refs, base_ref, book_ref, residual_ref, sums_ref, raised_hbm, inverse_ref, gaps_ref, raised_ref, sems = refs
    sub, rows = mean_ref.shape
    parts, held, _ = sums_ref.shape
    words = book_ref.shape[0]
    quarter = words // parts
    scale = 2.0 / math.sqrt(sub)
    stats = [(chip_ref[0:1], chip_ref[1:2])] + [unpacked(got[sub:, :]) for got in got_refs]
    shares, _, _ = weigh(*zip(*stats))
    mean = mean_ref[...] * shares[0]
    for got, share in zip(got_refs, shares[1:]):
        mean = mean + got[:sub, :].astype(jnp.float32) * share
    residual = (base_ref[...] - mean).astype(jnp.bfloat16)
    residual_ref[...] = residual

    spans = [slice(at, at + 256) for at in range(0, words, 256)]
    peak = jnp.full((8, rows), -jnp.inf, jnp.float32)
    for at in spans:
        block = book_ref[at, :]
        wide = block.astype(jnp.float32)
        half = 0.5 * jnp.sum(wide * wide, axis=1, keepdims=True)
        gap = jnp.dot(block, residual, preferred_element_type=jnp.float32) - half
        gaps_ref[at, :] = gap
        peak = jnp.maximum(peak, jnp.max(gap.reshape(32, 8, rows), axis=0))
    peak = jnp.max(peak, axis=0, keepdims=True)
    total = jnp.zeros((8, rows), jnp.float32)
    stores = []
    for j, at in enumerate(spans):
        raised = jnp.exp((gaps_ref[at, :] - peak) * scale)
        raised_ref[at, :] = raised.astype(jnp.bfloat16)
        total = total + jnp.sum(raised.reshape(32, 8, rows), axis=0)
        if j % 4 == 3:
            at = slice((j - 3) * 256, (j + 1) * 256)
            stores.append(pltpu.make_async_copy(raised_ref.at[at, :], raised_hbm.at[at, :], sems.at[j // 4]))
            stores[-1].start()
    inverse = 1.0 / jnp.sum(total, axis=0, keepdims=True)
    inverse_ref[...] = jnp.broadcast_to(inverse, inverse_ref.shape)

    scaled = residual.astype(jnp.float32) * inverse
    high, low = (jnp.broadcast_to(term, (sub // 2, rows)) for term in terms_of(inverse, 2))
    sides = jnp.transpose(jnp.concatenate([scaled, high, low], axis=0)).astype(jnp.bfloat16)
    row = lax.broadcasted_iota(jnp.int32, (128, 128), 0)
    diagonal = row == lax.broadcasted_iota(jnp.int32, (128, 128), 1)
    for part in range(parts):
        lines = []
        for at in range(0, quarter, 256):
            span = slice(part * quarter + at, part * quarter + at + 256)
            sums = jnp.dot(raised_ref[span, :], sides, preferred_element_type=jnp.float32)
            sums_ref[part, at : at + 256, :] = sums[:, :sub].astype(jnp.bfloat16)
            counts = sums[:, sub:]
            counts = counts + pltpu.roll(counts, sub // 2, 1)
            for k in range(2):
                tile = counts[k * 128 : k * 128 + 128]
                lines.append(jnp.sum(jnp.where(diagonal, tile, 0.0), axis=0, keepdims=True))
        counts = jnp.concatenate(lines, axis=0)
        sums_ref[part, quarter:, :] = jnp.concatenate(terms_of(counts, 2), axis=0).astype(jnp.bfloat16)
    for store in stores:
        store.wait()


def middle_kernel(sums_ref, out_ref):
    parts, held, sub = sums_ref.shape
    targets, rows, _ = out_ref.shape
    words = rows - 8
    quarter = targets * words
    counts = jnp.zeros((quarter // 128, 128), jnp.float32)
    for part in range(parts):
        pair = sums_ref[part, quarter:, :].astype(jnp.float32)
        counts = counts + (pair[: quarter // 128] + pair[quarter // 128 :])
    high, low = terms_of(counts, 2)
    left = lax.broadcasted_iota(jnp.int32, high.shape, 1) < 64
    even = jnp.where(left, high, pltpu.roll(low, 64, 1))
    odd = jnp.where(left, pltpu.roll(high, 64, 1), low)
    for target in range(targets):
        at = slice(target * words, target * words + words)
        total = sums_ref[0, at, :].astype(jnp.float32)
        for part in range(1, parts):
            total = total + sums_ref[part, at, :].astype(jnp.float32)
        row = (even if target % 2 == 0 else odd)[target // 2 : target // 2 + 1]
        row = jnp.concatenate([row, jnp.zeros((7, sub), jnp.float32)], axis=0)
        place = (target + BOOK_FIRST - SUMS_FIRST) % targets
        out_ref[place] = jnp.concatenate([total, row], axis=0).astype(jnp.bfloat16)


def last_kernel(sums_ref, own_ref, out_ref):
    parts = sums_ref.shape[0]
    words, sub = own_ref.shape
    total = sums_ref[0].astype(jnp.float32)
    for part in range(1, parts):
        total = total + sums_ref[part].astype(jnp.float32)
    pair = total[words : words + 1]
    counts = jnp.broadcast_to(pair + pltpu.roll(pair, 64, 1), (words, sub))
    diagonal = lax.broadcasted_iota(jnp.int32, (words, sub), 0) == lax.broadcasted_iota(jnp.int32, (words, sub), 1)
    counts = jnp.sum(jnp.where(diagonal, counts, 0.0), axis=1, keepdims=True)
    own = own_ref[...].astype(jnp.float32)
    out_ref[...] = (total[:words] + smoothing * own) / (counts + smoothing)


VMEM = pl.BlockSpec(memory_space=pltpu.VMEM)
SMEM = pl.BlockSpec(memory_space=pltpu.SMEM)
HBM = pl.BlockSpec(memory_space=pltpu.HBM)


def call(kernel, out_shape, ins, *args, outs=None, scratch=(), mib=8):
    return pl.pallas_call(
        kernel,
        out_shape=out_shape,
        in_specs=ins,
        out_specs=outs or jax.tree.map(lambda _: VMEM, out_shape),
        scratch_shapes=scratch,
        compiler_params=pltpu.CompilerParams(vmem_limit_bytes=mib * 2**20),
        cost_estimate=pl.CostEstimate(flops=1, bytes_accessed=1, transcendentals=0),
    )(*args)


def array(shape, dtype=jnp.float32):
    return jax.ShapeDtypeStruct(shape, dtype)


def coarse(embeddings, centroids, place):
    rows, width = embeddings.shape
    count = centroids.shape[0]
    half, sub, chunk = width // 2, 128, 256
    sent, stats, weights, inverse = call(
        coarse_kernel,
        (
            array((half + PACKED, rows), jnp.bfloat16),
            array((8, rows)),
            array((rows, count), jnp.bfloat16),
            array((rows, sub)),
        ),
        [SMEM, VMEM, VMEM],
        place,
        embeddings,
        centroids,
        scratch=[pltpu.VMEM((count // chunk, rows, chunk), jnp.float32)],
        mib=24,
    )
    kept, base = call(
        kept_kernel,
        (array((half, rows)), array((sub, rows))),
        [SMEM] + [VMEM] * 4,
        place,
        weights,
        inverse,
        centroids,
        embeddings,
        mib=24,
    )
    return kept, sent, stats, base


def chip(place, kept, got, stats):
    sub, rows, count = 128, stats.shape[1], 4
    blocks = [array((sub + PACKED, rows), jnp.bfloat16)] * (count - 1)
    return call(
        chip_kernel,
        [array((sub, rows)), array((8, rows))] + blocks,
        [SMEM] + [VMEM] * 3,
        place,
        kept,
        got,
        stats,
    )


def quantize(mean, stats, gots, base, book, parts):
    (sub, rows), words = mean.shape, book.shape[0]
    quarter = words // parts
    return call(
        quantize_kernel,
        (
            array((sub, rows), jnp.bfloat16),
            array((parts, quarter + quarter // 64, sub), jnp.bfloat16),
            array((words, rows), jnp.bfloat16),
            array((8, rows)),
        ),
        [VMEM] * (len(gots) + 4),
        mean,
        stats,
        *gots,
        base,
        book,
        outs=(VMEM, VMEM, HBM, VMEM),
        scratch=[
            pltpu.VMEM((words, rows), jnp.float32),
            pltpu.VMEM((words, rows), jnp.bfloat16),
            pltpu.SemaphoreType.DMA((parts,)),
        ],
        mib=51,
    )


def local(embeddings, centroids, codebook):
    _, book_rows, sub_width = codebook.shape
    y_count, z_count, x_count = lax.axis_size("y"), lax.axis_size("z"), lax.axis_size("x")
    words = book_rows * y_count * z_count
    place = jnp.stack([lax.axis_index("c"), lax.axis_index("x")]).astype(jnp.int32)

    own = codebook.reshape(book_rows, sub_width)
    book = exchange(jnp.broadcast_to(own, (z_count, book_rows, sub_width)), "z", BOOK_FIRST)
    book = book.reshape(words // y_count, sub_width)

    kept, sent, stats, base = coarse(embeddings, centroids, place)
    got = lax.ppermute(sent, "c", [(0, 1), (1, 0)])
    mean, stats, *blocks = chip(place, kept, got, stats)
    book, *blocks = lax.optimization_barrier((book, *blocks))
    gots = {}
    for step in (2, 1, 3):
        ring = [(i, (i + step) % x_count) for i in range(x_count)]
        gots[step] = lax.ppermute(blocks[step - 1], "x", ring)
    gots = [gots[step] for step in (1, 2, 3)]
    book = exchange(jnp.broadcast_to(book, (y_count,) + book.shape), "y").reshape(words, sub_width)
    residual, sums, raised, inverse = quantize(mean, stats, gots, base, book, y_count)

    sums = exchange(sums, "y")
    rebuilt = lax.dot_general(
        book, raised, (((0,), (0,)), ((), ())), preferred_element_type=jnp.float32
    ) * inverse[:1]
    pq_error = jnp.mean(jnp.square(residual.astype(jnp.float32) - rebuilt), axis=0)
    sums, pq_error = lax.optimization_barrier((sums, pq_error[None]))
    sums = call(
        middle_kernel, array((z_count, book_rows + 8, sub_width), jnp.bfloat16), [VMEM], sums
    )
    sums = exchange(sums, "z", SUMS_FIRST)
    new_codebook = call(last_kernel, array((book_rows, sub_width)), [VMEM] * 2, sums, own)
    return (residual, new_codebook[None], pq_error)


def solution(mesh):
    sizes = (4, 16, 4, 2)
    wide = Mesh(mesh.devices.reshape(sizes), ("y", "z", "x", "c"))
    rows = ("y", "z")
    placed = (P(rows, None), P(CENT, None), P(CENT, rows, None))
    return jax.shard_map(
        local,
        mesh=wide,
        in_specs=placed,
        out_specs=(P(CENT, rows), P(CENT, rows, None), P(CENT, rows)),
        check_vma=False,
    )
```

```python
import functools
import math

import jax
import jax.numpy as jnp
from jax import lax
from jax.experimental import pallas as pl
from jax.experimental.pallas import tpu as pltpu
from jax.sharding import Mesh, PartitionSpec as P

smoothing = 1.0
CENT = ("x", "c")


PACKED = 16
BOOK_FIRST = 10
SUMS_FIRST = 8
Y_FIRST = 2


def exchange(parts, axis, first=0):
    count = lax.axis_size(axis)
    order = [[(first + i) % count for i in range(count)]]
    return lax.all_to_all(parts, axis, 0, 0, axis_index_groups=order, tiled=True)


def wide_row(columns):
    return jnp.transpose(jnp.broadcast_to(columns, (columns.shape[0], 128)))[:1]


def coarse_kernel(place_ref, e_ref, c_ref, sent_ref, stats_ref, weights_ref, inverse_ref, logits_ref):
    rows, width = e_ref.shape
    chunks, _, chunk = logits_ref.shape
    used = sent_ref.shape[0] - PACKED
    scale = 2.0 / math.sqrt(width)

    def score(j, peak):
        block = c_ref[slice(j * chunk, j * chunk + chunk), :]
        wide = block.astype(jnp.float32)
        half_norm = wide_row(0.5 * jnp.sum(wide * wide, axis=1, keepdims=True))
        products = lax.dot_general(
            e_ref[...], block, (((1,), (1,)), ((), ())), preferred_element_type=jnp.float32
        )
        logits = (products - half_norm) * scale
        logits_ref[j] = logits
        for part in range(chunk // 128):
            peak = jnp.maximum(peak, logits[:, part * 128 : part * 128 + 128])
        return peak

    peak = jnp.full((rows, 128), -jnp.inf, jnp.float32)
    for j in range(chunks):
        peak = score(j, peak)
    peak = jnp.max(peak, axis=1, keepdims=True)

    def raise_(j, total):
        shifted = jnp.exp(logits_ref[j] - peak)
        weights_ref[:, slice(j * chunk, j * chunk + chunk)] = shifted.astype(jnp.bfloat16)
        for part in range(chunk // 128):
            total = total + shifted[:, part * 128 : part * 128 + 128]
        return total

    total = jnp.zeros((rows, 128), jnp.float32)
    for j in range(chunks):
        total = raise_(j, total)
    total = jnp.sum(total, axis=1, keepdims=True)
    inverse_ref[...] = jnp.broadcast_to(1.0 / total, inverse_ref.shape)
    pull(1 - place_ref[0], weights_ref, inverse_ref, c_ref, sent_ref)
    largest, total = wide_row(peak), wide_row(total)
    stats_ref[...] = jnp.concatenate([largest, total, jnp.zeros((6, rows), jnp.float32)], axis=0)
    sent_ref[used:, :] = packed(largest, total)


def pull(core, weights_ref, inverse_ref, c_ref, out_ref):
    sub = inverse_ref.shape[1]
    for pair in range(2):
        columns = [pl.ds(pl.multiple_of(((2 * pair + k) * 2 + core) * sub, sub), sub) for k in range(2)]
        block = jnp.concatenate([c_ref[:, column] for column in columns], axis=1)
        pulled = jnp.dot(weights_ref[...], block, preferred_element_type=jnp.float32)
        for k in range(2):
            part = pulled[:, k * sub : k * sub + sub] * inverse_ref[...]
            row = (2 * pair + k) * sub
            out_ref[row : row + sub, :] = jnp.transpose(part).astype(out_ref.dtype)


def kept_kernel(place_ref, weights_ref, inverse_ref, c_ref, e_ref, kept_ref, base_ref):
    pull(place_ref[0], weights_ref, inverse_ref, c_ref, kept_ref)
    sub = base_ref.shape[0]
    own = pl.multiple_of((2 * place_ref[1] + place_ref[0]) * sub, sub)
    base_ref[...] = jnp.transpose(e_ref[:, pl.ds(own, sub)].astype(jnp.float32))


def weigh(maxes, totals):
    largest = functools.reduce(jnp.maximum, maxes)
    shares = [jnp.exp(own - largest) * total for own, total in zip(maxes, totals)]
    whole = functools.reduce(jnp.add, shares)
    return [share / whole for share in shares], largest, whole


def terms_of(value, count=3):
    terms = []
    for _ in range(count):
        term = value.astype(jnp.bfloat16).astype(jnp.float32)
        terms.append(term)
        value = value - term
    return terms


def packed(largest, total):
    terms = terms_of(largest) + terms_of(total)
    terms.append(jnp.zeros((PACKED - len(terms), largest.shape[1]), jnp.float32))
    return jnp.concatenate(terms, axis=0).astype(jnp.bfloat16)


def unpacked(rows):
    wide = rows.astype(jnp.float32)
    return (wide[2:3] + wide[1:2]) + wide[0:1], (wide[5:6] + wide[4:5]) + wide[3:4]


def chip_kernel(place_ref, kept_ref, got_ref, stats_ref, mean_ref, chip_ref, *block_refs):
    sub, rows = mean_ref.shape
    count = len(block_refs) + 1
    used = count * sub
    other_max, other_total = unpacked(got_ref[used:, :])
    (own, other), largest, total = weigh(
        [stats_ref[0:1], other_max], [stats_ref[1:2], other_total]
    )
    chip_ref[...] = jnp.concatenate([largest, total, jnp.zeros((6, rows), jnp.float32)], axis=0)
    stats = packed(largest, total)
    for step in range(count):
        at = pl.ds(pl.multiple_of(lax.rem(place_ref[1] + step, count) * sub, sub), sub)
        mean = kept_ref[at, :] * own + got_ref[at, :].astype(jnp.float32) * other
        if step == 0:
            mean_ref[...] = mean
        else:
            block_refs[step - 1][:sub, :] = mean.astype(jnp.bfloat16)
            block_refs[step - 1][sub:, :] = stats


def quantize_kernel(mean_ref, chip_ref, *refs):
    *got_refs, base_ref, book_ref, residual_ref, sums_ref, raised_hbm, inverse_ref, gaps_ref, raised_ref, sems = refs
    sub, rows = mean_ref.shape
    parts, held, _ = sums_ref.shape
    words = book_ref.shape[0]
    quarter = words // parts
    scale = 2.0 / math.sqrt(sub)
    stats = [(chip_ref[0:1], chip_ref[1:2])] + [unpacked(got[sub:, :]) for got in got_refs]
    shares, _, _ = weigh(*zip(*stats))
    mean = mean_ref[...] * shares[0]
    for got, share in zip(got_refs, shares[1:]):
        mean = mean + got[:sub, :].astype(jnp.float32) * share
    residual = (base_ref[...] - mean).astype(jnp.bfloat16)
    residual_ref[...] = residual

    spans = [slice(at, at + 256) for at in range(0, words, 256)]
    peak = jnp.full((8, rows), -jnp.inf, jnp.float32)
    for at in spans:
        block = book_ref[at, :]
        wide = block.astype(jnp.float32)
        half = 0.5 * jnp.sum(wide * wide, axis=1, keepdims=True)
        gap = jnp.dot(block, residual, preferred_element_type=jnp.float32) - half
        gaps_ref[at, :] = gap
        peak = jnp.maximum(peak, jnp.max(gap.reshape(32, 8, rows), axis=0))
    peak = jnp.max(peak, axis=0, keepdims=True)
    total = jnp.zeros((8, rows), jnp.float32)
    stores = []
    for j, at in enumerate(spans):
        raised = jnp.exp((gaps_ref[at, :] - peak) * scale)
        raised_ref[at, :] = raised.astype(jnp.bfloat16)
        total = total + jnp.sum(raised.reshape(32, 8, rows), axis=0)
        if j % 4 == 3:
            at = slice((j - 3) * 256, (j + 1) * 256)
            stores.append(pltpu.make_async_copy(raised_ref.at[at, :], raised_hbm.at[at, :], sems.at[j // 4]))
            stores[-1].start()
    inverse = 1.0 / jnp.sum(total, axis=0, keepdims=True)
    inverse_ref[...] = jnp.broadcast_to(inverse, inverse_ref.shape)

    scaled = residual.astype(jnp.float32) * inverse
    high, low = (jnp.broadcast_to(term, (sub // 2, rows)) for term in terms_of(inverse, 2))
    sides = jnp.transpose(jnp.concatenate([scaled, high, low], axis=0)).astype(jnp.bfloat16)
    row = lax.broadcasted_iota(jnp.int32, (128, 128), 0)
    diagonal = row == lax.broadcasted_iota(jnp.int32, (128, 128), 1)
    for part in range(parts):
        lines = []
        for at in range(0, quarter, 256):
            span = slice(part * quarter + at, part * quarter + at + 256)
            sums = jnp.dot(raised_ref[span, :], sides, preferred_element_type=jnp.float32)
            sums_ref[part, at : at + 256, :] = sums[:, :sub].astype(jnp.bfloat16)
            counts = sums[:, sub:]
            counts = counts + pltpu.roll(counts, sub // 2, 1)
            for k in range(2):
                tile = counts[k * 128 : k * 128 + 128]
                lines.append(jnp.sum(jnp.where(diagonal, tile, 0.0), axis=0, keepdims=True))
        counts = jnp.concatenate(lines, axis=0)
        sums_ref[part, quarter:, :] = jnp.concatenate(terms_of(counts, 2), axis=0).astype(jnp.bfloat16)
    for store in stores:
        store.wait()


def middle_kernel(sums_ref, out_ref):
    parts, held, sub = sums_ref.shape
    targets, rows, _ = out_ref.shape
    words = rows - 8
    quarter = targets * words
    counts = jnp.zeros((quarter // 128, 128), jnp.float32)
    for part in range(parts):
        pair = sums_ref[part, quarter:, :].astype(jnp.float32)
        counts = counts + (pair[: quarter // 128] + pair[quarter // 128 :])
    high, low = terms_of(counts, 2)
    left = lax.broadcasted_iota(jnp.int32, high.shape, 1) < 64
    even = jnp.where(left, high, pltpu.roll(low, 64, 1))
    odd = jnp.where(left, pltpu.roll(high, 64, 1), low)
    for target in range(targets):
        at = slice(target * words, target * words + words)
        total = sums_ref[0, at, :].astype(jnp.float32)
        for part in range(1, parts):
            total = total + sums_ref[part, at, :].astype(jnp.float32)
        row = (even if target % 2 == 0 else odd)[target // 2 : target // 2 + 1]
        row = jnp.concatenate([row, jnp.zeros((7, sub), jnp.float32)], axis=0)
        place = (target + BOOK_FIRST - SUMS_FIRST) % targets
        out_ref[place] = jnp.concatenate([total, row], axis=0).astype(jnp.bfloat16)


def last_kernel(sums_ref, own_ref, out_ref):
    parts = sums_ref.shape[0]
    words, sub = own_ref.shape
    total = sums_ref[0].astype(jnp.float32)
    for part in range(1, parts):
        total = total + sums_ref[part].astype(jnp.float32)
    pair = total[words : words + 1]
    counts = jnp.broadcast_to(pair + pltpu.roll(pair, 64, 1), (words, sub))
    diagonal = lax.broadcasted_iota(jnp.int32, (words, sub), 0) == lax.broadcasted_iota(jnp.int32, (words, sub), 1)
    counts = jnp.sum(jnp.where(diagonal, counts, 0.0), axis=1, keepdims=True)
    own = own_ref[...].astype(jnp.float32)
    out_ref[...] = (total[:words] + smoothing * own) / (counts + smoothing)


VMEM = pl.BlockSpec(memory_space=pltpu.VMEM)
SMEM = pl.BlockSpec(memory_space=pltpu.SMEM)
HBM = pl.BlockSpec(memory_space=pltpu.HBM)


def call(kernel, out_shape, ins, *args, outs=None, scratch=(), mib=8):
    return pl.pallas_call(
        kernel,
        out_shape=out_shape,
        in_specs=ins,
        out_specs=outs or jax.tree.map(lambda _: VMEM, out_shape),
        scratch_shapes=scratch,
        compiler_params=pltpu.CompilerParams(vmem_limit_bytes=mib * 2**20),
        cost_estimate=pl.CostEstimate(flops=1, bytes_accessed=1, transcendentals=0),
    )(*args)


def array(shape, dtype=jnp.float32):
    return jax.ShapeDtypeStruct(shape, dtype)


def coarse(embeddings, centroids, place):
    rows, width = embeddings.shape
    count = centroids.shape[0]
    half, sub, chunk = width // 2, 128, 256
    sent, stats, weights, inverse = call(
        coarse_kernel,
        (
            array((half + PACKED, rows), jnp.bfloat16),
            array((8, rows)),
            array((rows, count), jnp.bfloat16),
            array((rows, sub)),
        ),
        [SMEM, VMEM, VMEM],
        place,
        embeddings,
        centroids,
        scratch=[pltpu.VMEM((count // chunk, rows, chunk), jnp.float32)],
        mib=24,
    )
    kept, base = call(
        kept_kernel,
        (array((half, rows)), array((sub, rows))),
        [SMEM] + [VMEM] * 4,
        place,
        weights,
        inverse,
        centroids,
        embeddings,
        mib=24,
    )
    return kept, sent, stats, base


def chip(place, kept, got, stats):
    sub, rows, count = 128, stats.shape[1], 4
    blocks = [array((sub + PACKED, rows), jnp.bfloat16)] * (count - 1)
    return call(
        chip_kernel,
        [array((sub, rows)), array((8, rows))] + blocks,
        [SMEM] + [VMEM] * 3,
        place,
        kept,
        got,
        stats,
    )


def quantize(mean, stats, gots, base, book, parts):
    (sub, rows), words = mean.shape, book.shape[0]
    quarter = words // parts
    return call(
        quantize_kernel,
        (
            array((sub, rows), jnp.bfloat16),
            array((parts, quarter + quarter // 64, sub), jnp.bfloat16),
            array((words, rows), jnp.bfloat16),
            array((8, rows)),
        ),
        [VMEM] * (len(gots) + 4),
        mean,
        stats,
        *gots,
        base,
        book,
        outs=(VMEM, VMEM, HBM, VMEM),
        scratch=[
            pltpu.VMEM((words, rows), jnp.float32),
            pltpu.VMEM((words, rows), jnp.bfloat16),
            pltpu.SemaphoreType.DMA((parts,)),
        ],
        mib=51,
    )


def local(embeddings, centroids, codebook):
    _, book_rows, sub_width = codebook.shape
    y_count, z_count, x_count = lax.axis_size("y"), lax.axis_size("z"), lax.axis_size("x")
    words = book_rows * y_count * z_count
    place = jnp.stack([lax.axis_index("c"), lax.axis_index("x")]).astype(jnp.int32)

    own = codebook.reshape(book_rows, sub_width)
    book = exchange(jnp.broadcast_to(own, (z_count, book_rows, sub_width)), "z", BOOK_FIRST)
    book = book.reshape(words // y_count, sub_width)

    kept, sent, stats, base = coarse(embeddings, centroids, place)
    got = lax.ppermute(sent, "c", [(0, 1), (1, 0)])
    mean, stats, *blocks = chip(place, kept, got, stats)
    book, *blocks = lax.optimization_barrier((book, *blocks))
    gots = {}
    for step in (2, 1, 3):
        ring = [(i, (i + step) % x_count) for i in range(x_count)]
        gots[step] = lax.ppermute(blocks[step - 1], "x", ring)
    gots = [gots[step] for step in (1, 2, 3)]
    book = exchange(jnp.broadcast_to(book, (y_count,) + book.shape), "y", Y_FIRST).reshape(words, sub_width)
    residual, sums, raised, inverse = quantize(mean, stats, gots, base, book, y_count)

    sums = exchange(sums, "y", Y_FIRST)
    rebuilt = lax.dot_general(
        book, raised, (((0,), (0,)), ((), ())), preferred_element_type=jnp.float32
    ) * inverse[:1]
    pq_error = jnp.mean(jnp.square(residual.astype(jnp.float32) - rebuilt), axis=0)
    sums, pq_error = lax.optimization_barrier((sums, pq_error[None]))
    sums = call(
        middle_kernel, array((z_count, book_rows + 8, sub_width), jnp.bfloat16), [VMEM], sums
    )
    sums = exchange(sums, "z", SUMS_FIRST)
    new_codebook = call(last_kernel, array((book_rows, sub_width)), [VMEM] * 2, sums, own)
    return (residual, new_codebook[None], pq_error)


def solution(mesh):
    sizes = (4, 16, 4, 2)
    wide = Mesh(mesh.devices.reshape(sizes), ("y", "z", "x", "c"))
    rows = ("y", "z")
    placed = (P(rows, None), P(CENT, None), P(CENT, rows, None))
    return jax.shard_map(
        local,
        mesh=wide,
        in_specs=placed,
        out_specs=(P(CENT, rows), P(CENT, rows, None), P(CENT, rows)),
        check_vma=False,
    )
```
